128 devices in a mesh: seq: 64 (over y_lo, x, z, core), head: 2 (over y_hi).
Axes of the slice: x: 4, y: 4 (y_hi: 2, y_lo: 2; y = y_hi * 2 + y_lo), z: 4, core: 2. Of those that a mesh axis runs over, the one named last changes fastest.
Arguments:
- tokens: bfloat16 [8192, 1024], P('seq'), may hold values from -6 to 6
- cotangent: bfloat16 [8192, 1024], P('seq'), may hold values from -6 to 6
- gain_first: float32 [1024], replicated, may hold values from 0.5 to 1.5
- z_weight: bfloat16 [1024, 1536], P('seq', 'head'), may hold values from -0.1875 to 0.1875
- x_weight: bfloat16 [1024, 1536], P('seq', 'head'), may hold values from -0.1875 to 0.1875
- bc_weight: bfloat16 [1024, 256], P('seq'), may hold values from -0.1875 to 0.1875
- dt_weight: bfloat16 [1024, 24], P('seq', 'head'), may hold values from -0.1875 to 0.1875
- conv_x_weight: float32 [4, 1536], P(None, 'head'), may hold values from -3 to 3
- conv_x_bias: float32 [1536], P('head'), may hold values from -2 to 2
- conv_bc_weight: float32 [4, 256], replicated, may hold values from -3 to 3
- conv_bc_bias: float32 [256], replicated, may hold values from -2 to 2
- dt_bias: float32 [24], P('head'), may hold values from -16 to -5
- decay_rate: float32 [24], P('head'), may hold values from 0.2 to 819
- skip_weight: float32 [24], P('head'), may hold values from 0.5 to 1.5
- out_weight: bfloat16 [1024, 1536], P('seq', 'head'), may hold values from -0.15625 to 0.15625
- q_weight: bfloat16 [1024, 512], P('seq', 'head'), may hold values from -0.1875 to 0.1875
- key_matrix: bfloat16 [1024, 128], P('seq', 'head'), may hold values from -0.1875 to 0.1875
- value_matrix: bfloat16 [1024, 128], P('seq', 'head'), may hold values from -0.1875 to 0.1875
- o_weight: bfloat16 [1024, 512], P('seq', 'head'), may hold values from -6 to 6
- gain_second: float32 [1024], replicated, may hold values from 0.5 to 1.5
- gate_weight: bfloat16 [1024, 2048], P('seq', 'head'), may hold values from -0.1875 to 0.1875
- up_weight: bfloat16 [1024, 2048], P('seq', 'head'), may hold values from -0.1875 to 0.1875
- down_weight: bfloat16 [1024, 2048], P('seq', 'head'), may hold values from -0.125 to 0.125
Outputs:
- output: bfloat16 [8192, 1024], P('seq')
- grad_tokens: float32 [8192, 1024], P('seq')
- grad_gain_first: float32 [1024], replicated
- grad_z_weight: float32 [1024, 1536], P('seq', 'head')
- grad_x_weight: float32 [1024, 1536], P('seq', 'head')
- grad_bc_weight: float32 [1024, 256], P('seq')
- grad_dt_weight: float32 [1024, 24], P('seq', 'head')
- grad_conv_x_weight: float32 [4, 1536], P(None, 'head')
- grad_conv_x_bias: float32 [1536], P('head')
- grad_conv_bc_weight: float32 [4, 256], replicated
- grad_conv_bc_bias: float32 [256], replicated
- grad_dt_bias: float32 [24], P('head')
- grad_decay_rate: float32 [24], P('head')
- grad_skip_weight: float32 [24], P('head')
- grad_out_weight: float32 [1024, 1536], P('seq', 'head')
- grad_q_weight: float32 [1024, 512], P('seq', 'head')
- grad_k_weight: float32 [1024, 128], P('seq', 'head')
- grad_v_weight: float32 [1024, 128], P('seq', 'head')
- grad_o_weight: float32 [1024, 512], P('seq', 'head')
- grad_gain_second: float32 [1024], replicated
- grad_gate_weight: float32 [1024, 2048], P('seq', 'head')
- grad_up_weight: float32 [1024, 2048], P('seq', 'head')
- grad_down_weight: float32 [1024, 2048], P('seq', 'head')
The draws below stay inside these ranges and needn't reach their ends.
All inputs are finite; a program needn't handle non-finite values.
Results may differ from the reference program's by a relative error of at most 0.014.
Values may be sent and summed in bfloat16 or wider, within the bound.
No kernel may reach another device: no remote copies, remote signals or barrier semaphores. Data moves between devices by JAX's collectives and lax.ppermute only.
A program may use at most 192 MiB of HBM per device.

```python
import math
import jax
import jax.numpy as jnp
from jax import lax

MODEL_WIDTH = 1024
NH = 24
P_SIZE = 64
NS = 128
QUERY_HEADS = 8
KEY_VALUE_HEADS = 2
HEAD_SIZE = 64
FF = 2048
CONV_K = 4
TOK_DEV = 128
SEQ_LEN = 8192
DSSM = 1536
N_HEAD = 2


def draw_dt_bias(key, part):
    key = jax.random.fold_in(key, 7)
    spread = jax.random.uniform(key, (NH,), jnp.float32, -1.0, 1.0)
    return spread - jnp.log(8.0 * SEQ_LEN)


def level_of(own_key, dims, cuts, low, high):
    def one(dim, shards_of):
        draws = jax.random.uniform(jax.random.fold_in(jax.random.fold_in(own_key, 6), dim), (shards_of,), jnp.float32, low / len(cuts), high / len(cuts))
        return jnp.repeat(jnp.exp(draws), dims[dim] // shards_of).reshape((-1,) + (1,) * (len(dims) - dim - 1))

    factor_of = one(*cuts[0])
    for cut in cuts[1:]:
        factor_of = factor_of * one(*cut)
    return factor_of


def bell_draw(rng, extent, deviation, most, cuts=(), kind=jnp.bfloat16):
    level = level_of(rng, extent, cuts, -0.22, 0.18) if cuts else 1.0
    values = jax.random.normal(rng, extent, jnp.float32) * deviation * level
    return jnp.minimum(jnp.maximum(values, -most), most).astype(kind)


def setup_inputs(seed: int = 0) -> dict:
    seeds = jax.random.split(jax.random.key(seed), 24)
    return {
        "tokens": bell_draw(seeds[0], (SEQ_LEN, MODEL_WIDTH), 1.0, 6.0, ((0, 64),)),
        "cotangent": bell_draw(seeds[1], (SEQ_LEN, MODEL_WIDTH), 1.0, 6.0, ((0, 64),)),
        "gain_first": jnp.clip(1.0 + 0.1 * jax.random.normal(seeds[2], (MODEL_WIDTH,), jnp.float32), 0.5, 1.5),
        "z_weight": bell_draw(seeds[3], (MODEL_WIDTH, DSSM), MODEL_WIDTH ** -0.5, 0.1875, ((0, 64), (1, 2))),
        "x_weight": bell_draw(seeds[4], (MODEL_WIDTH, DSSM), MODEL_WIDTH ** -0.5, 0.1875, ((0, 64), (1, 2))),
        "bc_weight": bell_draw(seeds[5], (MODEL_WIDTH, 2 * NS), MODEL_WIDTH ** -0.5, 0.1875, ((0, 64),)),
        "dt_weight": bell_draw(seeds[6], (MODEL_WIDTH, NH), MODEL_WIDTH ** -0.5, 0.1875, ((0, 64), (1, 2))),
        "conv_x_weight": bell_draw(seeds[7], (CONV_K, DSSM), 0.5, 3.0, ((1, 2),), jnp.float32),
        "conv_x_bias": bell_draw(seeds[8], (DSSM,), 0.3, 2.0, ((0, 2),), jnp.float32),
        "conv_bc_weight": bell_draw(seeds[9], (CONV_K, 2 * NS), 0.5, 3.0, (), jnp.float32),
        "conv_bc_bias": bell_draw(seeds[10], (2 * NS,), 0.3, 2.0, (), jnp.float32),
        "dt_bias": draw_dt_bias(jax.random.fold_in(seeds[23], 71), 0),
        "decay_rate": jnp.clip(jnp.exp(math.log(819.0) - 8.317522 * jax.random.uniform(seeds[12], (NH,), jnp.float32) ** level_of(seeds[12], (NH,), ((0, 2),), -0.2, 0.2)), 0.2, 819.0),
        "skip_weight": jnp.clip(0.5 + 1.0 * jax.random.uniform(seeds[13], (NH,), jnp.float32) ** level_of(seeds[13], (NH,), ((0, 2),), -0.2, 0.2), 0.5, 1.5),
        "out_weight": bell_draw(seeds[14], (MODEL_WIDTH, DSSM), DSSM ** -0.5, 0.15625, ((0, 64), (1, 2))),
        "q_weight": bell_draw(seeds[15], (MODEL_WIDTH, QUERY_HEADS * HEAD_SIZE), MODEL_WIDTH ** -0.5, 0.1875, ((0, 64), (1, 2))),
        "key_matrix": bell_draw(seeds[16], (MODEL_WIDTH, KEY_VALUE_HEADS * HEAD_SIZE), MODEL_WIDTH ** -0.5, 0.1875, ((0, 64), (1, 2))),
        "value_matrix": bell_draw(seeds[17], (MODEL_WIDTH, KEY_VALUE_HEADS * HEAD_SIZE), MODEL_WIDTH ** -0.5, 0.1875, ((0, 64), (1, 2))),
        "o_weight": bell_draw(seeds[18], (MODEL_WIDTH, QUERY_HEADS * HEAD_SIZE), (0.5 * SEQ_LEN ** 0.5 * (QUERY_HEADS * HEAD_SIZE) ** -0.5), 6.0, ((0, 64), (1, 2))),
        "gain_second": jnp.clip(1.0 + 0.1 * jax.random.normal(seeds[19], (MODEL_WIDTH,), jnp.float32), 0.5, 1.5),
        "gate_weight": bell_draw(seeds[20], (MODEL_WIDTH, FF), MODEL_WIDTH ** -0.5, 0.1875, ((0, 64), (1, 2))),
        "up_weight": bell_draw(seeds[21], (MODEL_WIDTH, FF), MODEL_WIDTH ** -0.5, 0.1875, ((0, 64), (1, 2))),
        "down_weight": bell_draw(seeds[22], (MODEL_WIDTH, FF), FF ** -0.5, 0.125, ((0, 64), (1, 2))),
    }


@jax.custom_vjp
def local_input(v):
    return lax.optimization_barrier(v.astype(jnp.bfloat16)).astype(jnp.float32)

@jax.custom_vjp
def local_gradient(v):
    return v

def low_keep(v):
    return (local_input(v), None)

def low_pass(kept, grad):
    return (grad,)

def back_keep(v):
    return (v, None)

def back_low(kept, grad):
    return (local_input(grad),)
local_input.defvjp(low_keep, low_pass)
local_gradient.defvjp(back_keep, back_low)
EPS = 1e-06
ROPE_BASE = 100000000000.0
MASKED = -1e+30
HIGHEST = lax.Precision.HIGHEST

def elementwise_product(left_side, right_side):
    return jnp.dot(left_side, right_side, precision=HIGHEST, preferred_element_type=jnp.float32)

def rms_norm(values, norm_gain):
    return values * lax.rsqrt(lax.optimization_barrier(jnp.mean(values * values, axis=-1, keepdims=True)) + EPS) * norm_gain

def rotary_embed(values, head_count, token_positions, sign_value):
    half_dim = HEAD_SIZE // 2
    frequency = ROPE_BASE ** (-jnp.arange(half_dim, dtype=jnp.float32) * (1.0 / half_dim))
    angles = token_positions[:, None] * frequency[None, :]
    cosine = jnp.cos(angles)[:, None, :]
    sine_part = sign_value * jnp.sin(angles)[:, None, :]
    shaped = values.reshape(values.shape[0], head_count, HEAD_SIZE)
    first_half = shaped[..., :half_dim]
    second_half = shaped[..., half_dim:]
    turned = jnp.concatenate([first_half * cosine - second_half * sine_part, second_half * cosine + first_half * sine_part], axis=-1)
    return turned.reshape(values.shape[0], head_count * HEAD_SIZE)

def causal_conv(values, conv_weight, conv_bias):
    kernel = conv_weight.shape[0]
    length_total = values.shape[0]
    padded = jnp.concatenate([jnp.zeros((kernel - 1, values.shape[1]), jnp.float32), values], axis=0)
    summed = conv_bias + sum((conv_weight[lag_index] * padded[lag_index:lag_index + length_total] for lag_index in range(kernel)))
    return jax.nn.silu(summed)

def ssd_span(carry_state, pieces, decay_rate, skip_weight):
    head_inputs, step_size, in_vectors, out_vectors = pieces
    step_count = head_inputs.shape[0]
    log_decay = jnp.cumsum(-step_size * decay_rate, axis=0)
    causal = jnp.arange(step_count)[:, None] >= jnp.arange(step_count)[None, :]
    differ = log_decay[:, None, :] - log_decay[None, :, :]
    weights_ts = jnp.where(causal[:, :, None], jnp.exp(jnp.where(causal[:, :, None], differ, 0.0)), 0.0)
    intersection = jnp.dot(out_vectors, in_vectors.T, precision=HIGHEST)
    mixing = intersection[:, :, None] * weights_ts * step_size[None, :, :]
    inner_out = jnp.einsum('tsh,shp->thp', mixing, head_inputs, precision=HIGHEST)
    decay_now = jnp.exp(log_decay)
    carried_out = decay_now[:, :, None] * jnp.einsum('tn,hpn->thp', out_vectors, carry_state, precision=HIGHEST)
    outputs = inner_out + carried_out + skip_weight[None, :, None] * head_inputs
    to_end = jnp.exp(log_decay[-1][None, :] - log_decay) * step_size
    new_state = decay_now[-1][:, None, None] * carry_state + jnp.einsum('sh,shp,sn->hpn', to_end, head_inputs, in_vectors, precision=HIGHEST)
    return (new_state, outputs)

def ssd_sequence(head_inputs, step_size, in_vectors, out_vectors, decay_rate, skip_weight):
    length_total = head_inputs.shape[0]
    head_count = head_inputs.shape[1]
    blocks = length_total // TOK_DEV
    pieces = (head_inputs.reshape(blocks, TOK_DEV, head_count, P_SIZE), step_size.reshape(blocks, TOK_DEV, head_count), in_vectors.reshape(blocks, TOK_DEV, NS), out_vectors.reshape(blocks, TOK_DEV, NS))

    def advance(carry_state, piece):
        return ssd_span(carry_state, piece, decay_rate, skip_weight)
    start_state = jnp.zeros((head_count, P_SIZE, NS), jnp.float32)
    final_state, outputs = lax.scan(jax.checkpoint(advance), start_state, pieces)
    return outputs.reshape(length_total, head_count * P_SIZE)

def mamba_branch(local_normed, z_weight, x_weight, bc_weight, dt_weight, conv_x_weight, conv_x_bias, conv_bc_weight, conv_bc_bias, dt_bias, decay_rate, skip_weight, out_weight):
    length_total = local_normed.shape[0]
    gate_raw = local_gradient(elementwise_product(local_normed, z_weight))
    x_raw = local_gradient(elementwise_product(local_normed, x_weight))
    dt_raw = local_gradient(elementwise_product(local_normed, dt_weight))
    x_conved = causal_conv(x_raw, conv_x_weight, conv_x_bias)
    step_size = jax.nn.softplus(dt_raw + dt_bias)
    group_heads = NH // N_HEAD
    group_width = group_heads * P_SIZE
    results = []
    for group_index in range(N_HEAD):
        bc_raw = local_gradient(elementwise_product(local_normed, bc_weight))
        bc_conved = causal_conv(bc_raw, conv_bc_weight, conv_bc_bias)
        head_lo = group_index * group_heads
        head_hi = head_lo + group_heads
        group_inputs = x_conved[:, group_index * group_width:(group_index + 1) * group_width].reshape(length_total, group_heads, P_SIZE)
        results.append(ssd_sequence(group_inputs, step_size[:, head_lo:head_hi], bc_conved[:, :NS], bc_conved[:, NS:], decay_rate[head_lo:head_hi], skip_weight[head_lo:head_hi]))
    outputs = jnp.concatenate(results, axis=1)
    gated = local_input(outputs * jax.nn.silu(gate_raw))
    return elementwise_product(gated, out_weight.T)

def attention_branch(local_normed, q_weight, key_matrix, value_matrix, o_weight):
    length_total = local_normed.shape[0]
    token_positions = jnp.arange(length_total, dtype=jnp.float32)
    queries = local_input(rotary_embed(local_gradient(elementwise_product(local_normed, q_weight)), QUERY_HEADS, token_positions, 1.0))
    key_rows = local_input(rotary_embed(local_gradient(elementwise_product(local_normed, key_matrix)), KEY_VALUE_HEADS, token_positions, 1.0))
    gathered_values = local_input(local_gradient(elementwise_product(local_normed, value_matrix)))
    repeat_factor = QUERY_HEADS // KEY_VALUE_HEADS
    keys_expanded = jnp.repeat(key_rows.reshape(length_total, KEY_VALUE_HEADS, HEAD_SIZE), repeat_factor, axis=1)
    values_expanded = jnp.repeat(gathered_values.reshape(length_total, KEY_VALUE_HEADS, HEAD_SIZE), repeat_factor, axis=1)
    block = math.gcd(512, length_total)
    query_blocks = queries.reshape(length_total // block, block, QUERY_HEADS, HEAD_SIZE)
    starts = jnp.arange(length_total // block, dtype=jnp.int32) * block

    def attend(pieces):
        query_block, first_row = pieces
        scores = local_gradient(jnp.einsum('qhd,khd->hqk', query_block, keys_expanded, precision=HIGHEST) * HEAD_SIZE ** (-0.5))
        row_pos = first_row + jnp.arange(block, dtype=jnp.int32)
        col_pos = jnp.arange(length_total, dtype=jnp.int32)
        allowed = col_pos[None, :] <= row_pos[:, None]
        scores = jnp.where(allowed[None], scores, MASKED)
        probability = local_input(jax.nn.softmax(scores, axis=-1))
        return jnp.einsum('hqk,khd->qhd', probability, values_expanded, precision=HIGHEST).reshape(block, QUERY_HEADS * HEAD_SIZE)
    outputs = lax.map(jax.checkpoint(attend), (query_blocks, starts)).reshape(length_total, QUERY_HEADS * HEAD_SIZE)
    attended = local_input(local_gradient(outputs))
    return elementwise_product(attended, o_weight.T)

def layer(inputs, gain_first, z_weight, x_weight, bc_weight, dt_weight, conv_x_weight, conv_x_bias, conv_bc_weight, conv_bc_bias, dt_bias, decay_rate, skip_weight, out_weight, q_weight, key_matrix, value_matrix, o_weight, gain_second, gate_weight, up_weight, down_weight):
    local_normed = local_input(rms_norm(inputs, gain_first))
    attention_out = attention_branch(local_normed, q_weight, key_matrix, value_matrix, o_weight)
    mamba_out = mamba_branch(local_normed, z_weight, x_weight, bc_weight, dt_weight, conv_x_weight, conv_x_bias, conv_bc_weight, conv_bc_bias, dt_bias, decay_rate, skip_weight, out_weight)
    mixer_out = local_gradient(attention_out + mamba_out)
    hidden = inputs + mixer_out
    normed_second = local_input(rms_norm(hidden, gain_second))
    gate_pre = local_gradient(elementwise_product(normed_second, gate_weight))
    up_pre = local_gradient(elementwise_product(normed_second, up_weight))
    inner = local_input(jax.nn.silu(gate_pre) * up_pre)
    return hidden + elementwise_product(inner, down_weight.T)

def reference(tokens, cotangent, gain_first, z_weight, x_weight, bc_weight, dt_weight, conv_x_weight, conv_x_bias, conv_bc_weight, conv_bc_bias, dt_bias, decay_rate, skip_weight, out_weight, q_weight, key_matrix, value_matrix, o_weight, gain_second, gate_weight, up_weight, down_weight):
    sources = [tokens, gain_first, z_weight, x_weight, bc_weight, dt_weight, conv_x_weight, conv_x_bias, conv_bc_weight, conv_bc_bias, dt_bias, decay_rate, skip_weight, out_weight, q_weight, key_matrix, value_matrix, o_weight, gain_second, gate_weight, up_weight, down_weight]
    floats = [source.astype(jnp.float32) for source in sources]
    output, pullback = jax.vjp(layer, *floats)
    grads = pullback(cotangent.astype(jnp.float32))
    return (output.astype(jnp.bfloat16), grads[0], grads[1], grads[2], grads[3], grads[4], grads[5], grads[6], grads[7], grads[8], grads[9], grads[10], grads[11], grads[12], grads[13], grads[14], grads[15], grads[16], grads[17], grads[18], grads[19], grads[20], grads[21])
```

```python
import functools

import jax
import jax.numpy as jnp
from jax import lax
from jax.experimental import pallas as pl
from jax.experimental.pallas import tpu as pltpu
from jax.sharding import PartitionSpec as P

MODEL_WIDTH = 1024
NH = 24
P_SIZE = 64
NS = 128
HEAD_SIZE = 64
DSSM = 1536
TOK = 128
SPANS = 64
HALF_KV = TOK // 2
KEY_ROWS = SPANS * HALF_KV

EPS = 1e-06
ROPE_BASE = 100000000000.0
MASKED = -1e30
HIGHEST = lax.Precision.HIGHEST
BF16 = jnp.bfloat16
F32 = jnp.float32
SEQ = "seq"


def place(index):
    return (index // 32, (index // 8) % 4, (index // 2) % 4, index % 2)


def index_of(y, x, z, core):
    return ((y * 4 + x) * 4 + z) * 2 + core


def pairs(move):
    return [(source, index_of(*move(*place(source)))) for source in range(SPANS)]


OTHER_CORE = pairs(lambda y, x, z, c: (y, x, z, 1 - c))
OTHER_Y = pairs(lambda y, x, z, c: (1 - y, x, z, c))


def groups_by(key):
    found = {}
    for device in range(SPANS):
        found.setdefault(key(*place(device)), []).append(device)
    return list(found.values())


ACROSS_XY = groups_by(lambda y, x, z, c: (z, c))
ALONG_ZC = groups_by(lambda y, x, z, c: (y, x))


def along_x(steps):
    return pairs(lambda y, x, z, c: (y, (x + steps) % 4, z, c))


def along_z(steps):
    return pairs(lambda y, x, z, c: (y, x, (z + steps) % 4, c))


def send(value, route):
    return lax.ppermute(value, SEQ, route)


def after(value, token):
    return lax.optimization_barrier((value, token))[0]


def fetch(value, along):
    return [value] + [send(value, along(-step)) for step in (1, 2, 3)]


def gather_two(first, second):
    width = first.shape[1]
    both = jnp.concatenate([first, second], axis=1)
    theirs = send(both, OTHER_Y)
    first = jnp.concatenate([first, theirs[:, :width]], axis=0)
    second = jnp.concatenate([second, theirs[:, width:]], axis=0)
    first = jnp.concatenate(fetch(first, along_x), axis=0)
    second = jnp.concatenate(fetch(second, along_z), axis=0)
    first = fetch(first, along_z)
    second = fetch(second, along_x)
    first = first + [send(piece, OTHER_CORE) for piece in first]
    second = second + [send(piece, OTHER_CORE) for piece in second]
    return (first, second)


def gather_one(value):
    value = jnp.concatenate([value, send(value, OTHER_Y)], axis=0)
    value = jnp.concatenate(fetch(value, along_x), axis=0)
    pieces = fetch(value, along_z)
    return joined(pieces + [send(piece, OTHER_CORE) for piece in pieces])


def joined(pieces):
    return jnp.concatenate(pieces, axis=0)


def sum_from(value, along):
    blocks = value.reshape(4, -1, value.shape[-1])
    total = blocks[0]
    for step in (1, 2, 3):
        total = total + send(blocks[step].astype(BF16), along(step)).astype(F32)
    return total


def scatter_two(first_keep, first_send, second_keep, second_send):
    first = first_keep.astype(F32) + send(first_send, OTHER_CORE).astype(F32)
    second = second_keep.astype(F32) + send(second_send, OTHER_CORE).astype(F32)
    first = sum_from(first, along_z)
    second = sum_from(second, along_x)
    first = sum_from(first, along_x)
    second = sum_from(second, along_z)
    rows = first.shape[0] // 2
    width = first.shape[1]
    away = jnp.concatenate([first[rows:], second[rows:]], axis=1).astype(BF16)
    theirs = send(away, OTHER_Y).astype(F32)
    return (first[:rows] + theirs[:, :width], second[:rows] + theirs[:, width:])


def sum_heads(value):
    low = value.astype(BF16)
    theirs = lax.ppermute(low, "head", [(0, 1), (1, 0)])
    return low.astype(F32) + theirs.astype(F32)


def one_hot_orders(index):
    y, x, z, c = place(index)
    row = jnp.arange(MODEL_WIDTH, dtype=jnp.int32)
    inner = row % 16
    dy, low, high, dc = ((row // 16) % 2, (row // 32) % 4, (row // 128) % 4, row // 512)

    def one_hot(dx, dz):
        device = index_of((y + dy) % 2, (x + dx) % 4, (z + dz) % 4, (c + dc) % 2)
        return (row[:, None] == (device * 16 + inner)[None, :]).astype(BF16)

    return (one_hot(low, high), one_hot(high, low))


def exact_dot(left_side, right_side):
    return jnp.dot(left_side, right_side, precision=HIGHEST, preferred_element_type=F32)


def two_part_dot(values, one_hot):
    high = values.astype(BF16)
    low = (values - high.astype(F32)).astype(BF16)
    return project(high, one_hot) + project(low, one_hot)


def slots_of(key_block, index):
    y, x, z, c = (index >> 5, (index >> 3) & 3, (index >> 1) & 3, index & 1)
    dy = ((key_block >> 5) - y) & 1
    dx = ((key_block >> 3) - x) & 3
    dz = ((key_block >> 1) - z) & 3
    dc = (key_block - c) & 1
    first = ((dc * 4 + dz) * 4 + dx) * 2 + dy
    second = ((dc * 4 + dx) * 4 + dz) * 2 + dy
    return (pl.multiple_of(first * HALF_KV, HALF_KV), pl.multiple_of(second * HALF_KV, HALF_KV))


def load_pair(pair, index, first_ref, second_ref):
    parts = []
    for core in (0, 1):
        first, second = slots_of(pair * 2 + core, index)
        parts.append(first_ref[pl.ds(first, HALF_KV), :])
        parts.append(second_ref[pl.ds(second, HALF_KV), :])
    return jnp.concatenate(parts, axis=0)


def head_columns(rows):
    turned = rows.T
    heads = rows.shape[1] // HEAD_SIZE
    return jnp.concatenate(
        [turned[head * HEAD_SIZE : (head + 1) * HEAD_SIZE] for head in range(heads)], axis=1
    )


def head_rows(rows):
    heads = rows.shape[1] // HEAD_SIZE
    return jnp.concatenate(
        [rows[:, head * HEAD_SIZE : (head + 1) * HEAD_SIZE] for head in range(heads)], axis=0
    )


def rows_of_columns(columns):
    heads = columns.shape[1] // TOK
    stacked = jnp.concatenate(
        [columns[:, head * TOK : (head + 1) * TOK] for head in range(heads)], axis=0
    )
    return stacked.T


def pair_mask(scores, pair, index):
    shape = scores.shape
    keys = pair * (2 * TOK) + lax.broadcasted_iota(jnp.int32, shape, 0)
    queries = index * TOK + (lax.broadcasted_iota(jnp.int32, shape, 1) & (TOK - 1))
    return keys <= queries


def attend_kernel(index_ref, query_ref, first_ref, second_ref, columns_ref, rows_ref, log_ref, total_ref):
    index = index_ref[0]
    query = head_columns(query_ref[...].astype(F32) * HEAD_SIZE ** (-0.5))
    padded = jnp.concatenate([query, jnp.zeros_like(query)], axis=0).astype(BF16)
    total_ref[...] = jnp.zeros_like(total_ref)

    def step(pair, carry, masked):
        peak, weight = carry
        pair_kv = load_pair(pair, index, first_ref, second_ref)
        scores = jnp.dot(pair_kv, padded, preferred_element_type=F32)
        if masked:
            scores = jnp.where(pair_mask(scores, pair, index), scores, MASKED)
        new_peak = jnp.maximum(peak, jnp.max(scores, axis=0, keepdims=True))
        shrink = jnp.exp(peak - new_peak)
        probs = jnp.exp(scores - new_peak)
        weight = weight * shrink + jnp.sum(probs, axis=0, keepdims=True)
        total_ref[...] = total_ref[...] * shrink + lax.dot_general(
            pair_kv, probs.astype(BF16), (((0,), (0,)), ((), ())), preferred_element_type=F32
        )
        return (new_peak, weight)

    lanes = (1, query.shape[1])
    last = index >> 1
    carry = step(last, (jnp.full(lanes, MASKED, F32), jnp.zeros(lanes, F32)), True)
    peak, weight = lax.fori_loop(0, last, lambda pair, carry: step(pair, carry, False), carry)
    columns = total_ref[HEAD_SIZE:, :] / weight
    columns_ref[...] = columns
    rows_ref[...] = rows_of_columns(columns).astype(BF16)
    log_ref[...] = peak + jnp.log(weight)


def attend(index, query_low, first_kv, second_kv):
    width = query_low.shape[1]
    lanes = width // HEAD_SIZE * TOK
    vmem = pl.BlockSpec(memory_space=pltpu.VMEM)
    return pl.pallas_call(
        attend_kernel,
        out_shape=(
            jax.ShapeDtypeStruct((HEAD_SIZE, lanes), F32),
            jax.ShapeDtypeStruct((TOK, width), BF16),
            jax.ShapeDtypeStruct((1, lanes), F32),
        ),
        in_specs=[pl.BlockSpec(memory_space=pltpu.SMEM), vmem, vmem, vmem],
        out_specs=(vmem, vmem, vmem),
        scratch_shapes=[pltpu.VMEM((2 * HEAD_SIZE, lanes), F32)],
        compiler_params=pltpu.CompilerParams(vmem_limit_bytes=32 * 2**20),
        cost_estimate=pl.CostEstimate(
            flops=20_000_000_000, bytes_accessed=2_500_000, transcendentals=4_000_000
        ),
    )(index, query_low, first_kv, second_kv)


def attend_back_kernel(
    index_ref, query_ref, grad_ref, columns_ref, log_ref, first_ref, second_ref,
    grad_query_ref, grad_first_ref, grad_second_ref, total_ref,
):
    index = index_ref[0]
    scale = HEAD_SIZE ** (-0.5)
    query_rows = query_ref[...].astype(F32) * scale
    grad_rows = grad_ref[...].astype(F32)
    query = head_columns(query_rows)
    grad = head_columns(grad_rows)
    blank = jnp.zeros_like(query)
    query_pad = jnp.concatenate([query, blank], axis=0).astype(BF16)
    grad_pad = jnp.concatenate([blank, grad], axis=0).astype(BF16)
    query_tall = head_rows(query_rows)
    grad_tall = head_rows(grad_rows)
    blank = jnp.zeros_like(query_tall)
    sides = jnp.concatenate(
        [
            jnp.concatenate([query_tall, blank], axis=1),
            jnp.concatenate([blank, grad_tall], axis=1),
        ],
        axis=0,
    ).astype(BF16)
    delta = jnp.sum(grad * columns_ref[...], axis=0, keepdims=True)
    log_total = log_ref[...]
    total_ref[...] = jnp.zeros_like(total_ref)
    grad_first_ref[...] = jnp.zeros_like(grad_first_ref)
    grad_second_ref[...] = jnp.zeros_like(grad_second_ref)

    def step(pair, masked):
        pair_kv = load_pair(pair, index, first_ref, second_ref)
        scores = jnp.dot(pair_kv, query_pad, preferred_element_type=F32)
        grad_probs = jnp.dot(pair_kv, grad_pad, preferred_element_type=F32)
        probs = jnp.exp(scores - log_total)
        if masked:
            probs = jnp.where(pair_mask(scores, pair, index), probs, 0.0)
        grad_scores = (probs * (grad_probs - delta)).astype(BF16)
        total_ref[...] += lax.dot_general(
            pair_kv, grad_scores, (((0,), (0,)), ((), ())), preferred_element_type=F32
        )
        both = jnp.concatenate([grad_scores, probs.astype(BF16)], axis=1)
        term = jnp.dot(both, sides, preferred_element_type=F32).astype(BF16)
        for core in (0, 1):
            first, second = slots_of(pair * 2 + core, index)
            low = core * TOK
            grad_first_ref[pl.ds(first, HALF_KV), :] = term[low : low + HALF_KV]
            grad_second_ref[pl.ds(second, HALF_KV), :] = term[low + HALF_KV : low + TOK]

    last = index >> 1
    step(last, True)

    def loop(pair, carry):
        step(pair, False)
        return carry

    lax.fori_loop(0, last, loop, 0)
    grad_query_ref[...] = rows_of_columns(total_ref[:HEAD_SIZE, :] * scale)


def attend_back(index, query_low, grad_low, columns, log_total, first_kv, second_kv):
    vmem = pl.BlockSpec(memory_space=pltpu.VMEM)
    return pl.pallas_call(
        attend_back_kernel,
        out_shape=(
            jax.ShapeDtypeStruct(query_low.shape, F32),
            jax.ShapeDtypeStruct(first_kv.shape, BF16),
            jax.ShapeDtypeStruct(second_kv.shape, BF16),
        ),
        in_specs=[pl.BlockSpec(memory_space=pltpu.SMEM)] + [vmem] * 6,
        out_specs=(vmem, vmem, vmem),
        scratch_shapes=[pltpu.VMEM((2 * HEAD_SIZE, columns.shape[1]), F32)],
        compiler_params=pltpu.CompilerParams(vmem_limit_bytes=40 * 2**20),
        cost_estimate=pl.CostEstimate(
            flops=40_000_000_000, bytes_accessed=5_000_000, transcendentals=4_000_000
        ),
    )(index, query_low, grad_low, columns, log_total, first_kv, second_kv)


def states_kernel(reverse, decay_ref, local_ref, out_ref):
    def step(position, state):
        span = SPANS - 1 - position if reverse else position
        out_ref[span] = state
        return decay_ref[span] * state + local_ref[span]

    lax.fori_loop(0, SPANS, step, jnp.zeros(out_ref.shape[1:], F32), unroll=8)


def states_between(decays, local, reverse):
    return pl.pallas_call(
        functools.partial(states_kernel, reverse),
        out_shape=jax.ShapeDtypeStruct(local.shape, F32),
        in_specs=[pl.BlockSpec(memory_space=pltpu.VMEM)] * 2,
        out_specs=pl.BlockSpec(memory_space=pltpu.VMEM),
    )(decays, local)


def swap_spans(value):
    return lax.all_to_all(value, SEQ, 0, 0, tiled=True)


def project(left_side, right_side):
    return jnp.dot(left_side, right_side, preferred_element_type=jnp.float32)


def project_back(left_side, right_side):
    return lax.dot_general(
        left_side, right_side, (((1,), (1,)), ((), ())), preferred_element_type=jnp.float32
    )


def weight_term(left_side, right_side):
    return lax.dot_general(
        left_side, right_side, (((0,), (0,)), ((), ())), preferred_element_type=jnp.float32
    )


def rms_norm(values, norm_gain):
    return values * lax.rsqrt(jnp.mean(values * values, axis=-1, keepdims=True) + EPS) * norm_gain


def rotary_embed(values, head_count, token_positions, sign_value):
    half_dim = HEAD_SIZE // 2
    frequency = ROPE_BASE ** (-jnp.arange(half_dim, dtype=jnp.float32) * (1.0 / half_dim))
    angles = token_positions[:, None] * frequency[None, :]
    cosine = jnp.cos(angles)[:, None, :]
    sine_part = sign_value * jnp.sin(angles)[:, None, :]
    shaped = values.reshape(values.shape[0], head_count, HEAD_SIZE)
    first_half = shaped[..., :half_dim]
    second_half = shaped[..., half_dim:]
    turned = jnp.concatenate(
        [
            first_half * cosine - second_half * sine_part,
            second_half * cosine + first_half * sine_part,
        ],
        axis=-1,
    )
    return turned.reshape(values.shape[0], head_count * HEAD_SIZE)


def conv_split(extended, conv_weight, conv_bias, dt_raw, dt_bias):
    kernel = conv_weight.shape[0]
    step_count = dt_raw.shape[0]
    head_count = dt_raw.shape[1]
    summed = conv_bias + sum(
        (
            conv_weight[lag_index] * extended[lag_index : lag_index + step_count]
            for lag_index in range(kernel)
        )
    )
    conved = jax.nn.silu(summed)
    width = head_count * P_SIZE
    head_inputs = conved[:, :width].reshape(step_count, head_count, P_SIZE)
    in_vectors = conved[:, width : width + NS]
    out_vectors = conved[:, width + NS :]
    step_size = jax.nn.softplus(dt_raw + dt_bias)
    return (head_inputs, step_size, in_vectors, out_vectors)


def ssd_span(carry_state, pieces, decay_rate, skip_weight):
    head_inputs, step_size, in_vectors, out_vectors = pieces
    step_count = head_inputs.shape[0]
    log_decay = jnp.cumsum(-step_size * decay_rate, axis=0)
    causal = jnp.arange(step_count)[:, None] >= jnp.arange(step_count)[None, :]
    differ = log_decay[:, None, :] - log_decay[None, :, :]
    weights_ts = jnp.where(
        causal[:, :, None], jnp.exp(jnp.where(causal[:, :, None], differ, 0.0)), 0.0
    )
    intersection = jnp.dot(out_vectors, in_vectors.T, precision=HIGHEST)
    mixing = intersection[:, :, None] * weights_ts * step_size[None, :, :]
    inner_out = jnp.einsum("tsh,shp->thp", mixing, head_inputs, precision=HIGHEST)
    decay_now = jnp.exp(log_decay)
    carried_out = decay_now[:, :, None] * jnp.einsum(
        "tn,hpn->thp", out_vectors, carry_state, precision=HIGHEST
    )
    outputs = inner_out + carried_out + skip_weight[None, :, None] * head_inputs
    to_end = jnp.exp(log_decay[-1][None, :] - log_decay) * step_size
    new_state = decay_now[-1][:, None, None] * carry_state + jnp.einsum(
        "sh,shp,sn->hpn", to_end, head_inputs, in_vectors, precision=HIGHEST
    )
    return (new_state, outputs)


def mamba_local(
    extended, dt_raw, gate_raw, conv_weight, conv_bias, dt_bias, decay_rate, skip_weight, state_in
):
    pieces = conv_split(extended, conv_weight, conv_bias, dt_raw, dt_bias)
    new_state, outputs = ssd_span(state_in, pieces, decay_rate, skip_weight)
    gated = outputs.reshape(outputs.shape[0], -1) * jax.nn.silu(gate_raw)
    return (gated, new_state)


def shards(
    tokens,
    cotangent,
    gain_first,
    z_weight,
    x_weight,
    bc_weight,
    dt_weight,
    conv_x_weight,
    conv_x_bias,
    conv_bc_weight,
    conv_bc_bias,
    dt_bias,
    decay_rate,
    skip_weight,
    out_weight,
    q_weight,
    key_matrix,
    value_matrix,
    o_weight,
    gain_second,
    gate_weight,
    up_weight,
    down_weight,
):
    index = lax.axis_index(SEQ)
    head_index = lax.axis_index("head")
    step_count = tokens.shape[0]
    index_word = jnp.reshape(index, (1,)).astype(jnp.int32)

    with jax.named_scope("gather_mixer_in"):
        dt_wide = jnp.pad(dt_weight, ((0, 0), (0, 128 - dt_weight.shape[1])))
        in_first, in_second = gather_two(
            jnp.concatenate([x_weight, bc_weight], axis=1),
            jnp.concatenate([z_weight, q_weight, key_matrix, value_matrix, dt_wide], axis=1),
        )
    with jax.named_scope("gather_rest"):
        rest_full = lax.all_gather(
            jnp.concatenate([gate_weight, up_weight, out_weight, o_weight, down_weight], axis=1),
            SEQ, axis=0, tiled=True,
        )
    with jax.named_scope("orders"):
        to_a, to_b = one_hot_orders(index)
        inputs = tokens.astype(F32)
        cot_float = cotangent.astype(F32)
        cot_low = cotangent
        normed = rms_norm(inputs, gain_first).astype(BF16)
        normed_a = project(normed, to_a).astype(BF16)
        normed_b = project(normed, to_b).astype(BF16)
    with jax.named_scope("project_in"):
        in_a = joined(in_first)
        in_b = joined(in_second)
        raw_a = project(normed_a, in_a)
        raw_b = project(normed_b, in_b)
        dssm_local = x_weight.shape[1]
        query_width = q_weight.shape[1]
        head_count = dt_weight.shape[1]
        query_at = dssm_local
        key_at = query_at + query_width
        value_at = key_at + HEAD_SIZE
        dt_at = value_at + HEAD_SIZE
        gate_raw = raw_b[:, :dssm_local]
        q_raw = raw_b[:, query_at:key_at]
        k_raw = raw_b[:, key_at:value_at]
        v_raw = raw_b[:, value_at:dt_at]
        dt_raw = raw_b[:, dt_at : dt_at + head_count]
    with jax.named_scope("rope"):
        token_positions = (index * step_count + jnp.arange(step_count, dtype=jnp.int32)).astype(F32)
        query_heads = query_width // HEAD_SIZE
        query_low = rotary_embed(q_raw, query_heads, token_positions, 1.0).astype(BF16)
        key_low = rotary_embed(k_raw, 1, token_positions, 1.0).astype(BF16)
        both_kv = jnp.concatenate([key_low, v_raw.astype(BF16)], axis=1)
    with jax.named_scope("gather_kv"):
        first_kv, second_kv = gather_two(both_kv[:HALF_KV], both_kv[HALF_KV:])
        first_kv, second_kv = (joined(first_kv), joined(second_kv))
    with jax.named_scope("conv"):
        kernel = conv_x_weight.shape[0]
        conv_input = raw_a
        halo_route = [(span, span + 1) for span in range(SPANS - 1)]
        halo_rows = send(conv_input[step_count - (kernel - 1) :], halo_route)
        extended = jnp.concatenate([halo_rows, conv_input], axis=0)
        conv_weight = jnp.concatenate([conv_x_weight, conv_bc_weight], axis=1)
        conv_bias = jnp.concatenate([conv_x_bias, conv_bc_bias], axis=0)
        head_inputs, step_size, in_vectors, out_vectors = conv_split(
            extended, conv_weight, conv_bias, dt_raw, dt_bias
        )
    with jax.named_scope("state_forward"):
        log_decay = jnp.cumsum(-step_size * decay_rate, axis=0)
        to_end = jnp.exp(log_decay[-1][None, :] - log_decay) * step_size
        local_state = jnp.einsum("sh,shp,sn->phn", to_end, head_inputs, in_vectors, precision=HIGHEST)
        span_decay = jnp.pad(jnp.exp(log_decay[-1]), (0, NS - head_count))
        payload = jnp.concatenate(
            [local_state, jnp.broadcast_to(span_decay[None, None, :], (P_SIZE, 1, NS))], axis=1
        )
        arrived = swap_spans(payload)
        decays = jnp.broadcast_to(arrived[:, head_count, :head_count, None], (SPANS, head_count, NS))
        entering = states_between(decays, arrived[:, :head_count], False)
        state_in = swap_spans(entering).transpose(1, 0, 2)

    def mamba_piece(
        extended, dt_raw, gate_raw, conv_weight, conv_bias, dt_bias, decay_rate, skip_weight
    ):
        return mamba_local(
            extended, dt_raw, gate_raw, conv_weight, conv_bias, dt_bias, decay_rate, skip_weight,
            state_in,
        )

    with jax.named_scope("ssd"):
        gated, state_out = mamba_piece(
            extended, dt_raw, gate_raw, conv_weight, conv_bias, dt_bias, decay_rate, skip_weight
        )
        gated_low = gated.astype(BF16)
    with jax.named_scope("attention"):
        attended_columns, attended_low, log_total = attend(index_word, query_low, first_kv, second_kv)
    with jax.named_scope("mixer_out"):
        ff_local = gate_weight.shape[1]
        at = 0
        parts = []
        for width in (ff_local, ff_local, dssm_local, query_width, ff_local):
            parts.append(rest_full[:, at : at + width])
            at += width
        gate_full, up_full, out_full, o_full, down_full = parts
        mixer_out = sum_heads(project_back(attended_low, o_full) + project_back(gated_low, out_full))
        hidden = inputs + mixer_out
    with jax.named_scope("ffn"):
        normed_second = rms_norm(hidden, gain_second).astype(BF16)
        gate_pre = project(normed_second, gate_full)
        up_pre = project(normed_second, up_full)
        sigmoid_gate = jax.nn.sigmoid(gate_pre)
        silu_gate = gate_pre * sigmoid_gate
        inner_low = (silu_gate * up_pre).astype(BF16)
        grad_inner = project(cot_low, down_full)
        silu_slope = sigmoid_gate * (1.0 + gate_pre * (1.0 - sigmoid_gate))
        grad_gate_low = (grad_inner * up_pre * silu_slope).astype(BF16)
        grad_up_low = (grad_inner * silu_gate).astype(BF16)
        second_part = project_back(grad_gate_low, gate_full) + project_back(grad_up_low, up_full)
    with jax.named_scope("norm_second_back"):
        grad_second = sum_heads(second_part)
        second_scale = lax.rsqrt(jnp.mean(hidden * hidden, axis=-1, keepdims=True) + EPS)
        gain_second_part = jnp.sum(second_part * hidden * second_scale, axis=0)
        second_out, second_pull = jax.vjp(lambda values: rms_norm(values, gain_second), hidden)
        grad_hidden = cot_float + second_pull(grad_second)[0]
        grad_mixed = grad_hidden.astype(BF16)
    with jax.named_scope("mixer_out_back"):
        grad_attended = project(grad_mixed, o_full).astype(BF16)
        grad_gated = project(grad_mixed, out_full)
    with jax.named_scope("output"):
        ffn_out = sum_heads(project_back(inner_low, down_full))
        output = (hidden + ffn_out).astype(BF16)
    with jax.named_scope("rest_grads"):
        rest_terms = jnp.concatenate(
            [
                weight_term(normed_second, grad_gate_low).astype(BF16),
                weight_term(normed_second, grad_up_low).astype(BF16),
                weight_term(grad_mixed, gated_low).astype(BF16),
                weight_term(grad_mixed, attended_low).astype(BF16),
                weight_term(cot_low, inner_low).astype(BF16),
            ],
            axis=1,
        )
        rest_terms = lax.psum_scatter(
            rest_terms, SEQ, scatter_dimension=0, axis_index_groups=ACROSS_XY, tiled=True
        )
        rest_grads = lax.psum_scatter(
            rest_terms.astype(F32), SEQ, scatter_dimension=0, axis_index_groups=ALONG_ZC, tiled=True
        )
        at = 0
        parts = []
        for width in (ff_local, ff_local, dssm_local, query_width, ff_local):
            parts.append(rest_grads[:, at : at + width])
            at += width
        grad_gate, grad_up, grad_out, grad_o, grad_down = parts
    with jax.named_scope("state_backward"):
        grad_outputs = (grad_gated * jax.nn.silu(gate_raw)).reshape(step_count, head_count, P_SIZE)
        local_grad = jnp.einsum(
            "th,thp,tn->phn", jnp.exp(log_decay), grad_outputs, out_vectors, precision=HIGHEST
        )
        leaving = states_between(decays, swap_spans(local_grad), True)
        state_grad = swap_spans(leaving).transpose(1, 0, 2)
    with jax.named_scope("attention_back"):
        grad_query, grad_first_kv, grad_second_kv = attend_back(
            index_word, query_low, grad_attended, attended_columns, log_total, first_kv, second_kv
        )
        split = KEY_ROWS // 2
        grad_first_kv, grad_second_kv = scatter_two(
            grad_first_kv[:split], grad_first_kv[split:], grad_second_kv[:split], grad_second_kv[split:]
        )
        own_kv = jnp.concatenate([grad_first_kv, grad_second_kv], axis=0)
        grad_q_low = rotary_embed(grad_query, query_heads, token_positions, -1.0).astype(BF16)
        grad_k_low = rotary_embed(own_kv[:, :HEAD_SIZE], 1, token_positions, -1.0).astype(BF16)
        grad_v_low = own_kv[:, HEAD_SIZE:].astype(BF16)
    with jax.named_scope("ssd_back"):
        primal, pullback = jax.vjp(
            mamba_piece, extended, dt_raw, gate_raw, conv_weight, conv_bias, dt_bias, decay_rate,
            skip_weight,
        )
        (
            grad_extended, grad_dt_raw, grad_gate_raw, grad_conv_weight, grad_conv_bias,
            grad_dt_bias, grad_decay, grad_skip,
        ) = pullback((grad_gated, state_grad))
        back_route = [(span + 1, span) for span in range(SPANS - 1)]
        returned = send(grad_extended[: kernel - 1], back_route)
        grad_conv_input = grad_extended[kernel - 1 :]
        split_row = step_count - (kernel - 1)
        grad_conv_input = jnp.concatenate(
            [grad_conv_input[:split_row], grad_conv_input[split_row:] + returned], axis=0
        )
    with jax.named_scope("project_in_back"):
        low_a = grad_conv_input.astype(BF16)
        grad_dt_wide = jnp.pad(grad_dt_raw.astype(BF16), ((0, 0), (0, 128 - head_count)))
        low_b = jnp.concatenate(
            [grad_gate_raw.astype(BF16), grad_q_low, grad_k_low, grad_v_low, grad_dt_wide], axis=1
        )
        first_part = two_part_dot(project_back(low_a, in_a), to_a.T)
        first_part = first_part + two_part_dot(project_back(low_b, in_b), to_b.T)
        first_scale = lax.rsqrt(jnp.mean(inputs * inputs, axis=-1, keepdims=True) + EPS)
        gain_first_part = jnp.sum(first_part * inputs * first_scale, axis=0)
        grad_first = sum_heads(first_part)
        first_out, first_pull = jax.vjp(lambda values: rms_norm(values, gain_first), inputs)
        grad_tokens = grad_hidden + first_pull(grad_first)[0]
    with jax.named_scope("in_grads"):
        half = MODEL_WIDTH // 2
        in_grad_a, in_grad_b = scatter_two(
            weight_term(normed_a[:, :half], low_a),
            weight_term(normed_a[:, half:], low_a).astype(BF16),
            weight_term(normed_b[:, :half], low_b),
            weight_term(normed_b[:, half:], low_b).astype(BF16),
        )
        grad_x = in_grad_a[:, :dssm_local]
        own_bc = in_grad_a[:, dssm_local:]
        grad_bc = own_bc + lax.ppermute(own_bc, "head", [(0, 1), (1, 0)])
        grad_z = in_grad_b[:, :dssm_local]
        grad_q = in_grad_b[:, query_at:key_at]
        grad_k = in_grad_b[:, key_at:value_at]
        grad_v = in_grad_b[:, value_at:dt_at]
        grad_dt = in_grad_b[:, dt_at : dt_at + head_count]
    with jax.named_scope("small_grads"):
        gain_parts = jnp.stack([gain_first_part, gain_second_part])
        shared = jnp.concatenate(
            [
                gain_parts.reshape(-1),
                grad_conv_weight[:, dssm_local:].reshape(-1),
                grad_conv_bias[dssm_local:],
            ]
        )
        apart = jnp.concatenate(
            [
                grad_conv_weight[:, :dssm_local].reshape(-1),
                grad_conv_bias[:dssm_local],
                grad_dt_bias,
                grad_decay,
                grad_skip,
            ]
        )
        shared_count = shared.shape[0]
        small = jnp.concatenate([shared, apart])
        small = jnp.pad(small, (0, -small.shape[0] % 1024)).reshape(-1, 128)
        for bit in (1, 2, 4, 8, 16, 32):
            small = small + send(small, [(span, span ^ bit) for span in range(SPANS)])
        rows = -(-shared_count // 128)
        shared = small[:rows]
        shared = (shared + lax.ppermute(shared, "head", [(0, 1), (1, 0)])).reshape(-1)
        apart = small.reshape(-1)[shared_count:]
        width = MODEL_WIDTH
        summed_gain_first, summed_gain_second = (shared[:width], shared[width : 2 * width])
        at = 2 * width
        summed_conv_bc = shared[at : at + kernel * 2 * NS].reshape(kernel, 2 * NS)
        at += kernel * 2 * NS
        summed_conv_bcb = shared[at : at + 2 * NS]
        grad_conv_x = apart[: kernel * dssm_local].reshape(kernel, dssm_local)
        at = kernel * dssm_local
        grad_conv_xb = apart[at : at + dssm_local]
        at += dssm_local
        grad_dt_bias_own = apart[at : at + head_count]
        grad_decay_own = apart[at + head_count : at + 2 * head_count]
        grad_skip_own = apart[at + 2 * head_count : at + 3 * head_count]
    return (
        output,
        grad_tokens,
        summed_gain_first,
        grad_z,
        grad_x,
        grad_bc,
        grad_dt,
        grad_conv_x,
        grad_conv_xb,
        summed_conv_bc,
        summed_conv_bcb,
        grad_dt_bias_own,
        grad_decay_own,
        grad_skip_own,
        grad_out,
        grad_q,
        grad_k,
        grad_v,
        grad_o,
        summed_gain_second,
        grad_gate,
        grad_up,
        grad_down,
    )


def solution(mesh):
    return jax.shard_map(
        shards,
        mesh=mesh,
        in_specs=(
            P("seq", None),
            P("seq", None),
            P(),
            P("seq", "head"),
            P("seq", "head"),
            P("seq", None),
            P("seq", "head"),
            P(None, "head"),
            P("head"),
            P(),
            P(),
            P("head"),
            P("head"),
            P("head"),
            P("seq", "head"),
            P("seq", "head"),
            P("seq", "head"),
            P("seq", "head"),
            P("seq", "head"),
            P(),
            P("seq", "head"),
            P("seq", "head"),
            P("seq", "head"),
        ),
        out_specs=(
            P("seq", None),
            P("seq", None),
            P(),
            P("seq", "head"),
            P("seq", "head"),
            P("seq", None),
            P("seq", "head"),
            P(None, "head"),
            P("head"),
            P(),
            P(),
            P("head"),
            P("head"),
            P("head"),
            P("seq", "head"),
            P("seq", "head"),
            P("seq", "head"),
            P("seq", "head"),
            P("seq", "head"),
            P(),
            P("seq", "head"),
            P("seq", "head"),
            P("seq", "head"),
        ),
        check_vma=False,
    )
```

```python
import functools

import jax
import jax.numpy as jnp
from jax import lax
from jax.experimental import pallas as pl
from jax.experimental.pallas import tpu as pltpu
from jax.sharding import PartitionSpec as P

MODEL_WIDTH = 1024
NH = 24
P_SIZE = 64
NS = 128
HEAD_SIZE = 64
CONV_K = 4
TOK = 128
SPANS = 64
HEADS = 12
WIDTH = HEADS * P_SIZE
QUERY_WIDTH = 256
ROPED = QUERY_WIDTH + 2 * HEAD_SIZE
SLOTS = 16
HALO = 16
KEY_ROWS = SPANS // 2 * TOK

EPS = 1e-06
ROPE_BASE = 100000000000.0
MASKED = -1e30
HIGHEST = lax.Precision.HIGHEST
BF16 = jnp.bfloat16
F32 = jnp.float32
SEQ = "seq"


def place(index):
    return (index // 32, (index // 8) % 4, (index // 2) % 4, index % 2)


def index_of(y, x, z, core):
    return ((y * 4 + x) * 4 + z) * 2 + core


def pairs(move):
    return [(source, index_of(*move(*place(source)))) for source in range(SPANS)]


OTHER_CORE = pairs(lambda y, x, z, c: (y, x, z, 1 - c))
OTHER_Y = pairs(lambda y, x, z, c: (1 - y, x, z, c))
OTHER_HEAD = [(0, 1), (1, 0)]
ONWARD = [(span, span + 1) for span in range(SPANS - 1)]
BACKWARD = [(span + 1, span) for span in range(SPANS - 1)]


def along_x(steps):
    return pairs(lambda y, x, z, c: (y, (x + steps) % 4, z, c))


def along_z(steps):
    return pairs(lambda y, x, z, c: (y, x, (z + steps) % 4, c))


def send(value, route):
    return lax.ppermute(value, SEQ, route)


def swap_heads(value):
    return lax.ppermute(value, "head", OTHER_HEAD)


def swap_spans(value):
    return lax.all_to_all(value, SEQ, 0, 0, tiled=True)


def after(value, *others):
    return lax.optimization_barrier((value, others))[0]


def joined(pieces):
    return jnp.concatenate(pieces, axis=0)


def fetch(value, along):
    return [value] + [send(value, along(-step)) for step in (1, 2, 3)]


def ring_near(value, along):
    return (value, send(value, along(-1)), send(value, along(1)))


def ring_far(near, along):
    own, ahead, behind = near
    half = own.shape[0] // 2
    first = send(ahead[:half], along(-1))
    second = send(behind[half:], along(1))
    return [own, ahead, first, second, behind]


def blocks_of(parts, count):
    rows = parts[0].shape[0] // count
    return [
        sum(part[block * rows : (block + 1) * rows].astype(F32) for part in parts)
        for block in range(count)
    ]


def spread(blocks, along):
    return [send(block.astype(BF16), along(step)) for step, block in enumerate(blocks) if step]


def ring_sum(blocks, arrived):
    return blocks[0] + sum(block.astype(F32) for block in arrived)


def scatter_ring(parts, along):
    blocks = blocks_of(parts, 4)
    return ring_sum(blocks, spread(blocks, along))


def one_hot_orders(index):
    y, x, z, c = place(index)
    row = jnp.arange(MODEL_WIDTH, dtype=jnp.int32)
    inner = row % 16
    dy, low, high, dc = ((row // 16) % 2, (row // 32) % 4, (row // 128) % 4, row // 512)

    def one_hot(dx, dz):
        device = index_of((y + dy) % 2, (x + dx) % 4, (z + dz) % 4, (c + dc) % 2)
        return (row[:, None] == (device * 16 + inner)[None, :]).astype(BF16)

    return (one_hot(low, high), one_hot(high, low))


def project(left_side, right_side):
    return jnp.dot(left_side, right_side, preferred_element_type=F32)


def rms_norm(values, norm_gain):
    return values * lax.rsqrt(jnp.mean(values * values, axis=-1, keepdims=True) + EPS) * norm_gain


def rotary_tables(index):
    half = HEAD_SIZE // 2
    frequency = ROPE_BASE ** (-jnp.arange(half, dtype=F32) * (1.0 / half))
    positions = (index * TOK + jnp.arange(TOK, dtype=jnp.int32)).astype(F32)
    angles = positions[:, None] * frequency[None, :]
    cosine, sine = (jnp.cos(angles), jnp.sin(angles))
    turns = QUERY_WIDTH // HEAD_SIZE + 1
    plain = jnp.ones((TOK, HEAD_SIZE), F32)
    return (
        jnp.concatenate([cosine, cosine] * turns + [plain], axis=1),
        jnp.concatenate([-sine, sine] * turns + [0.0 * plain], axis=1),
    )


def dot_f32(left_side, right_side, left_dim=1, right_dim=0):
    return lax.dot_general(
        left_side, right_side, (((left_dim,), (right_dim,)), ((), ())), precision=HIGHEST,
        preferred_element_type=F32,
    )


def dot_low(left_side, right_side, left_dim=1, right_dim=0):
    return lax.dot_general(
        left_side, right_side, (((left_dim,), (right_dim,)), ((), ())), preferred_element_type=F32
    )


def lanes_of(shape):
    return lax.broadcasted_iota(jnp.int32, shape, len(shape) - 1)


def rows_of(shape):
    return lax.broadcasted_iota(jnp.int32, shape, len(shape) - 2)


def head_spread():
    shape = (NS, HEADS * P_SIZE)
    return (lanes_of(shape) // P_SIZE == rows_of(shape)).astype(F32)


def causal_mask():
    return rows_of((TOK, TOK)) >= lanes_of((TOK, TOK))


def sigmoid(values):
    return 1.0 / (1.0 + jnp.exp(-values))


def softplus(values):
    small = jnp.exp(-jnp.abs(values))
    series = small * (1.0 - small * (0.5 - small * (1.0 / 3.0 - small * 0.25)))
    return jnp.maximum(values, 0.0) + jnp.where(small < 0.01, series, jnp.log(1.0 + small))


def turn(values, cosine, sine):
    width = values.shape[1]
    half = HEAD_SIZE // 2
    ahead = pltpu.roll(values, width - half, 1)
    behind = pltpu.roll(values, half, 1)
    other = jnp.where(lanes_of(values.shape) % HEAD_SIZE < half, ahead, behind)
    return values * cosine + other * sine


def kernel_call(body, outs, *operands, scratch=(), vmem=16, us=1, name=None):
    vspec = pl.BlockSpec(memory_space=pltpu.VMEM)
    return pl.pallas_call(
        body,
        out_shape=tuple(jax.ShapeDtypeStruct(shape, dtype) for shape, dtype in outs),
        in_specs=[vspec] * len(operands),
        out_specs=(vspec,) * len(outs),
        scratch_shapes=list(scratch),
        compiler_params=pltpu.CompilerParams(vmem_limit_bytes=vmem * 2**20),
        cost_estimate=pl.CostEstimate(flops=us * 10**9, bytes_accessed=0, transcendentals=0),
        name=name,
    )(*operands)


def attention_in_kernel(
    normed_ref, own_ref, other_ref, cosine_ref, sine_ref, dt_bias_ref, decay_ref,
    gate_ref, query_ref, kv_ref, dt_ref, step_ref, log_ref,
):
    normed = normed_ref[...]
    half = MODEL_WIDTH // 2
    raw = dot_low(normed[:, :half], own_ref[...]) + dot_low(normed[:, half:], other_ref[...])
    gate_ref[...] = raw[:, :WIDTH]
    turned = turn(raw[:, WIDTH : WIDTH + ROPED], cosine_ref[...], sine_ref[...]).astype(BF16)
    query_ref[...] = turned[:, :QUERY_WIDTH]
    kv_ref[...] = turned[:, QUERY_WIDTH:]
    dt = raw[:, WIDTH + ROPED :] + dt_bias_ref[...]
    step = softplus(dt)
    dt_ref[...] = dt
    step_ref[...] = step
    log_ref[...] = dot_f32(causal_mask().astype(F32), -step * decay_ref[...])


def convolved(ext_ref, conv_weight, conv_bias):
    summed = conv_bias
    for lag in range(CONV_K):
        summed = summed + conv_weight[lag : lag + 1] * ext_ref[pl.ds(HALO - CONV_K + 1 + lag, TOK), :]
    return summed


def ssm_in_kernel(
    normed_ref, own_ref, other_ref, conv_weight_ref, conv_bias_ref, step_ref, log_ref,
    ext_ref, conv_ref, state_ref,
):
    normed = normed_ref[...]
    half = MODEL_WIDTH // 2
    ext_ref[...] = dot_low(normed[:, :half], own_ref[...]) + dot_low(normed[:, half:], other_ref[...])
    summed = convolved(ext_ref, conv_weight_ref[...], conv_bias_ref[...])
    conved = summed * sigmoid(summed)
    conv_ref[...] = conved
    log_decay = log_ref[...]
    last = log_decay[TOK - 1 :]
    to_end = jnp.exp(last - log_decay) * step_ref[...]
    weighted = conved[:, :WIDTH] * dot_f32(to_end, head_spread())
    local = dot_f32(weighted.T, conved[:, WIDTH : WIDTH + NS])
    state_ref[...] = jnp.zeros_like(state_ref)
    for head in range(HEADS):
        state_ref[:, head, :] = local[head * P_SIZE : (head + 1) * P_SIZE]
    state_ref[:, HEADS, :] = jnp.broadcast_to(jnp.exp(last), (P_SIZE, NS))


def states_kernel(reverse, decay_ref, local_ref, out_ref):
    decays = decay_ref[:, HEADS, :].T[:SLOTS]
    state = jnp.zeros((SLOTS, NS), F32)
    for position in range(SPANS):
        span = SPANS - 1 - position if reverse else position
        out_ref[span] = state
        if position < SPANS - 1:
            state = decays[:, span : span + 1] * state + local_ref[span]


def states_between(decays, local, reverse):
    return kernel_call(
        functools.partial(states_kernel, reverse), [((SPANS, SLOTS, NS), F32)], decays, local,
        vmem=16, name="states",
    )[0]


def head_decay(log_decay, log_rows, head):
    apart = jnp.minimum(log_decay[:, head : head + 1] - log_rows[head : head + 1], 0.0)
    return jnp.where(causal_mask(), jnp.exp(apart), 0.0)


def stacked_states(state_ref):
    return jnp.concatenate([state_ref[:, head, :] for head in range(HEADS)], axis=0)


def first_of_pair(shape):
    return lanes_of(shape) < P_SIZE


def ssm_out_kernel(
    conv_ref, step_ref, log_ref, state_ref, gate_ref, skip_ref, gated_ref, y_ref
):
    conved = conv_ref[...]
    in_vectors = conved[:, WIDTH : WIDTH + NS]
    out_vectors = conved[:, WIDTH + NS :]
    log_decay = log_ref[...]
    log_rows = log_decay.T
    step_rows = step_ref[...].T
    spread = head_spread()
    both = dot_f32(out_vectors, in_vectors, 1, 1)
    carried = dot_f32(out_vectors, stacked_states(state_ref), 1, 1)
    skip = dot_f32(jnp.broadcast_to(skip_ref[...], (8, NS)), spread)[:1]
    outer = dot_f32(jnp.exp(log_decay), spread) * carried + skip * conved[:, :WIDTH]
    for pair in range(HEADS // 2):
        lanes = slice(pair * 2 * P_SIZE, (pair + 1) * 2 * P_SIZE)
        inputs = conved[:, lanes]
        parts = []
        for head in (2 * pair, 2 * pair + 1):
            mixing = both * head_decay(log_decay, log_rows, head) * step_rows[head : head + 1]
            parts.append(dot_f32(mixing, inputs))
        y = outer[:, lanes] + jnp.where(first_of_pair(inputs.shape), parts[0], parts[1])
        gate = gate_ref[:, lanes]
        y_ref[:, lanes] = y
        gated_ref[:, lanes] = (y * gate * sigmoid(gate)).astype(BF16)


def mixer_out_kernel(gated_ref, attended_ref, own_ref, other_ref, order_ref, out_ref):
    mixed = jnp.concatenate([gated_ref[...], attended_ref[...]], axis=1)
    wide = mixed.shape[1]
    parts = [dot_low(mixed, ref[:, :wide], 1, 1).astype(BF16) for ref in (own_ref, other_ref)]
    out_ref[...] = dot_low(jnp.concatenate(parts, axis=1), order_ref[...], 1, 1).astype(BF16)


def ffn_kernel(
    tokens_ref, mixed_ref, theirs_ref, gain_ref, grad_inner_ref, order_a_ref,
    gate_up_own_ref, gate_up_other_ref,
    hidden_ref, turned_ref, inner_ref, grad_ref, second_ref,
):
    half = MODEL_WIDTH // 2
    hidden = tokens_ref[...].astype(F32) + (mixed_ref[...].astype(F32) + theirs_ref[...].astype(F32))
    hidden_ref[...] = hidden
    scale = lax.rsqrt(jnp.mean(hidden * hidden, axis=1, keepdims=True) + EPS)
    normed = (hidden * scale * gain_ref[...]).astype(BF16)
    turned = dot_low(normed, order_a_ref[...]).astype(BF16)
    turned_ref[...] = turned
    ff = gate_up_own_ref.shape[1] // 2
    gate = dot_low(turned[:, :half], gate_up_own_ref[:, :ff]) + dot_low(
        turned[:, half:], gate_up_other_ref[:, :ff]
    )
    up = dot_low(turned[:, :half], gate_up_own_ref[:, ff:]) + dot_low(
        turned[:, half:], gate_up_other_ref[:, ff:]
    )
    grad_inner = grad_inner_ref[...]
    opened = sigmoid(gate)
    silu = gate * opened
    inner_ref[...] = (silu * up).astype(BF16)
    grad_gate = (grad_inner * up * (opened * (1.0 + gate * (1.0 - opened)))).astype(BF16)
    grads = jnp.concatenate([grad_gate, (grad_inner * silu).astype(BF16)], axis=1)
    grad_ref[...] = grads
    parts = [dot_low(grads, ref[...], 1, 1).astype(BF16) for ref in (gate_up_own_ref, gate_up_other_ref)]
    second_ref[...] = dot_low(jnp.concatenate(parts, axis=1), order_a_ref[...], 1, 1).astype(BF16)


def down_back_kernel(cot_ref, own_ref, other_ref, out_ref):
    ff = own_ref.shape[1] // 2
    half = MODEL_WIDTH // 2
    out_ref[...] = dot_low(cot_ref[:, :half], own_ref[:, ff:]) + dot_low(
        cot_ref[:, half:], other_ref[:, ff:]
    )


def ffn_out_kernel(inner_ref, own_ref, other_ref, order_ref, out_ref):
    ff = inner_ref.shape[1]
    inner = inner_ref[...]
    parts = [dot_low(inner, ref[:, ff:], 1, 1).astype(BF16) for ref in (own_ref, other_ref)]
    out_ref[...] = dot_low(jnp.concatenate(parts, axis=1), order_ref[...], 1, 1).astype(BF16)


def norm_back(values, gain, grad):
    scale = lax.rsqrt(jnp.mean(values * values, axis=1, keepdims=True) + EPS)
    weighted = grad * gain
    along = jnp.mean(weighted * values, axis=1, keepdims=True)
    return (scale, weighted * scale - values * (scale * scale * scale * along))


def mixer_back_kernel(
    hidden_ref, second_ref, theirs_ref, gain_ref, cot_ref, order_ref, own_ref, other_ref,
    gate_ref, y_ref, conv_ref, log_ref,
    grad_hidden_ref, turned_ref, grad_gain_ref, grad_attended_ref, grad_y_ref, grad_gate_ref,
    state_ref,
):
    half = MODEL_WIDTH // 2
    hidden = hidden_ref[...]
    mine = second_ref[...].astype(F32)
    scale, back = norm_back(hidden, gain_ref[...], mine + theirs_ref[...].astype(F32))
    grad_gain_ref[...] = jnp.sum(mine * hidden * scale, axis=0, keepdims=True)
    grad_hidden = cot_ref[...].astype(F32) + back
    grad_hidden_ref[...] = grad_hidden
    turned = dot_low(grad_hidden.astype(BF16), order_ref[...]).astype(BF16)
    turned_ref[...] = turned
    wide = WIDTH + QUERY_WIDTH
    grads = dot_low(turned[:, :half], own_ref[:, :wide]) + dot_low(turned[:, half:], other_ref[:, :wide])
    grad_attended_ref[...] = grads[:, WIDTH:].astype(BF16)
    grad_gated = grads[:, :WIDTH]
    gate = gate_ref[...]
    opened = sigmoid(gate)
    grad_y = grad_gated * gate * opened
    grad_y_ref[...] = grad_y
    grad_gate_ref[...] = (grad_gated * y_ref[...] * (opened * (1.0 + gate * (1.0 - opened)))).astype(BF16)
    weighted = grad_y * dot_f32(jnp.exp(log_ref[...]), head_spread())
    local = dot_f32(weighted.T, conv_ref[:, WIDTH + NS :])
    state_ref[...] = jnp.zeros_like(state_ref)
    for head in range(HEADS):
        state_ref[:, head, :] = local[head * P_SIZE : (head + 1) * P_SIZE]


def ffn_grads_kernel(
    normed_ref, grad_ff_ref, cot_ref, inner_ref, a_keep_ref, a_send_ref, b_keep_ref, b_send_ref
):
    half = MODEL_WIDTH // 2
    for part, (a_ref, b_ref) in enumerate(((a_keep_ref, b_keep_ref), (a_send_ref, b_send_ref))):
        lanes = slice(part * half, (part + 1) * half)
        a_ref[...] = dot_low(normed_ref[:, lanes], grad_ff_ref[...], 0, 0).astype(BF16)
        b_ref[...] = dot_low(cot_ref[:, lanes], inner_ref[...], 0, 0).astype(BF16)


def mixer_grads_kernel(
    normed_ref, grad_gate_ref, grad_mixed_ref, gated_ref, attended_ref,
    a_keep_ref, a_send_ref, b_keep_ref, b_send_ref,
):
    half = MODEL_WIDTH // 2
    for part, (a_ref, b_ref) in enumerate(((a_keep_ref, b_keep_ref), (a_send_ref, b_send_ref))):
        lanes = slice(part * half, (part + 1) * half)
        a_ref[...] = dot_low(normed_ref[HALO:, lanes], grad_gate_ref[...], 0, 0).astype(BF16)
        mixed = grad_mixed_ref[:, lanes]
        b_ref[:, :WIDTH] = dot_low(mixed, gated_ref[...], 0, 0).astype(BF16)
        b_ref[:, WIDTH:] = dot_low(mixed, attended_ref[...], 0, 0).astype(BF16)


def ssm_back_kernel(
    grad_y_ref, conv_ref, step_ref, log_ref, dt_ref, state_ref, grad_state_ref, ext_ref,
    conv_weight_ref, conv_bias_ref, decay_ref, skip_ref,
    grad_ext_ref, grad_dt_ref, small_ref, row_ref, pad_ref, grad_conv_ref,
):
    conved = conv_ref[...]
    grad_y = grad_y_ref[...]
    in_vectors = conved[:, WIDTH : WIDTH + NS]
    out_vectors = conved[:, WIDTH + NS :]
    step = step_ref[...]
    step_rows = step.T
    log_decay = log_ref[...]
    log_rows = log_decay.T
    last = log_decay[TOK - 1 :]
    spread = head_spread()
    states = stacked_states(state_ref)
    grad_states = stacked_states(grad_state_ref)
    now = jnp.exp(log_decay)
    leave = jnp.exp(last - log_decay)
    to_end = leave * step
    both = dot_f32(out_vectors, in_vectors, 1, 1)
    carried = dot_f32(out_vectors, states, 1, 1)
    pushed = dot_f32(in_vectors, grad_states, 1, 1)
    now_wide = dot_f32(now, spread)
    to_end_wide = dot_f32(to_end, spread)
    skip_wide = dot_f32(jnp.broadcast_to(skip_ref[...], (8, NS)), spread)[:1]
    inputs = conved[:, :WIDTH]
    grad_out = dot_f32(grad_y * now_wide, states)
    grad_in = dot_f32(inputs * to_end_wide, grad_states)
    outer = grad_y * skip_wide + to_end_wide * pushed
    grad_log = dot_f32(grad_y * carried * now_wide, spread, 1, 1)
    grad_to_end = dot_f32(inputs * pushed, spread, 1, 1)
    skip_sum = dot_f32(grad_y * inputs, spread, 1, 1)
    grad_step = grad_to_end * leave
    into_end = grad_to_end * to_end
    grad_log = grad_log - into_end
    stays = jnp.sum((states * grad_states).reshape(HEADS, P_SIZE, NS), axis=1)
    stays = jnp.concatenate([stays, jnp.zeros((NS - HEADS, NS), F32)], axis=0)
    stays = jnp.sum(stays.T, axis=0, keepdims=True)
    grad_last = jnp.sum(into_end, axis=0, keepdims=True) + jnp.exp(last) * stays
    grad_both = jnp.zeros((TOK, TOK), F32)
    row_ref[...] = jnp.zeros_like(row_ref)
    for pair in range(HEADS // 2):
        lanes = slice(pair * 2 * P_SIZE, (pair + 1) * 2 * P_SIZE)
        pair_inputs = conved[:, lanes]
        pair_grads = grad_y[:, lanes]
        first = first_of_pair(pair_inputs.shape)
        parts = []
        for side, head in enumerate((2 * pair, 2 * pair + 1)):
            decay = head_decay(log_decay, log_rows, head)
            step_row = step_rows[head : head + 1]
            mine = jnp.where(first if side == 0 else jnp.logical_not(first), pair_grads, 0.0)
            grad_mixing = dot_f32(mine, pair_inputs, 1, 1) * decay
            grad_both = grad_both + grad_mixing * step_row
            apart = grad_mixing * both
            row_ref[head : head + 1, :] = jnp.sum(apart, axis=0, keepdims=True)
            along = jnp.sum(apart * step_row, axis=1, keepdims=True)
            grad_log = grad_log + jnp.where(lanes_of((TOK, NS)) == head, along, 0.0)
            mixing = both * decay * step_row
            parts.append(dot_f32(mixing.T, pair_grads))
        grad_conv_ref[:, lanes] = outer[:, lanes] + jnp.where(first, parts[0], parts[1])
    rows = row_ref[...].T
    grad_step = grad_step + rows
    grad_log = grad_log - rows * step
    grad_log = grad_log + jnp.where(rows_of((TOK, NS)) == TOK - 1, grad_last, 0.0)
    grad_rate = dot_f32((rows_of((TOK, TOK)) <= lanes_of((TOK, TOK))).astype(F32), grad_log)
    grad_step = grad_step - grad_rate * decay_ref[...]
    grad_dt = grad_step * sigmoid(dt_ref[...])
    grad_dt_ref[...] = jnp.where(lanes_of((TOK, NS)) < HEADS, grad_dt, 0.0).astype(BF16)
    grad_conv_ref[:, WIDTH : WIDTH + NS] = grad_in + dot_f32(grad_both.T, out_vectors)
    grad_conv_ref[:, WIDTH + NS :] = grad_out + dot_f32(grad_both, in_vectors)
    summed = convolved(ext_ref, conv_weight_ref[...], conv_bias_ref[...])
    opened = sigmoid(summed)
    grad_summed = grad_conv_ref[...] * (opened * (1.0 + summed * (1.0 - opened)))
    pad_ref[...] = jnp.zeros_like(pad_ref)
    pad_ref[pl.ds(HALO, TOK), :] = grad_summed
    conv_weight = conv_weight_ref[...]
    total = 0.0
    for lag in range(CONV_K):
        total = total + conv_weight[lag : lag + 1] * pad_ref[pl.ds(CONV_K - 1 - lag, HALO + TOK), :]
        small_ref[lag : lag + 1, :] = jnp.sum(
            grad_summed * ext_ref[pl.ds(HALO - CONV_K + 1 + lag, TOK), :], axis=0, keepdims=True
        )
    grad_ext_ref[...] = total.astype(BF16)
    small_ref[CONV_K : CONV_K + 1, :] = jnp.sum(grad_summed, axis=0, keepdims=True)
    small_ref[CONV_K + 1 : CONV_K + 3, :] = jnp.zeros((2, MODEL_WIDTH), F32)
    heads_row = jnp.concatenate(
        [
            jnp.sum(grad_dt, axis=0, keepdims=True),
            -jnp.sum(grad_rate * step, axis=0, keepdims=True),
            jnp.sum(skip_sum, axis=0, keepdims=True),
            jnp.zeros((1, MODEL_WIDTH - 3 * NS), F32),
        ],
        axis=1,
    )
    small_ref[CONV_K + 3 : CONV_K + 4, :] = heads_row


def project_a_kernel(
    low_ref, grad_gate_ref, a_own_ref, a_other_ref, b_own_ref, b_other_ref, order_a_ref, order_b_ref, out_ref
):
    parts = [dot_low(low_ref[...], ref[...], 1, 1).astype(BF16) for ref in (a_own_ref, a_other_ref)]
    from_a = dot_low(jnp.concatenate(parts, axis=1), order_a_ref[...], 1, 1)
    gate = grad_gate_ref[...]
    parts = [dot_low(gate, ref[:, :WIDTH], 1, 1).astype(BF16) for ref in (b_own_ref, b_other_ref)]
    out_ref[...] = from_a + dot_low(jnp.concatenate(parts, axis=1), order_b_ref[...], 1, 1)


def project_b_kernel(
    low_ref, from_ref, own_ref, other_ref, order_ref, tokens_ref, first_ref, grad_gain_ref
):
    parts = [dot_low(low_ref[...], ref[:, WIDTH:], 1, 1).astype(BF16) for ref in (own_ref, other_ref)]
    first = from_ref[...] + dot_low(jnp.concatenate(parts, axis=1), order_ref[...], 1, 1)
    first = first.astype(BF16)
    first_ref[...] = first
    tokens = tokens_ref[...].astype(F32)
    scale = lax.rsqrt(jnp.mean(tokens * tokens, axis=1, keepdims=True) + EPS)
    grad_gain_ref[...] = jnp.sum(first.astype(F32) * tokens * scale, axis=0, keepdims=True)


def join_kernel(counts, *refs):
    pieces = list(refs[: sum(counts)])
    for count, out_ref in zip(counts, refs[sum(counts) :]):
        at = 0
        for ref in pieces[:count]:
            out_ref[at : at + ref.shape[0], :] = ref[...]
            at += ref.shape[0]
        pieces = pieces[count:]


def join_rings(*groups, vmem=12, far=False):
    outs = [((sum(piece.shape[0] for piece in group), group[0].shape[1]), BF16) for group in groups]
    pieces = [piece for group in groups for piece in group]
    if far:
        pieces = [pltpu.with_memory_space_constraint(piece, pltpu.HBM) for piece in pieces]
    counts = tuple(len(group) for group in groups)
    return kernel_call(functools.partial(join_kernel, counts), outs, *pieces, vmem=vmem, name="join_rings")


def pass_on_kernel(*refs):
    for ahead, behind, from_behind, from_ahead, ahead_out, behind_out in zip(*[iter(refs)] * 6):
        half = from_ahead.shape[0]
        ahead_out[:half, :] = (ahead[:half, :].astype(F32) + from_behind[...].astype(F32)).astype(BF16)
        ahead_out[half:, :] = ahead[half:, :]
        behind_out[:half, :] = behind[:half, :]
        behind_out[half:, :] = (behind[half:, :].astype(F32) + from_ahead[...].astype(F32)).astype(BF16)


def halve_kernel(*refs):
    groups = (len(refs) - 5) // 2
    rows = refs[0].shape[0] // 4
    outs = refs[2 * groups :]
    starts = ((0, rows), (rows, rows), (3 * rows, rows), (2 * rows, rows // 2), (2 * rows + rows // 2, rows // 2))
    at = 0
    for group in range(groups):
        keep_ref, arrived_ref = refs[2 * group : 2 * group + 2]
        lanes = slice(at, at + keep_ref.shape[1])
        at += keep_ref.shape[1]
        for (start, size), out_ref in zip(starts, outs):
            part = slice(start, start + size)
            total = keep_ref[part, :].astype(F32) + arrived_ref[part, :].astype(F32)
            out_ref[:, lanes] = total.astype(out_ref.dtype)


def halve(*parts, vmem=16):
    rows = parts[0].shape[0] // 4
    width = sum(part.shape[1] for part in parts[::2])
    sizes = ((rows, F32), (rows, BF16), (rows, BF16), (rows // 2, BF16), (rows // 2, BF16))
    return kernel_call(
        halve_kernel, [((size, width), dtype) for size, dtype in sizes], *parts, vmem=vmem, us=2,
        name="halve",
    )


def pass_on(*groups, vmem=16):
    def body(*refs):
        count = 4 * len(groups)
        ins, outs = (refs[:count], refs[count:])
        mixed = []
        for group in range(len(groups)):
            mixed += ins[4 * group : 4 * group + 4] + outs[2 * group : 2 * group + 2]
        pass_on_kernel(*mixed)

    outs = [(piece.shape, BF16) for group in groups for piece in group[:2]]
    pieces = [piece for group in groups for piece in group]
    return kernel_call(body, outs, *pieces, vmem=vmem, name="pass_on")


def two_halves(values):
    high = values.astype(BF16)
    return (high, (values - high.astype(F32)).astype(BF16))


def of_halves(high, low):
    return high.astype(F32) + low.astype(F32)


def late_b_kernel(normed_ref, low_ref, small_ref, keep_ref, send_ref, sent_ref):
    half = MODEL_WIDTH // 2
    low = low_ref[...]
    keep_ref[...] = dot_low(normed_ref[:, :half], low, 0, 0).astype(BF16)
    send_ref[:half, :] = dot_low(normed_ref[:, half:], low, 0, 0).astype(BF16)
    small = small_ref[...]
    high, rest = two_halves(jnp.concatenate([small[:, :half], small[:, half:]], axis=0))
    send_ref[half:, :] = jnp.concatenate([high, rest], axis=0)
    sent_ref[...] = of_halves(high, rest)


def late_b_ring_kernel(keep_ref, arrived_ref, small_ref, first_ref, *rest_refs):
    rows = TOK
    total = keep_ref[...].astype(F32) + arrived_ref[: 4 * rows, :].astype(F32)
    lines = small_ref.shape[0]
    small = small_ref[...] + of_halves(
        arrived_ref[4 * rows : 4 * rows + lines, :], arrived_ref[4 * rows + lines :, :]
    )
    high, rest = two_halves(small)
    first_ref[...] = total[:rows]
    tail = jnp.concatenate([high, rest], axis=0)
    for step in (1, 2, 3):
        rest_refs[step - 1][:rows, :] = total[step * rows : (step + 1) * rows].astype(BF16)
        rest_refs[step - 1][rows:, :] = tail
    rest_refs[3][...] = of_halves(high, rest)


def ring_total(refs, rows):
    return refs[0][...] + sum(ref[:rows, :].astype(F32) for ref in refs[1:])


def merge_a_kernel(*refs):
    early, late, (keep_ref, *send_refs) = (refs[:3], refs[3:6], refs[6:])
    total = jnp.concatenate([ring_total(early, TOK), ring_total(late, TOK)], axis=1)
    rows = TOK // 4
    keep_ref[...] = total[:rows]
    for step in (1, 2, 3):
        send_refs[step - 1][...] = total[step * rows : (step + 1) * rows].astype(BF16)


def ring_small(small_ref, pieces):
    first, second, third = pieces
    return (small_ref[...] + second) + (first + third)


def merge_b_kernel(*refs):
    early, late, small_ref = (refs[:3], refs[3:7], refs[7])
    keep_ref, *send_refs, sent_ref = refs[8:]
    total = jnp.concatenate([ring_total(early, TOK), ring_total(late, TOK)], axis=1)
    lines = small_ref.shape[0]
    small = ring_small(
        small_ref, [of_halves(ref[TOK : TOK + lines, :], ref[TOK + lines :, :]) for ref in late[1:]]
    )
    high, rest = two_halves(small)
    tail = jnp.concatenate([high, rest], axis=0)
    rows = TOK // 4
    keep_ref[...] = total[:rows]
    width = total.shape[1]
    for step in (1, 2, 3):
        send_refs[step - 1][:, :width] = total[step * rows : (step + 1) * rows].astype(BF16)
        send_refs[step - 1][:, width:] = tail
    sent_ref[...] = of_halves(high, rest)


def last_ring_kernel(*refs):
    a_refs, b_refs, small_ref = (refs[:4], refs[4:8], refs[8])
    keep_ref, away_ref, sent_ref = refs[9:]
    rows = TOK // 4
    width = b_refs[0].shape[1]
    lines = small_ref.shape[0]
    total_b = b_refs[0][...] + (
        b_refs[1][:, :width].astype(F32) + b_refs[2][:, :width].astype(F32) + b_refs[3][:, :width].astype(F32)
    )
    total = jnp.concatenate([ring_total(a_refs, rows), total_b], axis=1)
    small = ring_small(
        small_ref, [of_halves(ref[:lines, width:], ref[lines:, width:]) for ref in b_refs[1:]]
    )
    high, rest = two_halves(small)
    keep_ref[...] = total[: rows // 2]
    away_ref[:, : total.shape[1]] = total[rows // 2 :].astype(BF16)
    away_ref[:, total.shape[1] :] = jnp.concatenate([high, rest], axis=1)
    sent_ref[...] = of_halves(high, rest)


def in_grads_kernel(normed_ref, low_ref, keep_ref, send_ref):
    half = MODEL_WIDTH // 2
    low = low_ref[...]
    keep_ref[...] = dot_low(normed_ref[:, :half], low, 0, 0).astype(BF16)
    send_ref[...] = dot_low(normed_ref[:, half:], low, 0, 0).astype(BF16)


def finish_grads_kernel(keep_ref, theirs_ref, small_ref, *refs):
    *out_refs, sum_ref = refs
    at = 0
    for ref in out_refs:
        lanes = slice(at, at + ref.shape[1])
        ref[...] = keep_ref[:, lanes] + theirs_ref[:, lanes].astype(F32)
        at += ref.shape[1]
    at = keep_ref.shape[1]
    width = small_ref.shape[1]
    sum_ref[...] = small_ref[...] + of_halves(theirs_ref[:, at : at + width], theirs_ref[:, at + width :])


def low_b_kernel(query_ref, kv_ref, dt_ref, cosine_ref, sine_ref, out_ref):
    grads = jnp.concatenate([query_ref[...], kv_ref[...]], axis=1)
    out_ref[:, :ROPED] = turn(grads, cosine_ref[...], -sine_ref[...]).astype(BF16)
    out_ref[:, ROPED:] = dt_ref[...]


def slot_of(pair, index):
    y, x, z = (index >> 5, (index >> 3) & 3, (index >> 1) & 3)
    dy = ((pair >> 4) - y) & 1
    dx = ((pair >> 2) - x) & 3
    dz = (pair - z) & 3
    return pl.multiple_of(((dx * 4 + dz) * 2 + dy) * TOK, TOK)


def load_quad(quad, index, own_ref, other_ref):
    parts = []
    for side in (0, 1):
        slot = slot_of(quad * 2 + side, index)
        parts += [own_ref[pl.ds(slot, TOK), :], other_ref[pl.ds(slot, TOK), :]]
    return jnp.concatenate(parts, axis=0)


def head_columns(rows):
    turned = rows.T
    heads = rows.shape[1] // HEAD_SIZE
    return jnp.concatenate(
        [turned[head * HEAD_SIZE : (head + 1) * HEAD_SIZE] for head in range(heads)], axis=1
    )


def head_rows(rows):
    heads = rows.shape[1] // HEAD_SIZE
    return jnp.concatenate(
        [rows[:, head * HEAD_SIZE : (head + 1) * HEAD_SIZE] for head in range(heads)], axis=0
    )


def rows_of_columns(columns):
    heads = columns.shape[1] // TOK
    stacked = jnp.concatenate(
        [columns[:, head * TOK : (head + 1) * TOK] for head in range(heads)], axis=0
    )
    return stacked.T


def quad_mask(shape, quad, index):
    row = rows_of(shape)
    block = quad * 4 + (row >> 8) * 2 + ((index & 1) ^ ((row >> 7) & 1))
    keys = block * TOK + (row & (TOK - 1))
    queries = index * TOK + (lanes_of(shape) & (TOK - 1))
    return keys <= queries


def attend_kernel(index_ref, query_ref, own_ref, other_ref, columns_ref, rows_ref, log_ref, total_ref):
    index = index_ref[0]
    query = head_columns(query_ref[...].astype(F32) * HEAD_SIZE ** (-0.5))
    padded = jnp.concatenate([query, jnp.zeros_like(query)], axis=0).astype(BF16)
    total_ref[...] = jnp.zeros_like(total_ref)

    def step(quad, carry, masked):
        peak, weight = carry
        quad_kv = load_quad(quad, index, own_ref, other_ref)
        scores = jnp.dot(quad_kv, padded, preferred_element_type=F32)
        if masked:
            scores = jnp.where(quad_mask(scores.shape, quad, index), scores, MASKED)
        new_peak = jnp.maximum(peak, jnp.max(scores, axis=0, keepdims=True))
        shrink = jnp.exp(peak - new_peak)
        probs = jnp.exp(scores - new_peak)
        weight = weight * shrink + jnp.sum(probs, axis=0, keepdims=True)
        total_ref[...] = total_ref[...] * shrink + dot_low(quad_kv, probs.astype(BF16), 0, 0)
        return (new_peak, weight)

    lanes = (1, query.shape[1])
    last = index >> 2
    carry = step(last, (jnp.full(lanes, MASKED, F32), jnp.zeros(lanes, F32)), True)
    peak, weight = lax.fori_loop(0, last, lambda quad, carry: step(quad, carry, False), carry)
    columns = total_ref[HEAD_SIZE:, :] / weight
    columns_ref[...] = columns
    rows_ref[...] = rows_of_columns(columns).astype(BF16)
    log_ref[...] = peak + jnp.log(weight)


def attend(index, query_low, own_kv, other_kv):
    lanes = QUERY_WIDTH // HEAD_SIZE * TOK
    vmem = pl.BlockSpec(memory_space=pltpu.VMEM)
    return pl.pallas_call(
        attend_kernel,
        out_shape=(
            jax.ShapeDtypeStruct((HEAD_SIZE, lanes), F32),
            jax.ShapeDtypeStruct((TOK, QUERY_WIDTH), BF16),
            jax.ShapeDtypeStruct((1, lanes), F32),
        ),
        in_specs=[pl.BlockSpec(memory_space=pltpu.SMEM), vmem, vmem, vmem],
        out_specs=(vmem, vmem, vmem),
        scratch_shapes=[pltpu.VMEM((2 * HEAD_SIZE, lanes), F32)],
        compiler_params=pltpu.CompilerParams(vmem_limit_bytes=24 * 2**20),
        cost_estimate=pl.CostEstimate(flops=13 * 10**9, bytes_accessed=0, transcendentals=0),
        name="attend",
    )(index, query_low, own_kv, other_kv)


def attend_back_kernel(
    index_ref, query_ref, grad_ref, columns_ref, log_ref, own_ref, other_ref,
    grad_query_ref, grad_own_ref, grad_other_ref, total_ref,
):
    index = index_ref[0]
    scale = HEAD_SIZE ** (-0.5)
    query_rows = query_ref[...].astype(F32) * scale
    grad_rows = grad_ref[...].astype(F32)
    query = head_columns(query_rows)
    grad = head_columns(grad_rows)
    blank = jnp.zeros_like(query)
    query_pad = jnp.concatenate([query, blank], axis=0).astype(BF16)
    grad_pad = jnp.concatenate([blank, grad], axis=0).astype(BF16)
    query_tall = head_rows(query_rows)
    grad_tall = head_rows(grad_rows)
    blank = jnp.zeros_like(query_tall)
    sides = jnp.concatenate(
        [
            jnp.concatenate([query_tall, blank], axis=1),
            jnp.concatenate([blank, grad_tall], axis=1),
        ],
        axis=0,
    ).astype(BF16)
    delta = jnp.sum(grad * columns_ref[...], axis=0, keepdims=True)
    log_total = log_ref[...]
    total_ref[...] = jnp.zeros_like(total_ref)
    grad_own_ref[...] = jnp.zeros_like(grad_own_ref)
    grad_other_ref[...] = jnp.zeros_like(grad_other_ref)

    def step(quad, masked):
        quad_kv = load_quad(quad, index, own_ref, other_ref)
        scores = jnp.dot(quad_kv, query_pad, preferred_element_type=F32)
        grad_probs = jnp.dot(quad_kv, grad_pad, preferred_element_type=F32)
        probs = jnp.exp(scores - log_total)
        if masked:
            probs = jnp.where(quad_mask(scores.shape, quad, index), probs, 0.0)
        grad_scores = (probs * (grad_probs - delta)).astype(BF16)
        total_ref[...] += dot_low(quad_kv, grad_scores, 0, 0)
        both = jnp.concatenate([grad_scores, probs.astype(BF16)], axis=1)
        term = jnp.dot(both, sides, preferred_element_type=F32).astype(BF16)
        for side in (0, 1):
            slot = slot_of(quad * 2 + side, index)
            at = side * 2 * TOK
            grad_own_ref[pl.ds(slot, TOK), :] = term[at : at + TOK]
            grad_other_ref[pl.ds(slot, TOK), :] = term[at + TOK : at + 2 * TOK]

    last = index >> 2
    step(last, True)

    def loop(quad, carry):
        step(quad, False)
        return carry

    lax.fori_loop(0, last, loop, 0)
    grad_query_ref[...] = rows_of_columns(total_ref[:HEAD_SIZE, :] * scale)


def attend_back(index, query_low, grad_low, columns, log_total, own_kv, other_kv):
    vmem = pl.BlockSpec(memory_space=pltpu.VMEM)
    return pl.pallas_call(
        attend_back_kernel,
        out_shape=(
            jax.ShapeDtypeStruct(query_low.shape, F32),
            jax.ShapeDtypeStruct(own_kv.shape, BF16),
            jax.ShapeDtypeStruct(other_kv.shape, BF16),
        ),
        in_specs=[pl.BlockSpec(memory_space=pltpu.SMEM)] + [vmem] * 6,
        out_specs=(vmem, vmem, vmem),
        scratch_shapes=[pltpu.VMEM((2 * HEAD_SIZE, columns.shape[1]), F32)],
        compiler_params=pltpu.CompilerParams(vmem_limit_bytes=24 * 2**20),
        cost_estimate=pl.CostEstimate(flops=19 * 10**9, bytes_accessed=0, transcendentals=0),
        name="attend_back",
    )(index, query_low, grad_low, columns, log_total, own_kv, other_kv)


def shards(
    tokens,
    cotangent,
    gain_first,
    z_weight,
    x_weight,
    bc_weight,
    dt_weight,
    conv_x_weight,
    conv_x_bias,
    conv_bc_weight,
    conv_bc_bias,
    dt_bias,
    decay_rate,
    skip_weight,
    out_weight,
    q_weight,
    key_matrix,
    value_matrix,
    o_weight,
    gain_second,
    gate_weight,
    up_weight,
    down_weight,
):
    index = lax.axis_index(SEQ)
    index_word = jnp.reshape(index, (1,)).astype(jnp.int32)
    ff = gate_weight.shape[1]
    in_a_width = WIDTH + 2 * NS
    in_b_width = WIDTH + ROPED + NS

    def padded_heads(values):
        return jnp.pad(values, (0, NS - HEADS))[None, :]

    together = lax.optimization_barrier
    together = lax.optimization_barrier
    with jax.named_scope("gather_near"):
        dt_wide = jnp.pad(dt_weight, ((0, 0), (0, NS - HEADS)))
        near_a = jnp.concatenate([x_weight, bc_weight, gate_weight, up_weight], axis=1)
        near_b = jnp.concatenate(
            [z_weight, q_weight, key_matrix, value_matrix, dt_wide, out_weight, o_weight, down_weight],
            axis=1,
        )
        split = near_a.shape[1]
        theirs = send(jnp.concatenate([near_a, near_b], axis=1), OTHER_Y)
        near_a = fetch(joined([near_a, theirs[:, :split]]), along_x)
        near_b = fetch(joined([near_b, theirs[:, split:]]), along_z)
        near_a, near_b = join_rings(near_a, near_b, vmem=8)
    with jax.named_scope("orders"):
        halo = send(tokens[TOK - (CONV_K - 1) :], ONWARD)
        ahead = jnp.zeros((HALO - (CONV_K - 1), MODEL_WIDTH), BF16)
        tokens_ext = jnp.concatenate([ahead, halo, tokens], axis=0)
        to_a, to_b = one_hot_orders(index)
        normed = rms_norm(tokens_ext.astype(F32), gain_first).astype(BF16)
        normed_a = project(normed, to_a).astype(BF16)
        normed_b = project(normed[HALO:], to_b).astype(BF16)
        cot_b = project(cotangent, to_b).astype(BF16)
        cosine, sine = rotary_tables(index)
        conv_weight = jnp.concatenate([conv_x_weight, conv_bc_weight], axis=1)
        conv_bias = jnp.concatenate([conv_x_bias, conv_bc_bias], axis=0)[None, :]
        decay_wide = padded_heads(decay_rate)
        skip_wide = padded_heads(skip_weight)
        dt_bias_wide = padded_heads(dt_bias)
    with jax.named_scope("gather_in"):
        in_a, rest_a = (near_a[:, :in_a_width], near_a[:, in_a_width:])
        in_b, rest_b = (near_b[:, :in_b_width], near_b[:, in_b_width:])
        (in_a, in_b), (normed_a, normed_b, to_a, to_b) = together(
            ((ring_near(in_a, along_z), ring_near(in_b, along_x)), (normed_a, normed_b, to_a, to_b))
        )
        in_a, in_b = (ring_far(in_a, along_z), ring_far(in_b, along_x))
        (in_a, in_b), (cot_b, cosine, sine) = together(((in_a, in_b), (cot_b, cosine, sine)))
        in_a_own, in_b_own = join_rings(in_a, in_b)
        in_b_other = send(in_b_own, OTHER_CORE)
        in_a_other = send(in_a_own, OTHER_CORE)
        in_a_other, in_b_other = together((in_a_other, in_b_other))
    with jax.named_scope("attention_in"):
        gate_raw, query_low, kv_low, dt_pre, step_size, log_decay = kernel_call(
            attention_in_kernel,
            [((TOK, WIDTH), F32), ((TOK, QUERY_WIDTH), BF16), ((TOK, 2 * HEAD_SIZE), BF16)]
            + [((TOK, NS), F32)] * 3,
            normed_b, in_b_own, in_b_other, cosine, sine, dt_bias_wide, decay_wide,
            name="attention_in",
        )
    with jax.named_scope("gather_kv"):
        kv_low, rest_a, rest_b = together((kv_low, rest_a, rest_b))
        own_kv = joined([kv_low, send(kv_low, OTHER_Y)])
    with jax.named_scope("gather_rest"):
        rest_a, rest_b = (ring_near(rest_a, along_z), ring_near(rest_b, along_x))
    with jax.named_scope("ssm_in"):
        ext, conved, payload = kernel_call(
            ssm_in_kernel,
            [((HALO + TOK, MODEL_WIDTH), F32), ((TOK, MODEL_WIDTH), F32), ((P_SIZE, SLOTS, NS), F32)],
            normed_a, in_a_own, in_a_other, conv_weight, conv_bias, step_size, log_decay,
            us=3, name="ssm_in",
        )
    with jax.named_scope("state_forward"):
        payload, rest_a, rest_b, own_kv = together((payload, rest_a, rest_b, own_kv))
        spans = swap_spans(payload)
        own_kv = fetch(own_kv, along_z)
        spans, own_kv, rest_a, rest_b = together((spans, own_kv, rest_a, rest_b))
        entering = states_between(spans, spans, False)
        own_kv = fetch(join_rings(own_kv, vmem=4, far=True)[0], along_x)
        rest_a = ring_far(rest_a, along_z)
        entering, own_kv, rest_a, rest_b = together((entering, own_kv, rest_a, rest_b))
        own_kv = join_rings(own_kv, vmem=4)[0]
        other_kv = send(own_kv, OTHER_CORE)
        rest_b = ring_far(rest_b, along_x)
        state_in = swap_spans(entering)
        state_in, own_kv, other_kv, rest_a, rest_b = together((state_in, own_kv, other_kv, rest_a, rest_b))
    with jax.named_scope("gather_rest"):
        rest_a_own, rest_b_own = join_rings(rest_a, rest_b, far=True)
        rest_b_other = send(rest_b_own, OTHER_CORE)
        rest_a_other = send(rest_a_own, OTHER_CORE)
    with jax.named_scope("attention"):
        attended_columns, attended_low, log_total = attend(index_word, query_low, own_kv, other_kv)
    with jax.named_scope("ssm_out"):
        gated_low, y = kernel_call(
            ssm_out_kernel, [((TOK, WIDTH), BF16), ((TOK, WIDTH), F32)],
            conved, step_size, log_decay, state_in, gate_raw, skip_wide,
            us=2, name="ssm_out",
        )
        gated_low, attended_low, rest_a_other, rest_b_other = together(
            (gated_low, attended_low, rest_a_other, rest_b_other)
        )
    with jax.named_scope("mixer_out"):
        mixed = kernel_call(
            mixer_out_kernel, [((TOK, MODEL_WIDTH), BF16)],
            gated_low, attended_low, rest_b_own, rest_b_other, to_b,
            us=2, name="mixer_out",
        )[0]
        mixed_theirs = swap_heads(mixed)
    with jax.named_scope("ffn"):
        grad_inner = kernel_call(
            down_back_kernel, [((TOK, ff), F32)], cot_b, rest_b_own, rest_b_other,
            vmem=12, us=2, name="down_back",
        )[0]
        mixed_theirs, grad_inner = together((mixed_theirs, grad_inner))
        hidden, normed_second, inner_low, grad_ff, second_part = kernel_call(
            ffn_kernel,
            [((TOK, MODEL_WIDTH), F32), ((TOK, MODEL_WIDTH), BF16), ((TOK, ff), BF16),
             ((TOK, 2 * ff), BF16), ((TOK, MODEL_WIDTH), BF16)],
            tokens, mixed, mixed_theirs, gain_second[None, :], grad_inner, to_a,
            rest_a_own, rest_a_other,
            vmem=20, us=5, name="ffn",
        )
        second_theirs = swap_heads(second_part)
        ffn_part = kernel_call(
            ffn_out_kernel, [((TOK, MODEL_WIDTH), BF16)], inner_low, rest_b_own, rest_b_other, to_b,
            vmem=16, us=2, name="ffn_out",
        )[0]
        half = (MODEL_WIDTH // 2,)
        a_keep, a_send, b_keep, b_send = kernel_call(
            ffn_grads_kernel, [(half + (2 * ff,), BF16)] * 2 + [(half + (ff,), BF16)] * 2,
            normed_second, grad_ff, cot_b, inner_low, vmem=16, us=2, name="ffn_grads",
        )
        ffn_keep = (a_keep, b_keep)
        ffn_arrived = (send(a_send, OTHER_CORE), send(b_send, OTHER_CORE))
        second_theirs, ffn_part = together((second_theirs, ffn_part))
    with jax.named_scope("mixer_back"):
        (
            grad_hidden, grad_mixed_b, gain_second_part, grad_attended, grad_y, grad_gate_low, payload_back
        ) = kernel_call(
            mixer_back_kernel,
            [((TOK, MODEL_WIDTH), F32), ((TOK, MODEL_WIDTH), BF16), ((1, MODEL_WIDTH), F32),
             ((TOK, QUERY_WIDTH), BF16), ((TOK, WIDTH), F32), ((TOK, WIDTH), BF16),
             ((P_SIZE, SLOTS, NS), F32)],
            hidden, second_part, second_theirs, gain_second[None, :], cotangent, to_b,
            rest_b_own, rest_b_other, gate_raw, y, conved, log_decay,
            vmem=20, us=3, name="mixer_back",
        )
        ffn_theirs = swap_heads(ffn_part)
    with jax.named_scope("early_grads"):
        early_a, early_b = (2 * ff + WIDTH, ff + WIDTH + QUERY_WIDTH)
        a_keep, a_send, b_keep, b_send = kernel_call(
            mixer_grads_kernel,
            [(half + (WIDTH,), BF16)] * 2 + [(half + (WIDTH + QUERY_WIDTH,), BF16)] * 2,
            normed_a, grad_gate_low, grad_mixed_b, gated_low, attended_low, vmem=12, name="mixer_grads",
        )
    with jax.named_scope("state_backward"):
        arrived_back = swap_spans(payload_back)
        arrived_back, a_send, b_send, ffn_arrived = together((arrived_back, a_send, b_send, ffn_arrived))
        leaving = states_between(spans, arrived_back, True)
        a_arrived = send(a_send, OTHER_CORE)
        b_arrived = send(b_send, OTHER_CORE)
        state_grad = swap_spans(leaving)
        state_grad, a_arrived, b_arrived = together((state_grad, a_arrived, b_arrived))
    with jax.named_scope("early_grads"):
        a_keep, a_ahead, a_behind, a_first, a_second = halve(
            ffn_keep[0], ffn_arrived[0], a_keep, a_arrived
        )
        b_keep, b_ahead, b_behind, b_first, b_second = halve(
            ffn_keep[1], ffn_arrived[1], b_keep, b_arrived
        )
        a_passed = [send(a_first, along_z(1)), send(a_second, along_z(-1))]
        b_passed = [send(b_first, along_x(1)), send(b_second, along_x(-1))]
    with jax.named_scope("ssm_back"):
        low_a, grad_dt_low, small = kernel_call(
            ssm_back_kernel,
            [((HALO + TOK, MODEL_WIDTH), BF16), ((TOK, NS), BF16), ((2 * CONV_K, MODEL_WIDTH), F32)],
            grad_y, conved, step_size, log_decay, dt_pre, state_in, state_grad, ext,
            conv_weight, conv_bias, decay_wide, skip_wide,
            scratch=[
                pltpu.VMEM((NS, TOK), F32),
                pltpu.VMEM((2 * HALO + TOK, MODEL_WIDTH), F32),
                pltpu.VMEM((TOK, MODEL_WIDTH), F32),
            ],
            vmem=16, us=8, name="ssm_back",
        )
        low_a, grad_dt_low, small, a_passed, b_passed, ffn_theirs = together(
            (low_a, grad_dt_low, small, a_passed, b_passed, ffn_theirs)
        )
    with jax.named_scope("late_grads"):
        late_keep, late_send = kernel_call(
            in_grads_kernel, [(half + (in_a_width,), BF16)] * 2, normed_a, low_a,
            vmem=12, name="late_grads_a",
        )
        late_arrived = send(late_send, OTHER_CORE)
    with jax.named_scope("early_grads"):
        a_ahead, a_behind, b_ahead, b_behind = pass_on(
            [a_ahead, a_behind] + a_passed, [b_ahead, b_behind] + b_passed
        )
        a_ready = [a_keep, send(a_ahead, along_z(1)), send(a_behind, along_z(-1))]
        b_ready = [b_keep, send(b_ahead, along_x(1)), send(b_behind, along_x(-1))]
    with jax.named_scope("attention_back"):
        grad_query, grad_own_kv, grad_other_kv = attend_back(
            index_word, query_low, grad_attended, attended_columns, log_total, own_kv, other_kv
        )
        (grad_query, grad_own_kv, grad_other_kv), a_ready, b_ready, late_arrived = together(
            ((grad_query, grad_own_kv, grad_other_kv), a_ready, b_ready, late_arrived)
        )
    with jax.named_scope("late_grads"):
        late_keep, late_ahead, late_behind, late_first, late_second = halve(
            late_keep, late_arrived, vmem=8
        )
        late_passed = [send(late_first, along_z(1)), send(late_second, along_z(-1))]
    with jax.named_scope("scatter_kv"):
        kv_arrived = send(grad_other_kv, OTHER_CORE)
        kv_arrived, late_passed = together((kv_arrived, late_passed))
        grad_kv = blocks_of([grad_own_kv, kv_arrived], 4)
        kv_arrived = spread(grad_kv, along_x)
    with jax.named_scope("late_grads"):
        late_ahead, late_behind = pass_on([late_ahead, late_behind] + late_passed, vmem=8)
        a_late = [late_keep, send(late_ahead, along_z(1)), send(late_behind, along_z(-1))]
        kv_arrived, a_late = together((kv_arrived, a_late))
    with jax.named_scope("last_grads"):
        rows = TOK // 4
        wide_a = early_a + in_a_width
        a_last = kernel_call(
            merge_a_kernel, [((rows, wide_a), F32)] + [((rows, wide_a), BF16)] * 3,
            *a_ready, *a_late, vmem=12, name="merge_a",
        )
    with jax.named_scope("project_in_back"):
        returned = send(low_a[HALO - (CONV_K - 1) : HALO], BACKWARD)
        low_own = low_a[HALO:].astype(F32) + jnp.pad(
            returned.astype(F32), ((TOK - (CONV_K - 1), 0), (0, 0))
        )
        from_a = kernel_call(
            project_a_kernel, [((TOK, MODEL_WIDTH), F32)],
            low_own.astype(BF16), grad_gate_low, in_a_own, in_a_other, in_b_own, in_b_other, to_a, to_b,
            vmem=20, us=2, name="project_a",
        )[0]
    with jax.named_scope("scatter_kv"):
        grad_kv = ring_sum(grad_kv, kv_arrived)
        grad_kv = blocks_of([grad_kv], 4)
        kv_arrived = spread(grad_kv, along_z)
        kv_arrived, from_a, a_last = together((kv_arrived, from_a, a_last))
        grad_kv = ring_sum(grad_kv, kv_arrived)
        kv_theirs = send(grad_kv[TOK:].astype(BF16), OTHER_Y)
        a_last = [a_last[0]] + spread(a_last, along_x)
        grad_kv = grad_kv[:TOK] + kv_theirs.astype(F32)
    with jax.named_scope("project_in_back"):
        late_b = ROPED + NS
        low_b = kernel_call(
            low_b_kernel, [((TOK, late_b), BF16)],
            grad_query, grad_kv, grad_dt_low, cosine, sine, vmem=8, name="low_b",
        )[0]
        first_part, gain_first_part = kernel_call(
            project_b_kernel, [((TOK, MODEL_WIDTH), BF16), ((1, MODEL_WIDTH), F32)],
            low_b, from_a, in_b_own, in_b_other, to_b, tokens, vmem=12, us=1, name="project_b",
        )
    with jax.named_scope("late_grads"):
        small = jnp.concatenate(
            [small[: CONV_K + 1], gain_first_part, gain_second_part, small[CONV_K + 3 :]], axis=0
        )
        lines, line = (SLOTS, MODEL_WIDTH // 2)
        b_keep, b_send, small = kernel_call(
            late_b_kernel,
            [(half + (late_b,), BF16), ((line + 2 * lines, late_b), BF16), ((lines, line), F32)],
            normed_b, low_b, small, vmem=12, name="late_grads_b",
        )
        *b_late, small = kernel_call(
            late_b_ring_kernel,
            [((TOK, late_b), F32)] + [((TOK + 2 * lines, late_b), BF16)] * 3 + [((lines, line), F32)],
            b_keep, send(b_send, OTHER_CORE), small, vmem=8, name="late_ring_b",
        )
        b_late = [b_late[0]] + spread(b_late, along_x)
    with jax.named_scope("last_grads"):
        wide_b = early_b + late_b
        *b_last, small = kernel_call(
            merge_b_kernel,
            [((rows, wide_b), F32)] + [((rows, wide_b + line), BF16)] * 3 + [((lines, line), F32)],
            *b_ready, *b_late, small, vmem=12, name="merge_b",
        )
        b_last = [b_last[0]] + spread(b_last, along_z)
        rows = rows // 2
        own, away, small = kernel_call(
            last_ring_kernel,
            [((rows, wide_a + wide_b), F32), ((rows, wide_a + wide_b + 2 * line), BF16), ((lines, line), F32)],
            *a_last, *b_last, small, vmem=8, name="last_ring",
        )
    with jax.named_scope("finish_grads"):
        widths = (ff, ff, WIDTH, WIDTH, 2 * NS, ff, WIDTH, QUERY_WIDTH, QUERY_WIDTH, HEAD_SIZE, HEAD_SIZE, NS)
        (
            grad_gate, grad_up, grad_z, grad_x, own_bc, grad_down, grad_out, grad_o, grad_q, grad_k,
            grad_v, grad_dt, small
        ) = kernel_call(
            finish_grads_kernel,
            [((rows, width), F32) for width in widths] + [((lines, line), F32)],
            own, send(away, OTHER_Y), small, vmem=8, name="finish_grads",
        )
        grad_dt = grad_dt[:, :HEADS]
        theirs = swap_heads(jnp.concatenate([own_bc, small], axis=1))
        grad_bc = own_bc + theirs[:, : 2 * NS]
        total = small + theirs[:, 2 * NS :]
        small = jnp.concatenate([small[: 2 * CONV_K], small[2 * CONV_K :]], axis=1)
        total = jnp.concatenate([total[: 2 * CONV_K], total[2 * CONV_K :]], axis=1)
    with jax.named_scope("finish"):
        grad_first = first_part.astype(F32) + swap_heads(first_part).astype(F32)
        grad_tokens = grad_hidden + norm_back(tokens.astype(F32), gain_first[None, :], grad_first)[1]
        output = (hidden + (ffn_part.astype(F32) + ffn_theirs.astype(F32))).astype(BF16)
    with jax.named_scope("small_grads"):
        summed_gain_first = total[CONV_K + 1]
        summed_gain_second = total[CONV_K + 2]
        grad_conv_x = small[:CONV_K, :WIDTH]
        grad_conv_xb = small[CONV_K, :WIDTH]
        summed_conv_bc = total[:CONV_K, WIDTH:]
        summed_conv_bcb = total[CONV_K, WIDTH:]
        grad_dt_bias_own = small[CONV_K + 3, :HEADS]
        grad_decay_own = small[CONV_K + 3, NS : NS + HEADS]
        grad_skip_own = small[CONV_K + 3, 2 * NS : 2 * NS + HEADS]
    return (
        output,
        grad_tokens,
        summed_gain_first,
        grad_z,
        grad_x,
        grad_bc,
        grad_dt,
        grad_conv_x,
        grad_conv_xb,
        summed_conv_bc,
        summed_conv_bcb,
        grad_dt_bias_own,
        grad_decay_own,
        grad_skip_own,
        grad_out,
        grad_q,
        grad_k,
        grad_v,
        grad_o,
        summed_gain_second,
        grad_gate,
        grad_up,
        grad_down,
    )


def solution(mesh):
    return jax.shard_map(
        shards,
        mesh=mesh,
        in_specs=(
            P("seq", None),
            P("seq", None),
            P(),
            P("seq", "head"),
            P("seq", "head"),
            P("seq", None),
            P("seq", "head"),
            P(None, "head"),
            P("head"),
            P(),
            P(),
            P("head"),
            P("head"),
            P("head"),
            P("seq", "head"),
            P("seq", "head"),
            P("seq", "head"),
            P("seq", "head"),
            P("seq", "head"),
            P(),
            P("seq", "head"),
            P("seq", "head"),
            P("seq", "head"),
        ),
        out_specs=(
            P("seq", None),
            P("seq", None),
            P(),
            P("seq", "head"),
            P("seq", "head"),
            P("seq", None),
            P("seq", "head"),
            P(None, "head"),
            P("head"),
            P(),
            P(),
            P("head"),
            P("head"),
            P("head"),
            P("seq", "head"),
            P("seq", "head"),
            P("seq", "head"),
            P("seq", "head"),
            P("seq", "head"),
            P(),
            P("seq", "head"),
            P("seq", "head"),
            P("seq", "head"),
        ),
        check_vma=False,
    )
```

```python
import functools

import jax
import jax.numpy as jnp
from jax import lax
from jax.experimental import pallas as pl
from jax.experimental.pallas import tpu as pltpu
from jax.sharding import PartitionSpec as P

MODEL_WIDTH = 1024
NH = 24
P_SIZE = 64
NS = 128
HEAD_SIZE = 64
CONV_K = 4
TOK = 128
SPANS = 64
HEADS = 12
WIDTH = HEADS * P_SIZE
QUERY_WIDTH = 256
ROPED = QUERY_WIDTH + 2 * HEAD_SIZE
SLOTS = 16
SHARED = 4
HALO = 16
KEY_ROWS = SPANS // 2 * TOK

EPS = 1e-06
ROPE_BASE = 100000000000.0
MASKED = -1e30
HIGHEST = lax.Precision.HIGHEST
BF16 = jnp.bfloat16
F32 = jnp.float32
SEQ = "seq"


def place(index):
    return (index // 32, (index // 8) % 4, (index // 2) % 4, index % 2)


def index_of(y, x, z, core):
    return ((y * 4 + x) * 4 + z) * 2 + core


def pairs(move):
    return [(source, index_of(*move(*place(source)))) for source in range(SPANS)]


OTHER_CORE = pairs(lambda y, x, z, c: (y, x, z, 1 - c))
OTHER_Y = pairs(lambda y, x, z, c: (1 - y, x, z, c))
OTHER_HEAD = [(0, 1), (1, 0)]
OTHER_Y_AND_HEAD = [
    (source * 2 + head, target * 2 + 1 - head) for source, target in OTHER_Y for head in range(2)
]
ONWARD = [(span, span + 1) for span in range(SPANS - 1)]
BACKWARD = [(span + 1, span) for span in range(SPANS - 1)]


def along_x(steps):
    return pairs(lambda y, x, z, c: (y, (x + steps) % 4, z, c))


def along_z(steps):
    return pairs(lambda y, x, z, c: (y, x, (z + steps) % 4, c))


def send(value, route):
    return lax.ppermute(value, SEQ, route)


def swap_heads(value):
    return lax.ppermute(value, "head", OTHER_HEAD)


def swap_spans(value):
    return lax.all_to_all(value, SEQ, 0, 0, tiled=True)


def after(value, *others):
    return lax.optimization_barrier((value, others))[0]


def joined(pieces):
    return jnp.concatenate(pieces, axis=0)


def fetch(value, along):
    return [value] + [send(value, along(-step)) for step in (1, 2, 3)]


def ring_near(value, along):
    return (value, send(value, along(-1)), send(value, along(1)))


def ring_far(near, along):
    own, ahead, behind = near
    half = own.shape[0] // 2
    first = send(ahead[:half], along(-1))
    second = send(behind[half:], along(1))
    return [own, ahead, first, second, behind]


def blocks_of(parts, count):
    rows = parts[0].shape[0] // count
    return [
        sum(part[block * rows : (block + 1) * rows].astype(F32) for part in parts)
        for block in range(count)
    ]


def spread(blocks, along):
    return [send(block.astype(BF16), along(step)) for step, block in enumerate(blocks) if step]


def ring_sum(blocks, arrived):
    return blocks[0] + sum(block.astype(F32) for block in arrived)


def scatter_ring(parts, along):
    blocks = blocks_of(parts, 4)
    return ring_sum(blocks, spread(blocks, along))


def one_hot_orders(index):
    y, x, z, c = place(index)
    row = jnp.arange(MODEL_WIDTH, dtype=jnp.int32)
    inner = row % 16
    dy, low, high, dc = ((row // 16) % 2, (row // 32) % 4, (row // 128) % 4, row // 512)

    def one_hot(dx, dz):
        device = index_of((y + dy) % 2, (x + dx) % 4, (z + dz) % 4, (c + dc) % 2)
        return (row[:, None] == (device * 16 + inner)[None, :]).astype(BF16)

    return (one_hot(low, high), one_hot(high, low))


def project(left_side, right_side):
    return jnp.dot(left_side, right_side, preferred_element_type=F32)


def rms_norm(values, norm_gain):
    return values * lax.rsqrt(jnp.mean(values * values, axis=-1, keepdims=True) + EPS) * norm_gain


def rotary_tables(index):
    half = HEAD_SIZE // 2
    frequency = ROPE_BASE ** (-jnp.arange(half, dtype=F32) * (1.0 / half))
    positions = (index * TOK + jnp.arange(TOK, dtype=jnp.int32)).astype(F32)
    angles = positions[:, None] * frequency[None, :]
    cosine, sine = (jnp.cos(angles), jnp.sin(angles))
    turns = QUERY_WIDTH // HEAD_SIZE + 1
    plain = jnp.ones((TOK, HEAD_SIZE), F32)
    return (
        jnp.concatenate([cosine, cosine] * turns + [plain], axis=1),
        jnp.concatenate([-sine, sine] * turns + [0.0 * plain], axis=1),
    )


def dot_f32(left_side, right_side, left_dim=1, right_dim=0):
    return lax.dot_general(
        left_side, right_side, (((left_dim,), (right_dim,)), ((), ())), precision=HIGHEST,
        preferred_element_type=F32,
    )


def dot_low(left_side, right_side, left_dim=1, right_dim=0):
    return lax.dot_general(
        left_side, right_side, (((left_dim,), (right_dim,)), ((), ())), preferred_element_type=F32
    )


def lanes_of(shape):
    return lax.broadcasted_iota(jnp.int32, shape, len(shape) - 1)


def rows_of(shape):
    return lax.broadcasted_iota(jnp.int32, shape, len(shape) - 2)


def head_spread():
    shape = (NS, HEADS * P_SIZE)
    return (lanes_of(shape) // P_SIZE == rows_of(shape)).astype(F32)


def causal_mask():
    return rows_of((TOK, TOK)) >= lanes_of((TOK, TOK))


def sigmoid(values):
    return 1.0 / (1.0 + jnp.exp(-values))


def softplus(values):
    small = jnp.exp(-jnp.abs(values))
    series = small * (1.0 - small * (0.5 - small * (1.0 / 3.0 - small * 0.25)))
    return jnp.maximum(values, 0.0) + jnp.where(small < 0.01, series, jnp.log(1.0 + small))


def turn(values, cosine, sine):
    width = values.shape[1]
    half = HEAD_SIZE // 2
    ahead = pltpu.roll(values, width - half, 1)
    behind = pltpu.roll(values, half, 1)
    other = jnp.where(lanes_of(values.shape) % HEAD_SIZE < half, ahead, behind)
    return values * cosine + other * sine


FAR = "far"


def far_away(value):
    return pltpu.with_memory_space_constraint(value, pltpu.HBM)


def kernel_call(body, outs, *operands, far=(), scratch=(), vmem=16, us=1, name=None):
    vspec = pl.BlockSpec(memory_space=pltpu.VMEM)
    operands = [far_away(value) if at in far else value for at, value in enumerate(operands)]
    return pl.pallas_call(
        body,
        out_shape=tuple(
            pltpu.HBM(*out[:2]) if FAR in out else jax.ShapeDtypeStruct(*out) for out in outs
        ),
        in_specs=[vspec] * len(operands),
        out_specs=(vspec,) * len(outs),
        scratch_shapes=list(scratch),
        compiler_params=pltpu.CompilerParams(vmem_limit_bytes=vmem * 2**20),
        cost_estimate=pl.CostEstimate(flops=us * 10**9, bytes_accessed=0, transcendentals=0),
        name=name,
    )(*operands)


def attention_in_kernel(
    normed_ref, own_ref, other_ref, cosine_ref, sine_ref, dt_bias_ref, decay_ref,
    gate_ref, query_ref, kv_ref, dt_ref, step_ref, log_ref,
):
    normed = normed_ref[...]
    half = MODEL_WIDTH // 2
    raw = dot_low(normed[:, :half], own_ref[...]) + dot_low(normed[:, half:], other_ref[...])
    gate_ref[...] = raw[:, :WIDTH]
    turned = turn(raw[:, WIDTH : WIDTH + ROPED], cosine_ref[...], sine_ref[...]).astype(BF16)
    query_ref[...] = turned[:, :QUERY_WIDTH]
    kv_ref[...] = turned[:, QUERY_WIDTH:]
    dt = raw[:, WIDTH + ROPED :] + dt_bias_ref[...]
    step = softplus(dt)
    dt_ref[...] = dt
    step_ref[...] = step
    log_ref[...] = dot_f32(causal_mask().astype(F32), -step * decay_ref[...])


def convolved(ext_ref, conv_weight, conv_bias):
    summed = conv_bias
    for lag in range(CONV_K):
        summed = summed + conv_weight[lag : lag + 1] * ext_ref[pl.ds(HALO - CONV_K + 1 + lag, TOK), :]
    return summed


def ssm_in_kernel(
    normed_ref, own_ref, other_ref, conv_weight_ref, conv_bias_ref, step_ref, log_ref,
    ext_ref, conv_ref, state_ref,
):
    normed = normed_ref[...]
    half = MODEL_WIDTH // 2
    ext_ref[...] = dot_low(normed[:, :half], own_ref[...]) + dot_low(normed[:, half:], other_ref[...])
    summed = convolved(ext_ref, conv_weight_ref[...], conv_bias_ref[...])
    conved = summed * sigmoid(summed)
    conv_ref[...] = conved
    log_decay = log_ref[...]
    last = log_decay[TOK - 1 :]
    to_end = jnp.exp(last - log_decay) * step_ref[...]
    weighted = conved[:, :WIDTH] * dot_f32(to_end, head_spread())
    local = dot_f32(weighted.T, conved[:, WIDTH : WIDTH + NS])
    state_ref[...] = jnp.zeros_like(state_ref)
    for head in range(HEADS):
        state_ref[:, head, :] = local[head * P_SIZE : (head + 1) * P_SIZE]
    state_ref[:, HEADS, :] = jnp.broadcast_to(jnp.exp(last), (P_SIZE, NS))


def states_kernel(reverse, decay_ref, local_ref, out_ref):
    decays = decay_ref[:, HEADS, :].T[:SLOTS]
    state = jnp.zeros((SLOTS, NS), F32)
    for position in range(SPANS):
        span = SPANS - 1 - position if reverse else position
        out_ref[span] = state
        if position < SPANS - 1:
            state = decays[:, span : span + 1] * state + local_ref[span]


def states_between(decays, local, reverse):
    return kernel_call(
        functools.partial(states_kernel, reverse), [((SPANS, SLOTS, NS), F32)], decays, local,
        vmem=16, name="states",
    )[0]


def head_decay(log_decay, log_rows, head):
    apart = jnp.minimum(log_decay[:, head : head + 1] - log_rows[head : head + 1], 0.0)
    return jnp.where(causal_mask(), jnp.exp(apart), 0.0)


def stacked_states(state_ref):
    return jnp.concatenate([state_ref[:, head, :] for head in range(HEADS)], axis=0)


def first_of_pair(shape):
    return lanes_of(shape) < P_SIZE


def ssm_out_kernel(
    conv_ref, step_ref, log_ref, state_ref, gate_ref, skip_ref, gated_ref, y_ref
):
    conved = conv_ref[...]
    in_vectors = conved[:, WIDTH : WIDTH + NS]
    out_vectors = conved[:, WIDTH + NS :]
    log_decay = log_ref[...]
    log_rows = log_decay.T
    step_rows = step_ref[...].T
    spread = head_spread()
    both = dot_f32(out_vectors, in_vectors, 1, 1)
    carried = dot_f32(out_vectors, stacked_states(state_ref), 1, 1)
    skip = dot_f32(jnp.broadcast_to(skip_ref[...], (8, NS)), spread)[:1]
    outer = dot_f32(jnp.exp(log_decay), spread) * carried + skip * conved[:, :WIDTH]
    for pair in range(HEADS // 2):
        lanes = slice(pair * 2 * P_SIZE, (pair + 1) * 2 * P_SIZE)
        inputs = conved[:, lanes]
        parts = []
        for head in (2 * pair, 2 * pair + 1):
            mixing = both * head_decay(log_decay, log_rows, head) * step_rows[head : head + 1]
            parts.append(dot_f32(mixing, inputs))
        y = outer[:, lanes] + jnp.where(first_of_pair(inputs.shape), parts[0], parts[1])
        gate = gate_ref[:, lanes]
        y_ref[:, lanes] = y
        gated_ref[:, lanes] = (y * gate * sigmoid(gate)).astype(BF16)


def mixer_out_kernel(gated_ref, attended_ref, own_ref, other_ref, order_ref, out_ref):
    mixed = jnp.concatenate([gated_ref[...], attended_ref[...]], axis=1)
    wide = mixed.shape[1]
    parts = [dot_low(mixed, ref[:, :wide], 1, 1).astype(BF16) for ref in (own_ref, other_ref)]
    out_ref[...] = dot_low(jnp.concatenate(parts, axis=1), order_ref[...], 1, 1).astype(BF16)


def ffn_kernel(
    tokens_ref, mixed_ref, theirs_ref, gain_ref, grad_inner_ref, order_a_ref,
    gate_up_own_ref, gate_up_other_ref,
    hidden_ref, turned_ref, inner_ref, grad_ref, second_ref,
):
    half = MODEL_WIDTH // 2
    hidden = tokens_ref[...].astype(F32) + (mixed_ref[...].astype(F32) + theirs_ref[...].astype(F32))
    hidden_ref[...] = hidden
    scale = lax.rsqrt(jnp.mean(hidden * hidden, axis=1, keepdims=True) + EPS)
    normed = (hidden * scale * gain_ref[...]).astype(BF16)
    turned = dot_low(normed, order_a_ref[...]).astype(BF16)
    turned_ref[...] = turned
    ff = gate_up_own_ref.shape[1] // 2
    gate = dot_low(turned[:, :half], gate_up_own_ref[:, :ff]) + dot_low(
        turned[:, half:], gate_up_other_ref[:, :ff]
    )
    up = dot_low(turned[:, :half], gate_up_own_ref[:, ff:]) + dot_low(
        turned[:, half:], gate_up_other_ref[:, ff:]
    )
    grad_inner = grad_inner_ref[...]
    opened = sigmoid(gate)
    silu = gate * opened
    inner_ref[...] = (silu * up).astype(BF16)
    grad_gate = (grad_inner * up * (opened * (1.0 + gate * (1.0 - opened)))).astype(BF16)
    grads = jnp.concatenate([grad_gate, (grad_inner * silu).astype(BF16)], axis=1)
    grad_ref[...] = grads
    parts = [dot_low(grads, ref[...], 1, 1).astype(BF16) for ref in (gate_up_own_ref, gate_up_other_ref)]
    second_ref[...] = dot_low(jnp.concatenate(parts, axis=1), order_a_ref[...], 1, 1).astype(BF16)


def down_back_kernel(cot_ref, own_ref, other_ref, out_ref):
    ff = own_ref.shape[1] // 2
    half = MODEL_WIDTH // 2
    out_ref[...] = dot_low(cot_ref[:, :half], own_ref[:, ff:]) + dot_low(
        cot_ref[:, half:], other_ref[:, ff:]
    )


def ffn_out_kernel(inner_ref, own_ref, other_ref, order_ref, out_ref):
    ff = inner_ref.shape[1]
    inner = inner_ref[...]
    parts = [dot_low(inner, ref[:, ff:], 1, 1).astype(BF16) for ref in (own_ref, other_ref)]
    out_ref[...] = dot_low(jnp.concatenate(parts, axis=1), order_ref[...], 1, 1).astype(BF16)


def norm_back(values, gain, grad):
    scale = lax.rsqrt(jnp.mean(values * values, axis=1, keepdims=True) + EPS)
    weighted = grad * gain
    along = jnp.mean(weighted * values, axis=1, keepdims=True)
    return (scale, weighted * scale - values * (scale * scale * scale * along))


def mixer_back_kernel(
    hidden_ref, second_ref, theirs_ref, gain_ref, cot_ref, order_ref, own_ref, other_ref,
    gate_ref, y_ref, conv_ref, log_ref,
    grad_hidden_ref, turned_ref, grad_gain_ref, grad_attended_ref, grad_y_ref, grad_gate_ref,
    state_ref,
):
    half = MODEL_WIDTH // 2
    hidden = hidden_ref[...]
    mine = second_ref[...].astype(F32)
    scale, back = norm_back(hidden, gain_ref[...], mine + theirs_ref[...].astype(F32))
    grad_gain_ref[...] = jnp.sum(mine * hidden * scale, axis=0, keepdims=True)
    grad_hidden = cot_ref[...].astype(F32) + back
    grad_hidden_ref[...] = grad_hidden
    turned = dot_low(grad_hidden.astype(BF16), order_ref[...]).astype(BF16)
    turned_ref[...] = turned
    wide = WIDTH + QUERY_WIDTH
    grads = dot_low(turned[:, :half], own_ref[:, :wide]) + dot_low(turned[:, half:], other_ref[:, :wide])
    grad_attended_ref[...] = grads[:, WIDTH:].astype(BF16)
    grad_gated = grads[:, :WIDTH]
    gate = gate_ref[...]
    opened = sigmoid(gate)
    grad_y = grad_gated * gate * opened
    grad_y_ref[...] = grad_y
    grad_gate_ref[...] = (grad_gated * y_ref[...] * (opened * (1.0 + gate * (1.0 - opened)))).astype(BF16)
    weighted = grad_y * dot_f32(jnp.exp(log_ref[...]), head_spread())
    local = dot_f32(weighted.T, conv_ref[:, WIDTH + NS :])
    state_ref[...] = jnp.zeros_like(state_ref)
    for head in range(HEADS):
        state_ref[:, head, :] = local[head * P_SIZE : (head + 1) * P_SIZE]


def ffn_grads_kernel(
    normed_ref, grad_ff_ref, cot_ref, inner_ref, a_keep_ref, a_send_ref, b_keep_ref, b_send_ref
):
    half = MODEL_WIDTH // 2
    for part, (a_ref, b_ref) in enumerate(((a_keep_ref, b_keep_ref), (a_send_ref, b_send_ref))):
        lanes = slice(part * half, (part + 1) * half)
        a_ref[...] = dot_low(normed_ref[:, lanes], grad_ff_ref[...], 0, 0).astype(BF16)
        b_ref[...] = dot_low(cot_ref[:, lanes], inner_ref[...], 0, 0).astype(BF16)


def mixer_grads_kernel(
    normed_ref, grad_gate_ref, grad_mixed_ref, gated_ref, attended_ref,
    a_keep_ref, a_send_ref, b_keep_ref, b_send_ref,
):
    half = MODEL_WIDTH // 2
    for part, (a_ref, b_ref) in enumerate(((a_keep_ref, b_keep_ref), (a_send_ref, b_send_ref))):
        lanes = slice(part * half, (part + 1) * half)
        a_ref[...] = dot_low(normed_ref[HALO:, lanes], grad_gate_ref[...], 0, 0).astype(BF16)
        mixed = grad_mixed_ref[:, lanes]
        b_ref[:, :WIDTH] = dot_low(mixed, gated_ref[...], 0, 0).astype(BF16)
        b_ref[:, WIDTH:] = dot_low(mixed, attended_ref[...], 0, 0).astype(BF16)


def ssm_back_kernel(
    grad_y_ref, conv_ref, step_ref, log_ref, dt_ref, state_ref, grad_state_ref, ext_ref,
    conv_weight_ref, conv_bias_ref, decay_ref, skip_ref,
    grad_ext_ref, grad_dt_ref, small_ref, row_ref, pad_ref, grad_conv_ref,
):
    conved = conv_ref[...]
    grad_y = grad_y_ref[...]
    in_vectors = conved[:, WIDTH : WIDTH + NS]
    out_vectors = conved[:, WIDTH + NS :]
    step = step_ref[...]
    step_rows = step.T
    log_decay = log_ref[...]
    log_rows = log_decay.T
    last = log_decay[TOK - 1 :]
    spread = head_spread()
    states = stacked_states(state_ref)
    grad_states = stacked_states(grad_state_ref)
    now = jnp.exp(log_decay)
    leave = jnp.exp(last - log_decay)
    to_end = leave * step
    both = dot_f32(out_vectors, in_vectors, 1, 1)
    carried = dot_f32(out_vectors, states, 1, 1)
    pushed = dot_f32(in_vectors, grad_states, 1, 1)
    now_wide = dot_f32(now, spread)
    to_end_wide = dot_f32(to_end, spread)
    skip_wide = dot_f32(jnp.broadcast_to(skip_ref[...], (8, NS)), spread)[:1]
    inputs = conved[:, :WIDTH]
    grad_out = dot_f32(grad_y * now_wide, states)
    grad_in = dot_f32(inputs * to_end_wide, grad_states)
    outer = grad_y * skip_wide + to_end_wide * pushed
    grad_log = dot_f32(grad_y * carried * now_wide, spread, 1, 1)
    grad_to_end = dot_f32(inputs * pushed, spread, 1, 1)
    skip_sum = dot_f32(grad_y * inputs, spread, 1, 1)
    grad_step = grad_to_end * leave
    into_end = grad_to_end * to_end
    grad_log = grad_log - into_end
    stays = jnp.sum((states * grad_states).reshape(HEADS, P_SIZE, NS), axis=1)
    stays = jnp.concatenate([stays, jnp.zeros((NS - HEADS, NS), F32)], axis=0)
    stays = jnp.sum(stays.T, axis=0, keepdims=True)
    grad_last = jnp.sum(into_end, axis=0, keepdims=True) + jnp.exp(last) * stays
    grad_both = jnp.zeros((TOK, TOK), F32)
    row_ref[...] = jnp.zeros_like(row_ref)
    for pair in range(HEADS // 2):
        lanes = slice(pair * 2 * P_SIZE, (pair + 1) * 2 * P_SIZE)
        pair_inputs = conved[:, lanes]
        pair_grads = grad_y[:, lanes]
        first = first_of_pair(pair_inputs.shape)
        parts = []
        for side, head in enumerate((2 * pair, 2 * pair + 1)):
            decay = head_decay(log_decay, log_rows, head)
            step_row = step_rows[head : head + 1]
            mine = jnp.where(first if side == 0 else jnp.logical_not(first), pair_grads, 0.0)
            grad_mixing = dot_f32(mine, pair_inputs, 1, 1) * decay
            grad_both = grad_both + grad_mixing * step_row
            apart = grad_mixing * both
            row_ref[head : head + 1, :] = jnp.sum(apart, axis=0, keepdims=True)
            along = jnp.sum(apart * step_row, axis=1, keepdims=True)
            grad_log = grad_log + jnp.where(lanes_of((TOK, NS)) == head, along, 0.0)
            mixing = both * decay * step_row
            parts.append(dot_f32(mixing.T, pair_grads))
        grad_conv_ref[:, lanes] = outer[:, lanes] + jnp.where(first, parts[0], parts[1])
    rows = row_ref[...].T
    grad_step = grad_step + rows
    grad_log = grad_log - rows * step
    grad_log = grad_log + jnp.where(rows_of((TOK, NS)) == TOK - 1, grad_last, 0.0)
    grad_rate = dot_f32((rows_of((TOK, TOK)) <= lanes_of((TOK, TOK))).astype(F32), grad_log)
    grad_step = grad_step - grad_rate * decay_ref[...]
    grad_dt = grad_step * sigmoid(dt_ref[...])
    grad_dt_ref[...] = jnp.where(lanes_of((TOK, NS)) < HEADS, grad_dt, 0.0).astype(BF16)
    grad_conv_ref[:, WIDTH : WIDTH + NS] = grad_in + dot_f32(grad_both.T, out_vectors)
    grad_conv_ref[:, WIDTH + NS :] = grad_out + dot_f32(grad_both, in_vectors)
    summed = convolved(ext_ref, conv_weight_ref[...], conv_bias_ref[...])
    opened = sigmoid(summed)
    grad_summed = grad_conv_ref[...] * (opened * (1.0 + summed * (1.0 - opened)))
    pad_ref[...] = jnp.zeros_like(pad_ref)
    pad_ref[pl.ds(HALO, TOK), :] = grad_summed
    conv_weight = conv_weight_ref[...]
    total = 0.0
    for lag in range(CONV_K):
        total = total + conv_weight[lag : lag + 1] * pad_ref[pl.ds(CONV_K - 1 - lag, HALO + TOK), :]
        small_ref[lag : lag + 1, :] = jnp.sum(
            grad_summed * ext_ref[pl.ds(HALO - CONV_K + 1 + lag, TOK), :], axis=0, keepdims=True
        )
    grad_ext_ref[...] = total.astype(BF16)
    small_ref[CONV_K : CONV_K + 1, :] = jnp.sum(grad_summed, axis=0, keepdims=True)
    small_ref[CONV_K + 1 : CONV_K + 3, :] = jnp.zeros((2, MODEL_WIDTH), F32)
    heads_row = jnp.concatenate(
        [
            jnp.sum(grad_dt, axis=0, keepdims=True),
            -jnp.sum(grad_rate * step, axis=0, keepdims=True),
            jnp.sum(skip_sum, axis=0, keepdims=True),
            jnp.zeros((1, MODEL_WIDTH - 3 * NS), F32),
        ],
        axis=1,
    )
    small_ref[CONV_K + 3 : CONV_K + 4, :] = heads_row


def project_a_kernel(
    low_ref, grad_gate_ref, a_own_ref, a_other_ref, b_own_ref, b_other_ref, order_a_ref, order_b_ref, out_ref
):
    parts = [dot_low(low_ref[...], ref[...], 1, 1).astype(BF16) for ref in (a_own_ref, a_other_ref)]
    from_a = dot_low(jnp.concatenate(parts, axis=1), order_a_ref[...], 1, 1)
    gate = grad_gate_ref[...]
    parts = [dot_low(gate, ref[:, :WIDTH], 1, 1).astype(BF16) for ref in (b_own_ref, b_other_ref)]
    out_ref[...] = from_a + dot_low(jnp.concatenate(parts, axis=1), order_b_ref[...], 1, 1)


def project_b_kernel(
    low_ref, from_ref, own_ref, other_ref, order_ref, tokens_ref, first_ref, grad_gain_ref
):
    parts = [dot_low(low_ref[...], ref[:, WIDTH:], 1, 1).astype(BF16) for ref in (own_ref, other_ref)]
    first = from_ref[...] + dot_low(jnp.concatenate(parts, axis=1), order_ref[...], 1, 1)
    first = first.astype(BF16)
    first_ref[...] = first
    tokens = tokens_ref[...].astype(F32)
    scale = lax.rsqrt(jnp.mean(tokens * tokens, axis=1, keepdims=True) + EPS)
    grad_gain_ref[...] = jnp.sum(first.astype(F32) * tokens * scale, axis=0, keepdims=True)


def join_kernel(counts, *refs):
    pieces = list(refs[: sum(counts)])
    for count, out_ref in zip(counts, refs[sum(counts) :]):
        at = 0
        for ref in pieces[:count]:
            out_ref[at : at + ref.shape[0], :] = ref[...]
            at += ref.shape[0]
        pieces = pieces[count:]


def join_rings(*groups, vmem=12, far=False):
    outs = [((sum(piece.shape[0] for piece in group), group[0].shape[1]), BF16) for group in groups]
    pieces = [piece for group in groups for piece in group]
    if far:
        pieces = [far_away(piece) for piece in pieces]
    counts = tuple(len(group) for group in groups)
    return kernel_call(functools.partial(join_kernel, counts), outs, *pieces, vmem=vmem, name="join_rings")


def pass_on_kernel(*refs):
    for ahead, behind, from_behind, from_ahead, ahead_out, behind_out in zip(*[iter(refs)] * 6):
        half = from_ahead.shape[0]
        ahead_out[:half, :] = (ahead[:half, :].astype(F32) + from_behind[...].astype(F32)).astype(BF16)
        ahead_out[half:, :] = ahead[half:, :]
        behind_out[:half, :] = behind[:half, :]
        behind_out[half:, :] = (behind[half:, :].astype(F32) + from_ahead[...].astype(F32)).astype(BF16)


def halve_kernel(*refs):
    groups = (len(refs) - 5) // 2
    rows = refs[0].shape[0] // 4
    outs = refs[2 * groups :]
    starts = ((0, rows), (rows, rows), (3 * rows, rows), (2 * rows, rows // 2), (2 * rows + rows // 2, rows // 2))
    at = 0
    for group in range(groups):
        keep_ref, arrived_ref = refs[2 * group : 2 * group + 2]
        lanes = slice(at, at + keep_ref.shape[1])
        at += keep_ref.shape[1]
        for (start, size), out_ref in zip(starts, outs):
            part = slice(start, start + size)
            total = keep_ref[part, :].astype(F32) + arrived_ref[part, :].astype(F32)
            out_ref[:, lanes] = total.astype(out_ref.dtype)


def halve(*parts, vmem=16):
    rows = parts[0].shape[0] // 4
    width = sum(part.shape[1] for part in parts[::2])
    sizes = ((rows, F32), (rows, BF16), (rows, BF16), (rows // 2, BF16), (rows // 2, BF16))
    return kernel_call(
        halve_kernel, [((size, width), dtype) for size, dtype in sizes], *parts, vmem=vmem, us=2,
        name="halve",
    )


def pass_on(*groups, vmem=16):
    def body(*refs):
        count = 4 * len(groups)
        ins, outs = (refs[:count], refs[count:])
        mixed = []
        for group in range(len(groups)):
            mixed += ins[4 * group : 4 * group + 4] + outs[2 * group : 2 * group + 2]
        pass_on_kernel(*mixed)

    outs = [(piece.shape, BF16) for group in groups for piece in group[:2]]
    pieces = [piece for group in groups for piece in group]
    return kernel_call(body, outs, *pieces, vmem=vmem, name="pass_on")


def two_halves(values):
    high = values.astype(BF16)
    return (high, (values - high.astype(F32)).astype(BF16))


def of_halves(high, low):
    return high.astype(F32) + low.astype(F32)


def late_b_kernel(normed_ref, low_ref, small_ref, keep_ref, send_ref, sent_ref):
    half = MODEL_WIDTH // 2
    low = low_ref[...]
    keep_ref[...] = dot_low(normed_ref[:, :half], low, 0, 0).astype(BF16)
    send_ref[:half, :] = dot_low(normed_ref[:, half:], low, 0, 0).astype(BF16)
    small = small_ref[...]
    high, rest = two_halves(jnp.concatenate([small[:, :half], small[:, half:]], axis=0))
    send_ref[half:, :] = jnp.concatenate([high, rest], axis=0)
    sent_ref[...] = of_halves(high, rest)


def late_b_ring_kernel(keep_ref, arrived_ref, small_ref, first_ref, *rest_refs):
    rows = TOK
    total = keep_ref[...].astype(F32) + arrived_ref[: 4 * rows, :].astype(F32)
    lines = small_ref.shape[0]
    small = small_ref[...] + of_halves(
        arrived_ref[4 * rows : 4 * rows + lines, :], arrived_ref[4 * rows + lines :, :]
    )
    high, rest = two_halves(small)
    first_ref[...] = total[:rows]
    tail = jnp.concatenate([high, rest], axis=0)
    for step in (1, 2, 3):
        rest_refs[step - 1][:rows, :] = total[step * rows : (step + 1) * rows].astype(BF16)
        rest_refs[step - 1][rows:, :] = tail
    rest_refs[3][...] = of_halves(high, rest)


def ring_total(refs, rows):
    return refs[0][...] + sum(ref[:rows, :].astype(F32) for ref in refs[1:])


def merge_a_kernel(*refs):
    early, late, (keep_ref, *send_refs) = (refs[:3], refs[3:6], refs[6:])
    total = jnp.concatenate([ring_total(early, TOK), ring_total(late, TOK)], axis=1)
    rows = TOK // 4
    keep_ref[...] = total[:rows]
    for step in (1, 2, 3):
        send_refs[step - 1][...] = total[step * rows : (step + 1) * rows].astype(BF16)


def ring_small(small_ref, pieces):
    first, second, third = pieces
    return (small_ref[...] + second) + (first + third)


def merge_b_kernel(*refs):
    early, late, small_ref = (refs[:3], refs[3:7], refs[7])
    keep_ref, *send_refs, sent_ref = refs[8:]
    total = jnp.concatenate([ring_total(early, TOK), ring_total(late, TOK)], axis=1)
    lines = small_ref.shape[0]
    small = ring_small(
        small_ref, [of_halves(ref[TOK : TOK + lines, :], ref[TOK + lines :, :]) for ref in late[1:]]
    )
    high, rest = two_halves(small)
    tail = jnp.concatenate([high, rest], axis=0)
    rows = TOK // 4
    keep_ref[...] = total[:rows]
    width = total.shape[1]
    for step in (1, 2, 3):
        send_refs[step - 1][:, :width] = total[step * rows : (step + 1) * rows].astype(BF16)
        send_refs[step - 1][:, width:] = tail
    sent_ref[...] = of_halves(high, rest)


def last_ring_kernel(*refs):
    a_refs, b_refs, small_ref = (refs[:4], refs[4:8], refs[8])
    keep_ref, away_ref, sent_ref, pair_ref, cross_ref = refs[9:]
    rows = TOK // 4
    width = b_refs[0].shape[1]
    lines = small_ref.shape[0]
    total_b = b_refs[0][...] + (
        b_refs[1][:, :width].astype(F32) + b_refs[2][:, :width].astype(F32) + b_refs[3][:, :width].astype(F32)
    )
    total = jnp.concatenate([ring_total(a_refs, rows), total_b], axis=1)
    small = ring_small(
        small_ref, [of_halves(ref[:lines, width:], ref[lines:, width:]) for ref in b_refs[1:]]
    )
    high, rest = two_halves(small)
    keep_ref[...] = total[: rows // 2]
    away_ref[:, : total.shape[1]] = total[rows // 2 :].astype(BF16)
    away_ref[:, total.shape[1] :] = jnp.concatenate([high, rest], axis=1)
    small = of_halves(high, rest)
    sent_ref[...] = small
    stop = a_refs[0].shape[1]
    shared = total[:, stop - 2 * NS : stop]
    pair_ref[...] = jnp.concatenate([shared[: rows // 2], small], axis=1)
    shared = shared[rows // 2 :].astype(BF16).astype(F32)
    cross_ref[...] = jnp.concatenate([shared, small], axis=1)


def in_grads_kernel(normed_ref, low_ref, keep_ref, send_ref):
    half = MODEL_WIDTH // 2
    low = low_ref[...]
    keep_ref[...] = dot_low(normed_ref[:, :half], low, 0, 0).astype(BF16)
    send_ref[...] = dot_low(normed_ref[:, half:], low, 0, 0).astype(BF16)


def finish_grads_kernel(keep_ref, theirs_ref, small_ref, pair_ref, cross_ref, *refs):
    *out_refs, own_ref, sum_ref = refs
    others = pair_ref[...] + cross_ref[...]
    at = 0
    for number, ref in enumerate(out_refs):
        lanes = slice(at, at + ref.shape[1])
        total = keep_ref[:, lanes] + theirs_ref[:, lanes].astype(F32)
        ref[...] = total + others[:, : 2 * NS] if number == SHARED else total
        at += ref.shape[1]
    at = keep_ref.shape[1]
    width = small_ref.shape[1]
    own = small_ref[...] + of_halves(theirs_ref[:, at : at + width], theirs_ref[:, at + width :])
    own_ref[...] = own
    sum_ref[...] = own + others[:, 2 * NS :]


def low_b_kernel(query_ref, kv_ref, dt_ref, cosine_ref, sine_ref, out_ref):
    grads = jnp.concatenate([query_ref[...], kv_ref[...]], axis=1)
    out_ref[:, :ROPED] = turn(grads, cosine_ref[...], -sine_ref[...]).astype(BF16)
    out_ref[:, ROPED:] = dt_ref[...]


def slot_of(pair, index):
    y, x, z = (index >> 5, (index >> 3) & 3, (index >> 1) & 3)
    dy = ((pair >> 4) - y) & 1
    dx = ((pair >> 2) - x) & 3
    dz = (pair - z) & 3
    return pl.multiple_of(((dx * 4 + dz) * 2 + dy) * TOK, TOK)


def load_quad(quad, index, own_ref, other_ref):
    parts = []
    for side in (0, 1):
        slot = slot_of(quad * 2 + side, index)
        parts += [own_ref[pl.ds(slot, TOK), :], other_ref[pl.ds(slot, TOK), :]]
    return jnp.concatenate(parts, axis=0)


def head_columns(rows):
    turned = rows.T
    heads = rows.shape[1] // HEAD_SIZE
    return jnp.concatenate(
        [turned[head * HEAD_SIZE : (head + 1) * HEAD_SIZE] for head in range(heads)], axis=1
    )


def head_rows(rows):
    heads = rows.shape[1] // HEAD_SIZE
    return jnp.concatenate(
        [rows[:, head * HEAD_SIZE : (head + 1) * HEAD_SIZE] for head in range(heads)], axis=0
    )


def rows_of_columns(columns):
    heads = columns.shape[1] // TOK
    stacked = jnp.concatenate(
        [columns[:, head * TOK : (head + 1) * TOK] for head in range(heads)], axis=0
    )
    return stacked.T


def quad_mask(shape, quad, index):
    row = rows_of(shape)
    block = quad * 4 + (row >> 8) * 2 + ((index & 1) ^ ((row >> 7) & 1))
    keys = block * TOK + (row & (TOK - 1))
    queries = index * TOK + (lanes_of(shape) & (TOK - 1))
    return keys <= queries


def attend_kernel(index_ref, query_ref, own_ref, other_ref, columns_ref, rows_ref, log_ref, total_ref, even_ref, odd_ref):
    index = index_ref[0]
    query = head_columns(query_ref[...].astype(F32) * HEAD_SIZE ** (-0.5))
    padded = jnp.concatenate([query, jnp.zeros_like(query)], axis=0).astype(BF16)
    total_ref[...] = jnp.zeros_like(total_ref)

    def scores_of(quad):
        quad_kv = load_quad(quad, index, own_ref, other_ref)
        return jnp.dot(quad_kv, padded, preferred_element_type=F32)

    def step(quad, carry, scores):
        peak, weight = carry
        quad_kv = load_quad(quad, index, own_ref, other_ref)
        new_peak = jnp.maximum(peak, jnp.max(scores, axis=0, keepdims=True))
        shrink = jnp.exp(peak - new_peak)
        probs = jnp.exp(scores - new_peak)
        weight = weight * shrink + jnp.sum(probs, axis=0, keepdims=True)
        total_ref[...] = total_ref[...] * shrink + dot_low(quad_kv, probs.astype(BF16), 0, 0)
        return (new_peak, weight)

    lanes = (1, query.shape[1])
    last = index >> 2
    even_ref[...] = scores_of(0)
    scores = scores_of(last)
    scores = jnp.where(quad_mask(scores.shape, last, index), scores, MASKED)
    carry = step(last, (jnp.full(lanes, MASKED, F32), jnp.zeros(lanes, F32)), scores)

    def two_steps(count, carry):
        quad = 2 * count
        odd_ref[...] = scores_of(quad + 1)
        carry = step(quad, carry, even_ref[...])
        even_ref[...] = scores_of(jnp.minimum(quad + 2, last))
        return step(quad + 1, carry, odd_ref[...])

    carry = lax.fori_loop(0, last >> 1, two_steps, carry)
    peak, weight = lax.fori_loop(
        0, last & 1, lambda count, carry: step(last - 1, carry, even_ref[...]), carry
    )
    columns = total_ref[HEAD_SIZE:, :] / weight
    columns_ref[...] = columns
    rows_ref[...] = rows_of_columns(columns).astype(BF16)
    log_ref[...] = peak + jnp.log(weight)


def attend(index, query_low, own_kv, other_kv):
    lanes = QUERY_WIDTH // HEAD_SIZE * TOK
    vmem = pl.BlockSpec(memory_space=pltpu.VMEM)
    return pl.pallas_call(
        attend_kernel,
        out_shape=(
            jax.ShapeDtypeStruct((HEAD_SIZE, lanes), F32),
            jax.ShapeDtypeStruct((TOK, QUERY_WIDTH), BF16),
            jax.ShapeDtypeStruct((1, lanes), F32),
        ),
        in_specs=[pl.BlockSpec(memory_space=pltpu.SMEM), vmem, vmem, vmem],
        out_specs=(vmem, vmem, vmem),
        scratch_shapes=[pltpu.VMEM((2 * HEAD_SIZE, lanes), F32)] + [pltpu.VMEM((4 * TOK, lanes), F32)] * 2,
        compiler_params=pltpu.CompilerParams(vmem_limit_bytes=24 * 2**20),
        cost_estimate=pl.CostEstimate(flops=13 * 10**9, bytes_accessed=0, transcendentals=0),
        name="attend",
    )(index, query_low, own_kv, other_kv)


def attend_back_kernel(
    index_ref, query_ref, grad_ref, columns_ref, log_ref, own_ref, other_ref,
    grad_query_ref, grad_own_ref, grad_other_ref, total_ref, even_ref, odd_ref,
):
    index = index_ref[0]
    scale = HEAD_SIZE ** (-0.5)
    query_rows = query_ref[...].astype(F32) * scale
    grad_rows = grad_ref[...].astype(F32)
    query = head_columns(query_rows)
    grad = head_columns(grad_rows)
    blank = jnp.zeros_like(query)
    query_pad = jnp.concatenate([query, blank], axis=0).astype(BF16)
    grad_pad = jnp.concatenate([blank, grad], axis=0).astype(BF16)
    query_tall = head_rows(query_rows)
    grad_tall = head_rows(grad_rows)
    blank = jnp.zeros_like(query_tall)
    sides = jnp.concatenate(
        [
            jnp.concatenate([query_tall, blank], axis=1),
            jnp.concatenate([blank, grad_tall], axis=1),
        ],
        axis=0,
    ).astype(BF16)
    delta = jnp.sum(grad * columns_ref[...], axis=0, keepdims=True)
    log_total = log_ref[...]
    total_ref[...] = jnp.zeros_like(total_ref)
    grad_own_ref[...] = jnp.zeros_like(grad_own_ref)
    grad_other_ref[...] = jnp.zeros_like(grad_other_ref)

    def products_of(quad):
        quad_kv = load_quad(quad, index, own_ref, other_ref)
        return (
            jnp.dot(quad_kv, query_pad, preferred_element_type=F32),
            jnp.dot(quad_kv, grad_pad, preferred_element_type=F32),
        )

    def step(quad, scores, grad_probs, masked):
        quad_kv = load_quad(quad, index, own_ref, other_ref)
        probs = jnp.exp(scores - log_total)
        if masked:
            probs = jnp.where(quad_mask(scores.shape, quad, index), probs, 0.0)
        grad_scores = (probs * (grad_probs - delta)).astype(BF16)
        total_ref[...] += dot_low(quad_kv, grad_scores, 0, 0)
        both = jnp.concatenate([grad_scores, probs.astype(BF16)], axis=1)
        term = jnp.dot(both, sides, preferred_element_type=F32).astype(BF16)
        for side in (0, 1):
            slot = slot_of(quad * 2 + side, index)
            at = side * 2 * TOK
            grad_own_ref[pl.ds(slot, TOK), :] = term[at : at + TOK]
            grad_other_ref[pl.ds(slot, TOK), :] = term[at + TOK : at + 2 * TOK]

    last = index >> 2
    even_ref[0], even_ref[1] = products_of(0)
    step(last, *products_of(last), True)

    def two_steps(count, carry):
        quad = 2 * count
        odd_ref[0], odd_ref[1] = products_of(quad + 1)
        step(quad, even_ref[0], even_ref[1], False)
        even_ref[0], even_ref[1] = products_of(jnp.minimum(quad + 2, last))
        step(quad + 1, odd_ref[0], odd_ref[1], False)
        return carry

    lax.fori_loop(0, last >> 1, two_steps, 0)

    def final_step(count, carry):
        step(last - 1, even_ref[0], even_ref[1], False)
        return carry

    lax.fori_loop(0, last & 1, final_step, 0)
    grad_query_ref[...] = rows_of_columns(total_ref[:HEAD_SIZE, :] * scale)


def attend_back(index, query_low, grad_low, columns, log_total, own_kv, other_kv):
    vmem = pl.BlockSpec(memory_space=pltpu.VMEM)
    return pl.pallas_call(
        attend_back_kernel,
        out_shape=(
            jax.ShapeDtypeStruct(query_low.shape, F32),
            jax.ShapeDtypeStruct(own_kv.shape, BF16),
            jax.ShapeDtypeStruct(other_kv.shape, BF16),
        ),
        in_specs=[pl.BlockSpec(memory_space=pltpu.SMEM)] + [vmem] * 6,
        out_specs=(vmem, vmem, vmem),
        scratch_shapes=[pltpu.VMEM((2 * HEAD_SIZE, columns.shape[1]), F32)]
        + [pltpu.VMEM((2, 4 * TOK, columns.shape[1]), F32)] * 2,
        compiler_params=pltpu.CompilerParams(vmem_limit_bytes=24 * 2**20),
        cost_estimate=pl.CostEstimate(flops=19 * 10**9, bytes_accessed=0, transcendentals=0),
        name="attend_back",
    )(index, query_low, grad_low, columns, log_total, own_kv, other_kv)


def shards(
    tokens,
    cotangent,
    gain_first,
    z_weight,
    x_weight,
    bc_weight,
    dt_weight,
    conv_x_weight,
    conv_x_bias,
    conv_bc_weight,
    conv_bc_bias,
    dt_bias,
    decay_rate,
    skip_weight,
    out_weight,
    q_weight,
    key_matrix,
    value_matrix,
    o_weight,
    gain_second,
    gate_weight,
    up_weight,
    down_weight,
):
    index = lax.axis_index(SEQ)
    index_word = jnp.reshape(index, (1,)).astype(jnp.int32)
    ff = gate_weight.shape[1]
    in_a_width = WIDTH + 2 * NS
    in_b_width = WIDTH + ROPED + NS

    def padded_heads(values):
        return jnp.pad(values, (0, NS - HEADS))[None, :]

    together = lax.optimization_barrier
    together = lax.optimization_barrier
    with jax.named_scope("gather_near"):
        dt_wide = jnp.pad(dt_weight, ((0, 0), (0, NS - HEADS)))
        near_a = jnp.concatenate([x_weight, bc_weight, gate_weight, up_weight], axis=1)
        near_b = jnp.concatenate(
            [z_weight, q_weight, key_matrix, value_matrix, dt_wide, out_weight, o_weight, down_weight],
            axis=1,
        )
        split = near_a.shape[1]
        theirs = send(jnp.concatenate([near_a, near_b], axis=1), OTHER_Y)
        near_a = fetch(joined([near_a, theirs[:, :split]]), along_x)
        near_b = fetch(joined([near_b, theirs[:, split:]]), along_z)
        near_a, near_b = join_rings(near_a, near_b, vmem=8)
    with jax.named_scope("orders"):
        halo = send(tokens[TOK - (CONV_K - 1) :], ONWARD)
        ahead = jnp.zeros((HALO - (CONV_K - 1), MODEL_WIDTH), BF16)
        tokens_ext = jnp.concatenate([ahead, halo, tokens], axis=0)
        to_a, to_b = one_hot_orders(index)
        normed = rms_norm(tokens_ext.astype(F32), gain_first).astype(BF16)
        normed_a = project(normed, to_a).astype(BF16)
        normed_b = project(normed[HALO:], to_b).astype(BF16)
        cot_b = project(cotangent, to_b).astype(BF16)
        cosine, sine = rotary_tables(index)
        conv_weight = jnp.concatenate([conv_x_weight, conv_bc_weight], axis=1)
        conv_bias = jnp.concatenate([conv_x_bias, conv_bc_bias], axis=0)[None, :]
        decay_wide = padded_heads(decay_rate)
        skip_wide = padded_heads(skip_weight)
        dt_bias_wide = padded_heads(dt_bias)
    with jax.named_scope("gather_in"):
        in_a, rest_a = (near_a[:, :in_a_width], near_a[:, in_a_width:])
        in_b, rest_b = (near_b[:, :in_b_width], near_b[:, in_b_width:])
        (in_a, in_b), (normed_a, normed_b, to_a, to_b) = together(
            ((ring_near(in_a, along_z), ring_near(in_b, along_x)), (normed_a, normed_b, to_a, to_b))
        )
        in_a, in_b = (ring_far(in_a, along_z), ring_far(in_b, along_x))
        (in_a, in_b), (cot_b, cosine, sine) = together(((in_a, in_b), (cot_b, cosine, sine)))
        in_a_own, in_b_own = join_rings(in_a, in_b)
        in_b_other = send(in_b_own, OTHER_CORE)
        in_a_other = send(in_a_own, OTHER_CORE)
        in_a_other, in_b_other = together((in_a_other, in_b_other))
    with jax.named_scope("attention_in"):
        gate_raw, query_low, kv_low, dt_pre, step_size, log_decay = kernel_call(
            attention_in_kernel,
            [((TOK, WIDTH), F32), ((TOK, QUERY_WIDTH), BF16), ((TOK, 2 * HEAD_SIZE), BF16)]
            + [((TOK, NS), F32)] * 3,
            normed_b, in_b_own, in_b_other, cosine, sine, dt_bias_wide, decay_wide,
            name="attention_in",
        )
    with jax.named_scope("gather_kv"):
        kv_low, rest_a, rest_b = together((kv_low, rest_a, rest_b))
        own_kv = joined([kv_low, send(kv_low, OTHER_Y)])
    with jax.named_scope("gather_rest"):
        rest_a, rest_b = (ring_near(rest_a, along_z), ring_near(rest_b, along_x))
    with jax.named_scope("ssm_in"):
        ext, conved, payload = kernel_call(
            ssm_in_kernel,
            [((HALO + TOK, MODEL_WIDTH), F32), ((TOK, MODEL_WIDTH), F32), ((P_SIZE, SLOTS, NS), F32)],
            normed_a, in_a_own, in_a_other, conv_weight, conv_bias, step_size, log_decay,
            us=3, name="ssm_in",
        )
    with jax.named_scope("state_forward"):
        payload, rest_a, rest_b, own_kv = together((payload, rest_a, rest_b, own_kv))
        spans = swap_spans(payload)
        own_kv = fetch(own_kv, along_z)
        rest_b = ring_far(rest_b, along_x)
        spans, own_kv, rest_a, rest_b = together((spans, own_kv, rest_a, rest_b))
        entering = states_between(spans, spans, False)
        own_kv = fetch(join_rings(own_kv, vmem=4, far=True)[0], along_x)
        rest_a = ring_far(rest_a, along_z)
        entering, own_kv, rest_a, rest_b = together((entering, own_kv, rest_a, rest_b))
        own_kv = join_rings(own_kv, vmem=4)[0]
        other_kv = send(own_kv, OTHER_CORE)
        state_in = swap_spans(entering)
        state_in, own_kv, other_kv, rest_a, rest_b = together((state_in, own_kv, other_kv, rest_a, rest_b))
    with jax.named_scope("gather_rest"):
        rest_a_own, rest_b_own = join_rings(rest_a, rest_b, far=True)
        rest_b_other = send(rest_b_own, OTHER_CORE)
        rest_a_other = send(rest_a_own, OTHER_CORE)
    with jax.named_scope("attention"):
        attended_columns, attended_low, log_total = attend(index_word, query_low, own_kv, other_kv)
    with jax.named_scope("ssm_out"):
        gated_low, y = kernel_call(
            ssm_out_kernel, [((TOK, WIDTH), BF16), ((TOK, WIDTH), F32)],
            conved, step_size, log_decay, state_in, gate_raw, skip_wide,
            us=2, name="ssm_out",
        )
        gated_low, attended_low, rest_a_other, rest_b_other = together(
            (gated_low, attended_low, rest_a_other, rest_b_other)
        )
    with jax.named_scope("mixer_out"):
        mixed = kernel_call(
            mixer_out_kernel, [((TOK, MODEL_WIDTH), BF16)],
            gated_low, attended_low, rest_b_own, rest_b_other, to_b,
            us=2, name="mixer_out",
        )[0]
        mixed_theirs = swap_heads(mixed)
    with jax.named_scope("ffn"):
        grad_inner = kernel_call(
            down_back_kernel, [((TOK, ff), F32)], cot_b, rest_b_own, rest_b_other,
            vmem=12, us=2, name="down_back",
        )[0]
        mixed_theirs, grad_inner = together((mixed_theirs, grad_inner))
        hidden, normed_second, inner_low, grad_ff, second_part = kernel_call(
            ffn_kernel,
            [((TOK, MODEL_WIDTH), F32), ((TOK, MODEL_WIDTH), BF16), ((TOK, ff), BF16),
             ((TOK, 2 * ff), BF16), ((TOK, MODEL_WIDTH), BF16)],
            tokens, mixed, mixed_theirs, gain_second[None, :], grad_inner, to_a,
            rest_a_own, rest_a_other,
            vmem=20, us=5, name="ffn",
        )
        second_theirs = swap_heads(second_part)
        ffn_part = kernel_call(
            ffn_out_kernel, [((TOK, MODEL_WIDTH), BF16)], inner_low, rest_b_own, rest_b_other, to_b,
            vmem=16, us=2, name="ffn_out",
        )[0]
        half = (MODEL_WIDTH // 2,)
        a_keep, a_send, b_keep, b_send = kernel_call(
            ffn_grads_kernel, [(half + (2 * ff,), BF16)] * 2 + [(half + (ff,), BF16)] * 2,
            normed_second, grad_ff, cot_b, inner_low, vmem=16, us=2, name="ffn_grads",
        )
        ffn_keep = (a_keep, b_keep)
        ffn_arrived = (send(a_send, OTHER_CORE), send(b_send, OTHER_CORE))
        second_theirs, ffn_part = together((second_theirs, ffn_part))
    with jax.named_scope("mixer_back"):
        (
            grad_hidden, grad_mixed_b, gain_second_part, grad_attended, grad_y, grad_gate_low, payload_back
        ) = kernel_call(
            mixer_back_kernel,
            [((TOK, MODEL_WIDTH), F32, FAR), ((TOK, MODEL_WIDTH), BF16, FAR), ((1, MODEL_WIDTH), F32),
             ((TOK, QUERY_WIDTH), BF16, FAR), ((TOK, WIDTH), F32, FAR), ((TOK, WIDTH), BF16, FAR),
             ((P_SIZE, SLOTS, NS), F32, FAR)],
            hidden, second_part, second_theirs, gain_second[None, :], cotangent, to_b,
            rest_b_own, rest_b_other, gate_raw, y, conved, log_decay,
            vmem=20, us=3, name="mixer_back",
        )
        ffn_theirs = swap_heads(ffn_part)
    with jax.named_scope("early_grads"):
        early_a, early_b = (2 * ff + WIDTH, ff + WIDTH + QUERY_WIDTH)
        a_keep, a_send, b_keep, b_send = kernel_call(
            mixer_grads_kernel,
            [(half + (WIDTH,), BF16, FAR)] * 2 + [(half + (WIDTH + QUERY_WIDTH,), BF16, FAR)] * 2,
            normed_a, grad_gate_low, grad_mixed_b, gated_low, attended_low, far=range(5), vmem=12, name="mixer_grads",
        )
    with jax.named_scope("state_backward"):
        arrived_back = swap_spans(payload_back)
        arrived_back, a_send, b_send, ffn_arrived = together((arrived_back, a_send, b_send, ffn_arrived))
        leaving = states_between(spans, arrived_back, True)
        a_arrived = send(a_send, OTHER_CORE)
        b_arrived = send(b_send, OTHER_CORE)
        state_grad = swap_spans(leaving)
        state_grad, a_arrived, b_arrived = together((state_grad, a_arrived, b_arrived))
    with jax.named_scope("early_grads"):
        a_keep, a_ahead, a_behind, a_first, a_second = halve(
            ffn_keep[0], ffn_arrived[0], a_keep, a_arrived
        )
        b_keep, b_ahead, b_behind, b_first, b_second = halve(
            ffn_keep[1], ffn_arrived[1], b_keep, b_arrived
        )
        a_passed = [send(a_first, along_z(1)), send(a_second, along_z(-1))]
        b_passed = [send(b_first, along_x(1)), send(b_second, along_x(-1))]
    with jax.named_scope("ssm_back"):
        low_a, grad_dt_low, small = kernel_call(
            ssm_back_kernel,
            [((HALO + TOK, MODEL_WIDTH), BF16), ((TOK, NS), BF16), ((2 * CONV_K, MODEL_WIDTH), F32)],
            grad_y, conved, step_size, log_decay, dt_pre, state_in, state_grad, ext,
            conv_weight, conv_bias, decay_wide, skip_wide,
            scratch=[
                pltpu.VMEM((NS, TOK), F32),
                pltpu.VMEM((2 * HALO + TOK, MODEL_WIDTH), F32),
                pltpu.VMEM((TOK, MODEL_WIDTH), F32),
            ],
            vmem=16, us=8, name="ssm_back",
        )
        low_a, grad_dt_low, small, a_passed, b_passed, ffn_theirs = together(
            (low_a, grad_dt_low, small, a_passed, b_passed, ffn_theirs)
        )
    with jax.named_scope("late_grads"):
        late_keep, late_send = kernel_call(
            in_grads_kernel, [(half + (in_a_width,), BF16)] * 2, normed_a, low_a,
            vmem=12, name="late_grads_a",
        )
        late_arrived = send(late_send, OTHER_CORE)
    with jax.named_scope("early_grads"):
        a_ahead, a_behind, b_ahead, b_behind = pass_on(
            [a_ahead, a_behind] + a_passed, [b_ahead, b_behind] + b_passed
        )
        a_ready = [a_keep, send(a_ahead, along_z(1)), send(a_behind, along_z(-1))]
        b_ready = [b_keep, send(b_ahead, along_x(1)), send(b_behind, along_x(-1))]
    with jax.named_scope("attention_back"):
        grad_query, grad_own_kv, grad_other_kv = attend_back(
            index_word, query_low, grad_attended, attended_columns, log_total, own_kv, other_kv
        )
        (grad_query, grad_own_kv, grad_other_kv), a_ready, b_ready, late_arrived = together(
            ((grad_query, grad_own_kv, grad_other_kv), a_ready, b_ready, late_arrived)
        )
    with jax.named_scope("late_grads"):
        late_keep, late_ahead, late_behind, late_first, late_second = halve(
            late_keep, late_arrived, vmem=8
        )
        late_passed = [send(late_first, along_z(1)), send(late_second, along_z(-1))]
    with jax.named_scope("scatter_kv"):
        kv_arrived = send(grad_other_kv, OTHER_CORE)
        kv_arrived, late_passed = together((kv_arrived, late_passed))
        grad_kv = blocks_of([grad_own_kv, kv_arrived], 4)
        kv_arrived = spread(grad_kv, along_x)
    with jax.named_scope("late_grads"):
        late_ahead, late_behind = pass_on([late_ahead, late_behind] + late_passed, vmem=8)
        a_late = [late_keep, send(late_ahead, along_z(1)), send(late_behind, along_z(-1))]
        kv_arrived, a_late = together((kv_arrived, a_late))
    with jax.named_scope("last_grads"):
        rows = TOK // 4
        wide_a = early_a + in_a_width
        a_last = kernel_call(
            merge_a_kernel, [((rows, wide_a), F32)] + [((rows, wide_a), BF16)] * 3,
            *a_ready, *a_late, vmem=12, name="merge_a",
        )
    with jax.named_scope("project_in_back"):
        returned = send(low_a[HALO - (CONV_K - 1) : HALO], BACKWARD)
        low_own = low_a[HALO:].astype(F32) + jnp.pad(
            returned.astype(F32), ((TOK - (CONV_K - 1), 0), (0, 0))
        )
        from_a = kernel_call(
            project_a_kernel, [((TOK, MODEL_WIDTH), F32)],
            low_own.astype(BF16), grad_gate_low, in_a_own, in_a_other, in_b_own, in_b_other, to_a, to_b,
            vmem=20, us=2, name="project_a",
        )[0]
    with jax.named_scope("scatter_kv"):
        grad_kv = ring_sum(grad_kv, kv_arrived)
        grad_kv = blocks_of([grad_kv], 4)
        kv_arrived = spread(grad_kv, along_z)
        kv_arrived, from_a, a_last = together((kv_arrived, from_a, a_last))
        grad_kv = ring_sum(grad_kv, kv_arrived)
        kv_theirs = send(grad_kv[TOK:].astype(BF16), OTHER_Y)
        a_last = [a_last[0]] + spread(a_last, along_x)
        grad_kv = grad_kv[:TOK] + kv_theirs.astype(F32)
    with jax.named_scope("project_in_back"):
        late_b = ROPED + NS
        low_b = kernel_call(
            low_b_kernel, [((TOK, late_b), BF16)],
            grad_query, grad_kv, grad_dt_low, cosine, sine, vmem=8, name="low_b",
        )[0]
        first_part, gain_first_part = kernel_call(
            project_b_kernel, [((TOK, MODEL_WIDTH), BF16), ((1, MODEL_WIDTH), F32)],
            low_b, from_a, in_b_own, in_b_other, to_b, tokens, vmem=12, us=1, name="project_b",
        )
    with jax.named_scope("late_grads"):
        small = jnp.concatenate(
            [small[: CONV_K + 1], gain_first_part, gain_second_part, small[CONV_K + 3 :]], axis=0
        )
        lines, line = (SLOTS, MODEL_WIDTH // 2)
        b_keep, b_send, small = kernel_call(
            late_b_kernel,
            [(half + (late_b,), BF16), ((line + 2 * lines, late_b), BF16), ((lines, line), F32)],
            normed_b, low_b, small, vmem=12, name="late_grads_b",
        )
        *b_late, small = kernel_call(
            late_b_ring_kernel,
            [((TOK, late_b), F32)] + [((TOK + 2 * lines, late_b), BF16)] * 3 + [((lines, line), F32)],
            b_keep, send(b_send, OTHER_CORE), small, vmem=8, name="late_ring_b",
        )
        b_late = [b_late[0]] + spread(b_late, along_x)
    with jax.named_scope("last_grads"):
        wide_b = early_b + late_b
        *b_last, small = kernel_call(
            merge_b_kernel,
            [((rows, wide_b), F32)] + [((rows, wide_b + line), BF16)] * 3 + [((lines, line), F32)],
            *b_ready, *b_late, small, vmem=12, name="merge_b",
        )
        b_last = [b_last[0]] + spread(b_last, along_z)
        rows = rows // 2
        own, away, small, pair, cross = kernel_call(
            last_ring_kernel,
            [((rows, wide_a + wide_b), F32), ((rows, wide_a + wide_b + 2 * line), BF16),
             ((lines, line), F32), ((rows, 2 * NS + line), F32), ((rows, 2 * NS + line), F32)],
            *a_last, *b_last, small, vmem=8, name="last_ring",
        )
    with jax.named_scope("finish_grads"):
        widths = (ff, ff, WIDTH, WIDTH, 2 * NS, ff, WIDTH, QUERY_WIDTH, QUERY_WIDTH, HEAD_SIZE, HEAD_SIZE, NS)
        (
            grad_gate, grad_up, grad_z, grad_x, grad_bc, grad_down, grad_out, grad_o, grad_q, grad_k,
            grad_v, grad_dt, small, total
        ) = kernel_call(
            finish_grads_kernel,
            [((rows, width), F32) for width in widths] + [((lines, line), F32)] * 2,
            own, send(away, OTHER_Y), small, swap_heads(pair),
            lax.ppermute(cross, (SEQ, "head"), OTHER_Y_AND_HEAD), vmem=8, name="finish_grads",
        )
        grad_dt = grad_dt[:, :HEADS]
        small = jnp.concatenate([small[: 2 * CONV_K], small[2 * CONV_K :]], axis=1)
        total = jnp.concatenate([total[: 2 * CONV_K], total[2 * CONV_K :]], axis=1)
    with jax.named_scope("finish"):
        grad_first = first_part.astype(F32) + swap_heads(first_part).astype(F32)
        grad_tokens = grad_hidden + norm_back(tokens.astype(F32), gain_first[None, :], grad_first)[1]
        output = (hidden + (ffn_part.astype(F32) + ffn_theirs.astype(F32))).astype(BF16)
    with jax.named_scope("small_grads"):
        summed_gain_first = total[CONV_K + 1]
        summed_gain_second = total[CONV_K + 2]
        grad_conv_x = small[:CONV_K, :WIDTH]
        grad_conv_xb = small[CONV_K, :WIDTH]
        summed_conv_bc = total[:CONV_K, WIDTH:]
        summed_conv_bcb = total[CONV_K, WIDTH:]
        grad_dt_bias_own = small[CONV_K + 3, :HEADS]
        grad_decay_own = small[CONV_K + 3, NS : NS + HEADS]
        grad_skip_own = small[CONV_K + 3, 2 * NS : 2 * NS + HEADS]
    return (
        output,
        grad_tokens,
        summed_gain_first,
        grad_z,
        grad_x,
        grad_bc,
        grad_dt,
        grad_conv_x,
        grad_conv_xb,
        summed_conv_bc,
        summed_conv_bcb,
        grad_dt_bias_own,
        grad_decay_own,
        grad_skip_own,
        grad_out,
        grad_q,
        grad_k,
        grad_v,
        grad_o,
        summed_gain_second,
        grad_gate,
        grad_up,
        grad_down,
    )


def solution(mesh):
    return jax.shard_map(
        shards,
        mesh=mesh,
        in_specs=(
            P("seq", None),
            P("seq", None),
            P(),
            P("seq", "head"),
            P("seq", "head"),
            P("seq", None),
            P("seq", "head"),
            P(None, "head"),
            P("head"),
            P(),
            P(),
            P("head"),
            P("head"),
            P("head"),
            P("seq", "head"),
            P("seq", "head"),
            P("seq", "head"),
            P("seq", "head"),
            P("seq", "head"),
            P(),
            P("seq", "head"),
            P("seq", "head"),
            P("seq", "head"),
        ),
        out_specs=(
            P("seq", None),
            P("seq", None),
            P(),
            P("seq", "head"),
            P("seq", "head"),
            P("seq", None),
            P("seq", "head"),
            P(None, "head"),
            P("head"),
            P(),
            P(),
            P("head"),
            P("head"),
            P("head"),
            P("seq", "head"),
            P("seq", "head"),
            P("seq", "head"),
            P("seq", "head"),
            P("seq", "head"),
            P(),
            P("seq", "head"),
            P("seq", "head"),
            P("seq", "head"),
        ),
        check_vma=False,
    )
```

```python
import functools

import jax
import jax.numpy as jnp
from jax import lax
from jax.experimental import pallas as pl
from jax.experimental.pallas import tpu as pltpu
from jax.sharding import PartitionSpec as P

MODEL_WIDTH = 1024
NH = 24
P_SIZE = 64
NS = 128
HEAD_SIZE = 64
CONV_K = 4
TOK = 128
SPANS = 64
HEADS = 12
WIDTH = HEADS * P_SIZE
QUERY_WIDTH = 256
ROPED = QUERY_WIDTH + 2 * HEAD_SIZE
SLOTS = 16
SHARED = 4
HALO = 16
KEY_ROWS = SPANS // 2 * TOK

EPS = 1e-06
ROPE_BASE = 100000000000.0
MASKED = -1e30
HIGHEST = lax.Precision.HIGHEST
BF16 = jnp.bfloat16
F32 = jnp.float32
SEQ = "seq"


def place(index):
    return (index // 32, (index // 8) % 4, (index // 2) % 4, index % 2)


def index_of(y, x, z, core):
    return ((y * 4 + x) * 4 + z) * 2 + core


def pairs(move):
    return [(source, index_of(*move(*place(source)))) for source in range(SPANS)]


OTHER_CORE = pairs(lambda y, x, z, c: (y, x, z, 1 - c))
OTHER_Y = pairs(lambda y, x, z, c: (1 - y, x, z, c))
OTHER_HEAD = [(0, 1), (1, 0)]
OTHER_Y_AND_HEAD = [
    (source * 2 + head, target * 2 + 1 - head) for source, target in OTHER_Y for head in range(2)
]
ONWARD = [(span, span + 1) for span in range(SPANS - 1)]
BACKWARD = [(span + 1, span) for span in range(SPANS - 1)]


def along_x(steps):
    return pairs(lambda y, x, z, c: (y, (x + steps) % 4, z, c))


def along_z(steps):
    return pairs(lambda y, x, z, c: (y, x, (z + steps) % 4, c))


def send(value, route):
    return lax.ppermute(value, SEQ, route)


def swap_heads(value):
    return lax.ppermute(value, "head", OTHER_HEAD)


def swap_spans(value):
    return lax.all_to_all(value, SEQ, 0, 0, tiled=True)


def after(value, *others):
    return lax.optimization_barrier((value, others))[0]


def joined(pieces):
    return jnp.concatenate(pieces, axis=0)


def fetch(value, along):
    return [value] + [send(value, along(-step)) for step in (1, 2, 3)]


def ring_near(value, along):
    return (value, send(value, along(-1)), send(value, along(1)))


def ring_far(near, along):
    own, ahead, behind = near
    half = own.shape[0] // 2
    first = send(ahead[:half], along(-1))
    second = send(behind[half:], along(1))
    return [own, ahead, first, second, behind]


def blocks_of(parts, count):
    rows = parts[0].shape[0] // count
    return [
        sum(part[block * rows : (block + 1) * rows].astype(F32) for part in parts)
        for block in range(count)
    ]


def spread(blocks, along):
    return [send(block.astype(BF16), along(step)) for step, block in enumerate(blocks) if step]


def ring_sum(blocks, arrived):
    return blocks[0] + sum(block.astype(F32) for block in arrived)


def scatter_ring(parts, along):
    blocks = blocks_of(parts, 4)
    return ring_sum(blocks, spread(blocks, along))


def one_hot_orders(index):
    y, x, z, c = place(index)
    row = jnp.arange(MODEL_WIDTH, dtype=jnp.int32)
    inner = row % 16
    dy, low, high, dc = ((row // 16) % 2, (row // 32) % 4, (row // 128) % 4, row // 512)

    def one_hot(dx, dz):
        device = index_of((y + dy) % 2, (x + dx) % 4, (z + dz) % 4, (c + dc) % 2)
        return (row[:, None] == (device * 16 + inner)[None, :]).astype(BF16)

    return (one_hot(low, high), one_hot(high, low))


def project(left_side, right_side):
    return jnp.dot(left_side, right_side, preferred_element_type=F32)


def rms_norm(values, norm_gain):
    return values * lax.rsqrt(jnp.mean(values * values, axis=-1, keepdims=True) + EPS) * norm_gain


def rotary_tables(index):
    half = HEAD_SIZE // 2
    frequency = ROPE_BASE ** (-jnp.arange(half, dtype=F32) * (1.0 / half))
    positions = (index * TOK + jnp.arange(TOK, dtype=jnp.int32)).astype(F32)
    angles = positions[:, None] * frequency[None, :]
    cosine, sine = (jnp.cos(angles), jnp.sin(angles))
    turns = QUERY_WIDTH // HEAD_SIZE + 1
    plain = jnp.ones((TOK, HEAD_SIZE), F32)
    return (
        jnp.concatenate([cosine, cosine] * turns + [plain], axis=1),
        jnp.concatenate([-sine, sine] * turns + [0.0 * plain], axis=1),
    )


def dot_f32(left_side, right_side, left_dim=1, right_dim=0):
    return lax.dot_general(
        left_side, right_side, (((left_dim,), (right_dim,)), ((), ())), precision=HIGHEST,
        preferred_element_type=F32,
    )


def dot_low(left_side, right_side, left_dim=1, right_dim=0):
    return lax.dot_general(
        left_side, right_side, (((left_dim,), (right_dim,)), ((), ())), preferred_element_type=F32
    )


def lanes_of(shape):
    return lax.broadcasted_iota(jnp.int32, shape, len(shape) - 1)


def rows_of(shape):
    return lax.broadcasted_iota(jnp.int32, shape, len(shape) - 2)


def head_spread():
    shape = (NS, HEADS * P_SIZE)
    return (lanes_of(shape) // P_SIZE == rows_of(shape)).astype(F32)


def causal_mask():
    return rows_of((TOK, TOK)) >= lanes_of((TOK, TOK))


def sigmoid(values):
    return 1.0 / (1.0 + jnp.exp(-values))


def softplus(values):
    small = jnp.exp(-jnp.abs(values))
    series = small * (1.0 - small * (0.5 - small * (1.0 / 3.0 - small * 0.25)))
    return jnp.maximum(values, 0.0) + jnp.where(small < 0.01, series, jnp.log(1.0 + small))


def turn(values, cosine, sine):
    width = values.shape[1]
    half = HEAD_SIZE // 2
    ahead = pltpu.roll(values, width - half, 1)
    behind = pltpu.roll(values, half, 1)
    other = jnp.where(lanes_of(values.shape) % HEAD_SIZE < half, ahead, behind)
    return values * cosine + other * sine


FAR = "far"


def far_away(value):
    return pltpu.with_memory_space_constraint(value, pltpu.HBM)


def kernel_call(body, outs, *operands, far=(), scratch=(), vmem=16, us=1, name=None):
    vspec = pl.BlockSpec(memory_space=pltpu.VMEM)
    operands = [far_away(value) if at in far else value for at, value in enumerate(operands)]
    return pl.pallas_call(
        body,
        out_shape=tuple(
            pltpu.HBM(*out[:2]) if FAR in out else jax.ShapeDtypeStruct(*out) for out in outs
        ),
        in_specs=[vspec] * len(operands),
        out_specs=(vspec,) * len(outs),
        scratch_shapes=list(scratch),
        compiler_params=pltpu.CompilerParams(vmem_limit_bytes=vmem * 2**20),
        cost_estimate=pl.CostEstimate(flops=us * 10**9, bytes_accessed=0, transcendentals=0),
        name=name,
    )(*operands)


def attention_in_kernel(
    normed_ref, own_ref, other_ref, cosine_ref, sine_ref, dt_bias_ref, decay_ref,
    gate_ref, query_ref, kv_ref, dt_ref, step_ref, log_ref,
):
    normed = normed_ref[...]
    half = MODEL_WIDTH // 2
    raw = dot_low(normed[:, :half], own_ref[...]) + dot_low(normed[:, half:], other_ref[...])
    gate_ref[...] = raw[:, :WIDTH]
    turned = turn(raw[:, WIDTH : WIDTH + ROPED], cosine_ref[...], sine_ref[...]).astype(BF16)
    query_ref[...] = turned[:, :QUERY_WIDTH]
    kv_ref[...] = turned[:, QUERY_WIDTH:]
    dt = raw[:, WIDTH + ROPED :] + dt_bias_ref[...]
    step = softplus(dt)
    dt_ref[...] = dt
    step_ref[...] = step
    log_ref[...] = dot_f32(causal_mask().astype(F32), -step * decay_ref[...])


def convolved(ext_ref, conv_weight, conv_bias):
    summed = conv_bias
    for lag in range(CONV_K):
        summed = summed + conv_weight[lag : lag + 1] * ext_ref[pl.ds(HALO - CONV_K + 1 + lag, TOK), :]
    return summed


def ssm_in_kernel(
    normed_ref, own_ref, other_ref, conv_weight_ref, conv_bias_ref, step_ref, log_ref,
    ext_ref, conv_ref, state_ref,
):
    normed = normed_ref[...]
    half = MODEL_WIDTH // 2
    ext_ref[...] = dot_low(normed[:, :half], own_ref[...]) + dot_low(normed[:, half:], other_ref[...])
    summed = convolved(ext_ref, conv_weight_ref[...], conv_bias_ref[...])
    conved = summed * sigmoid(summed)
    conv_ref[...] = conved
    log_decay = log_ref[...]
    last = log_decay[TOK - 1 :]
    to_end = jnp.exp(last - log_decay) * step_ref[...]
    weighted = conved[:, :WIDTH] * dot_f32(to_end, head_spread())
    local = dot_f32(weighted.T, conved[:, WIDTH : WIDTH + NS])
    state_ref[...] = jnp.zeros_like(state_ref)
    for head in range(HEADS):
        state_ref[:, head, :] = local[head * P_SIZE : (head + 1) * P_SIZE]
    state_ref[:, HEADS, :] = jnp.broadcast_to(jnp.exp(last), (P_SIZE, NS))


def states_kernel(reverse, decay_ref, local_ref, out_ref):
    decays = decay_ref[:, HEADS, :].T[:SLOTS]
    state = jnp.zeros((SLOTS, NS), F32)
    for position in range(SPANS):
        span = SPANS - 1 - position if reverse else position
        out_ref[span] = state
        if position < SPANS - 1:
            state = decays[:, span : span + 1] * state + local_ref[span]


def states_between(decays, local, reverse):
    return kernel_call(
        functools.partial(states_kernel, reverse), [((SPANS, SLOTS, NS), F32, FAR)], decays, local,
        vmem=16, name="states",
    )[0]


def head_decay(log_decay, log_rows, head):
    apart = jnp.minimum(log_decay[:, head : head + 1] - log_rows[head : head + 1], 0.0)
    return jnp.where(causal_mask(), jnp.exp(apart), 0.0)


def stacked_states(state_ref):
    return jnp.concatenate([state_ref[:, head, :] for head in range(HEADS)], axis=0)


def first_of_pair(shape):
    return lanes_of(shape) < P_SIZE


def ssm_out_kernel(
    conv_ref, step_ref, log_ref, state_ref, gate_ref, skip_ref, gated_ref, y_ref
):
    conved = conv_ref[...]
    in_vectors = conved[:, WIDTH : WIDTH + NS]
    out_vectors = conved[:, WIDTH + NS :]
    log_decay = log_ref[...]
    log_rows = log_decay.T
    step_rows = step_ref[...].T
    spread = head_spread()
    both = dot_f32(out_vectors, in_vectors, 1, 1)
    carried = dot_f32(out_vectors, stacked_states(state_ref), 1, 1)
    skip = dot_f32(jnp.broadcast_to(skip_ref[...], (8, NS)), spread)[:1]
    outer = dot_f32(jnp.exp(log_decay), spread) * carried + skip * conved[:, :WIDTH]
    for pair in range(HEADS // 2):
        lanes = slice(pair * 2 * P_SIZE, (pair + 1) * 2 * P_SIZE)
        inputs = conved[:, lanes]
        parts = []
        for head in (2 * pair, 2 * pair + 1):
            mixing = both * head_decay(log_decay, log_rows, head) * step_rows[head : head + 1]
            parts.append(dot_f32(mixing, inputs))
        y = outer[:, lanes] + jnp.where(first_of_pair(inputs.shape), parts[0], parts[1])
        gate = gate_ref[:, lanes]
        y_ref[:, lanes] = y
        gated_ref[:, lanes] = (y * gate * sigmoid(gate)).astype(BF16)


def mixer_out_kernel(gated_ref, attended_ref, own_ref, other_ref, order_ref, out_ref):
    mixed = jnp.concatenate([gated_ref[...], attended_ref[...]], axis=1)
    wide = mixed.shape[1]
    parts = [dot_low(mixed, ref[:, :wide], 1, 1).astype(BF16) for ref in (own_ref, other_ref)]
    out_ref[...] = dot_low(jnp.concatenate(parts, axis=1), order_ref[...], 1, 1).astype(BF16)


def ffn_kernel(
    tokens_ref, mixed_ref, theirs_ref, gain_ref, grad_inner_ref, order_a_ref,
    gate_up_own_ref, gate_up_other_ref,
    hidden_ref, turned_ref, inner_ref, grad_ref, second_ref,
):
    half = MODEL_WIDTH // 2
    hidden = tokens_ref[...].astype(F32) + (mixed_ref[...].astype(F32) + theirs_ref[...].astype(F32))
    hidden_ref[...] = hidden
    scale = lax.rsqrt(jnp.mean(hidden * hidden, axis=1, keepdims=True) + EPS)
    normed = (hidden * scale * gain_ref[...]).astype(BF16)
    turned = dot_low(normed, order_a_ref[...]).astype(BF16)
    turned_ref[...] = turned
    ff = gate_up_own_ref.shape[1] // 2
    gate = dot_low(turned[:, :half], gate_up_own_ref[:, :ff]) + dot_low(
        turned[:, half:], gate_up_other_ref[:, :ff]
    )
    up = dot_low(turned[:, :half], gate_up_own_ref[:, ff:]) + dot_low(
        turned[:, half:], gate_up_other_ref[:, ff:]
    )
    grad_inner = grad_inner_ref[...]
    opened = sigmoid(gate)
    silu = gate * opened
    inner_ref[...] = (silu * up).astype(BF16)
    grad_gate = (grad_inner * up * (opened * (1.0 + gate * (1.0 - opened)))).astype(BF16)
    grads = jnp.concatenate([grad_gate, (grad_inner * silu).astype(BF16)], axis=1)
    grad_ref[...] = grads
    parts = [dot_low(grads, ref[...], 1, 1).astype(BF16) for ref in (gate_up_own_ref, gate_up_other_ref)]
    second_ref[...] = dot_low(jnp.concatenate(parts, axis=1), order_a_ref[...], 1, 1).astype(BF16)


def down_back_kernel(cot_ref, own_ref, other_ref, out_ref):
    ff = own_ref.shape[1] // 2
    half = MODEL_WIDTH // 2
    out_ref[...] = dot_low(cot_ref[:, :half], own_ref[:, ff:]) + dot_low(
        cot_ref[:, half:], other_ref[:, ff:]
    )


def ffn_out_kernel(inner_ref, own_ref, other_ref, order_ref, out_ref):
    ff = inner_ref.shape[1]
    inner = inner_ref[...]
    parts = [dot_low(inner, ref[:, ff:], 1, 1).astype(BF16) for ref in (own_ref, other_ref)]
    out_ref[...] = dot_low(jnp.concatenate(parts, axis=1), order_ref[...], 1, 1).astype(BF16)


def norm_back(values, gain, grad):
    scale = lax.rsqrt(jnp.mean(values * values, axis=1, keepdims=True) + EPS)
    weighted = grad * gain
    along = jnp.mean(weighted * values, axis=1, keepdims=True)
    return (scale, weighted * scale - values * (scale * scale * scale * along))


def mixer_back_kernel(
    hidden_ref, second_ref, theirs_ref, gain_ref, cot_ref, order_ref, own_ref, other_ref,
    gate_ref, y_ref, conv_ref, log_ref,
    grad_hidden_ref, turned_ref, grad_gain_ref, grad_attended_ref, grad_y_ref, grad_gate_ref,
    state_ref,
):
    half = MODEL_WIDTH // 2
    hidden = hidden_ref[...]
    mine = second_ref[...].astype(F32)
    scale, back = norm_back(hidden, gain_ref[...], mine + theirs_ref[...].astype(F32))
    grad_gain_ref[...] = jnp.sum(mine * hidden * scale, axis=0, keepdims=True)
    grad_hidden = cot_ref[...].astype(F32) + back
    grad_hidden_ref[...] = grad_hidden
    turned = dot_low(grad_hidden.astype(BF16), order_ref[...]).astype(BF16)
    turned_ref[...] = turned
    wide = WIDTH + QUERY_WIDTH
    grads = dot_low(turned[:, :half], own_ref[:, :wide]) + dot_low(turned[:, half:], other_ref[:, :wide])
    grad_attended_ref[...] = grads[:, WIDTH:].astype(BF16)
    grad_gated = grads[:, :WIDTH]
    gate = gate_ref[...]
    opened = sigmoid(gate)
    grad_y = grad_gated * gate * opened
    grad_y_ref[...] = grad_y
    grad_gate_ref[...] = (grad_gated * y_ref[...] * (opened * (1.0 + gate * (1.0 - opened)))).astype(BF16)
    weighted = grad_y * dot_f32(jnp.exp(log_ref[...]), head_spread())
    local = dot_f32(weighted.T, conv_ref[:, WIDTH + NS :])
    state_ref[...] = jnp.zeros_like(state_ref)
    for head in range(HEADS):
        state_ref[:, head, :] = local[head * P_SIZE : (head + 1) * P_SIZE]


def ffn_grads_kernel(
    normed_ref, grad_ff_ref, cot_ref, inner_ref, a_keep_ref, a_send_ref, b_keep_ref, b_send_ref
):
    half = MODEL_WIDTH // 2
    for part, (a_ref, b_ref) in enumerate(((a_keep_ref, b_keep_ref), (a_send_ref, b_send_ref))):
        lanes = slice(part * half, (part + 1) * half)
        a_ref[...] = dot_low(normed_ref[:, lanes], grad_ff_ref[...], 0, 0).astype(BF16)
        b_ref[...] = dot_low(cot_ref[:, lanes], inner_ref[...], 0, 0).astype(BF16)


def mixer_grads_kernel(
    normed_ref, grad_gate_ref, grad_mixed_ref, gated_ref, attended_ref,
    a_keep_ref, a_send_ref, b_keep_ref, b_send_ref,
):
    half = MODEL_WIDTH // 2
    for part, (a_ref, b_ref) in enumerate(((a_keep_ref, b_keep_ref), (a_send_ref, b_send_ref))):
        lanes = slice(part * half, (part + 1) * half)
        a_ref[...] = dot_low(normed_ref[HALO:, lanes], grad_gate_ref[...], 0, 0).astype(BF16)
        mixed = grad_mixed_ref[:, lanes]
        b_ref[:, :WIDTH] = dot_low(mixed, gated_ref[...], 0, 0).astype(BF16)
        b_ref[:, WIDTH:] = dot_low(mixed, attended_ref[...], 0, 0).astype(BF16)


def ssm_back_kernel(
    grad_y_ref, conv_ref, step_ref, log_ref, dt_ref, state_ref, grad_state_ref, ext_ref,
    conv_weight_ref, conv_bias_ref, decay_ref, skip_ref,
    grad_ext_ref, grad_dt_ref, small_ref, row_ref, pad_ref, grad_conv_ref,
):
    conved = conv_ref[...]
    grad_y = grad_y_ref[...]
    in_vectors = conved[:, WIDTH : WIDTH + NS]
    out_vectors = conved[:, WIDTH + NS :]
    step = step_ref[...]
    step_rows = step.T
    log_decay = log_ref[...]
    log_rows = log_decay.T
    last = log_decay[TOK - 1 :]
    spread = head_spread()
    states = stacked_states(state_ref)
    grad_states = stacked_states(grad_state_ref)
    now = jnp.exp(log_decay)
    leave = jnp.exp(last - log_decay)
    to_end = leave * step
    both = dot_f32(out_vectors, in_vectors, 1, 1)
    carried = dot_f32(out_vectors, states, 1, 1)
    pushed = dot_f32(in_vectors, grad_states, 1, 1)
    now_wide = dot_f32(now, spread)
    to_end_wide = dot_f32(to_end, spread)
    skip_wide = dot_f32(jnp.broadcast_to(skip_ref[...], (8, NS)), spread)[:1]
    inputs = conved[:, :WIDTH]
    grad_out = dot_f32(grad_y * now_wide, states)
    grad_in = dot_f32(inputs * to_end_wide, grad_states)
    outer = grad_y * skip_wide + to_end_wide * pushed
    grad_log = dot_f32(grad_y * carried * now_wide, spread, 1, 1)
    grad_to_end = dot_f32(inputs * pushed, spread, 1, 1)
    skip_sum = dot_f32(grad_y * inputs, spread, 1, 1)
    grad_step = grad_to_end * leave
    into_end = grad_to_end * to_end
    grad_log = grad_log - into_end
    stays = jnp.sum((states * grad_states).reshape(HEADS, P_SIZE, NS), axis=1)
    stays = jnp.concatenate([stays, jnp.zeros((NS - HEADS, NS), F32)], axis=0)
    stays = jnp.sum(stays.T, axis=0, keepdims=True)
    grad_last = jnp.sum(into_end, axis=0, keepdims=True) + jnp.exp(last) * stays
    grad_both = jnp.zeros((TOK, TOK), F32)
    row_ref[...] = jnp.zeros_like(row_ref)
    for pair in range(HEADS // 2):
        lanes = slice(pair * 2 * P_SIZE, (pair + 1) * 2 * P_SIZE)
        pair_inputs = conved[:, lanes]
        pair_grads = grad_y[:, lanes]
        first = first_of_pair(pair_inputs.shape)
        parts = []
        for side, head in enumerate((2 * pair, 2 * pair + 1)):
            decay = head_decay(log_decay, log_rows, head)
            step_row = step_rows[head : head + 1]
            mine = jnp.where(first if side == 0 else jnp.logical_not(first), pair_grads, 0.0)
            grad_mixing = dot_f32(mine, pair_inputs, 1, 1) * decay
            grad_both = grad_both + grad_mixing * step_row
            apart = grad_mixing * both
            row_ref[head : head + 1, :] = jnp.sum(apart, axis=0, keepdims=True)
            along = jnp.sum(apart * step_row, axis=1, keepdims=True)
            grad_log = grad_log + jnp.where(lanes_of((TOK, NS)) == head, along, 0.0)
            mixing = both * decay * step_row
            parts.append(dot_f32(mixing.T, pair_grads))
        grad_conv_ref[:, lanes] = outer[:, lanes] + jnp.where(first, parts[0], parts[1])
    rows = row_ref[...].T
    grad_step = grad_step + rows
    grad_log = grad_log - rows * step
    grad_log = grad_log + jnp.where(rows_of((TOK, NS)) == TOK - 1, grad_last, 0.0)
    grad_rate = dot_f32((rows_of((TOK, TOK)) <= lanes_of((TOK, TOK))).astype(F32), grad_log)
    grad_step = grad_step - grad_rate * decay_ref[...]
    grad_dt = grad_step * sigmoid(dt_ref[...])
    grad_dt_ref[...] = jnp.where(lanes_of((TOK, NS)) < HEADS, grad_dt, 0.0).astype(BF16)
    grad_conv_ref[:, WIDTH : WIDTH + NS] = grad_in + dot_f32(grad_both.T, out_vectors)
    grad_conv_ref[:, WIDTH + NS :] = grad_out + dot_f32(grad_both, in_vectors)
    summed = convolved(ext_ref, conv_weight_ref[...], conv_bias_ref[...])
    opened = sigmoid(summed)
    grad_summed = grad_conv_ref[...] * (opened * (1.0 + summed * (1.0 - opened)))
    pad_ref[...] = jnp.zeros_like(pad_ref)
    pad_ref[pl.ds(HALO, TOK), :] = grad_summed
    conv_weight = conv_weight_ref[...]
    total = 0.0
    for lag in range(CONV_K):
        total = total + conv_weight[lag : lag + 1] * pad_ref[pl.ds(CONV_K - 1 - lag, HALO + TOK), :]
        small_ref[lag : lag + 1, :] = jnp.sum(
            grad_summed * ext_ref[pl.ds(HALO - CONV_K + 1 + lag, TOK), :], axis=0, keepdims=True
        )
    grad_ext_ref[...] = total.astype(BF16)
    small_ref[CONV_K : CONV_K + 1, :] = jnp.sum(grad_summed, axis=0, keepdims=True)
    small_ref[CONV_K + 1 : CONV_K + 3, :] = jnp.zeros((2, MODEL_WIDTH), F32)
    heads_row = jnp.concatenate(
        [
            jnp.sum(grad_dt, axis=0, keepdims=True),
            -jnp.sum(grad_rate * step, axis=0, keepdims=True),
            jnp.sum(skip_sum, axis=0, keepdims=True),
            jnp.zeros((1, MODEL_WIDTH - 3 * NS), F32),
        ],
        axis=1,
    )
    small_ref[CONV_K + 3 : CONV_K + 4, :] = heads_row


def project_a_kernel(
    low_ref, grad_gate_ref, a_own_ref, a_other_ref, b_own_ref, b_other_ref, order_a_ref, order_b_ref, out_ref
):
    parts = [dot_low(low_ref[...], ref[...], 1, 1).astype(BF16) for ref in (a_own_ref, a_other_ref)]
    from_a = dot_low(jnp.concatenate(parts, axis=1), order_a_ref[...], 1, 1)
    gate = grad_gate_ref[...]
    parts = [dot_low(gate, ref[:, :WIDTH], 1, 1).astype(BF16) for ref in (b_own_ref, b_other_ref)]
    out_ref[...] = from_a + dot_low(jnp.concatenate(parts, axis=1), order_b_ref[...], 1, 1)


def project_b_kernel(
    low_ref, from_ref, own_ref, other_ref, order_ref, tokens_ref, first_ref, grad_gain_ref
):
    parts = [dot_low(low_ref[...], ref[:, WIDTH:], 1, 1).astype(BF16) for ref in (own_ref, other_ref)]
    first = from_ref[...] + dot_low(jnp.concatenate(parts, axis=1), order_ref[...], 1, 1)
    first = first.astype(BF16)
    first_ref[...] = first
    tokens = tokens_ref[...].astype(F32)
    scale = lax.rsqrt(jnp.mean(tokens * tokens, axis=1, keepdims=True) + EPS)
    grad_gain_ref[...] = jnp.sum(first.astype(F32) * tokens * scale, axis=0, keepdims=True)


def join_kernel(counts, *refs):
    pieces = list(refs[: sum(counts)])
    for count, out_ref in zip(counts, refs[sum(counts) :]):
        at = 0
        for ref in pieces[:count]:
            out_ref[at : at + ref.shape[0], :] = ref[...]
            at += ref.shape[0]
        pieces = pieces[count:]


def join_rings(*groups, vmem=12, far=False):
    outs = [((sum(piece.shape[0] for piece in group), group[0].shape[1]), BF16) for group in groups]
    pieces = [piece for group in groups for piece in group]
    if far:
        pieces = [far_away(piece) for piece in pieces]
    counts = tuple(len(group) for group in groups)
    return kernel_call(functools.partial(join_kernel, counts), outs, *pieces, vmem=vmem, name="join_rings")


def pass_on_kernel(*refs):
    for ahead, behind, from_behind, from_ahead, ahead_out, behind_out in zip(*[iter(refs)] * 6):
        half = from_ahead.shape[0]
        ahead_out[:half, :] = (ahead[:half, :].astype(F32) + from_behind[...].astype(F32)).astype(BF16)
        ahead_out[half:, :] = ahead[half:, :]
        behind_out[:half, :] = behind[:half, :]
        behind_out[half:, :] = (behind[half:, :].astype(F32) + from_ahead[...].astype(F32)).astype(BF16)


def halve_kernel(*refs):
    groups = (len(refs) - 5) // 2
    rows = refs[0].shape[0] // 4
    outs = refs[2 * groups :]
    starts = ((0, rows), (rows, rows), (3 * rows, rows), (2 * rows, rows // 2), (2 * rows + rows // 2, rows // 2))
    at = 0
    for group in range(groups):
        keep_ref, arrived_ref = refs[2 * group : 2 * group + 2]
        lanes = slice(at, at + keep_ref.shape[1])
        at += keep_ref.shape[1]
        for (start, size), out_ref in zip(starts, outs):
            part = slice(start, start + size)
            total = keep_ref[part, :].astype(F32) + arrived_ref[part, :].astype(F32)
            out_ref[:, lanes] = total.astype(out_ref.dtype)


def halve(*parts, vmem=16, far=False):
    rows = parts[0].shape[0] // 4
    width = sum(part.shape[1] for part in parts[::2])
    sizes = ((rows, F32), (rows, BF16), (rows, BF16), (rows // 2, BF16), (rows // 2, BF16))
    return kernel_call(
        halve_kernel, [((size, width), dtype) + ((FAR,) if far else ()) for size, dtype in sizes], *parts,
        far=range(len(parts)) if far else (), vmem=vmem, us=2,
        name="halve",
    )


def pass_on(*groups, vmem=16):
    def body(*refs):
        count = 4 * len(groups)
        ins, outs = (refs[:count], refs[count:])
        mixed = []
        for group in range(len(groups)):
            mixed += ins[4 * group : 4 * group + 4] + outs[2 * group : 2 * group + 2]
        pass_on_kernel(*mixed)

    outs = [(piece.shape, BF16) for group in groups for piece in group[:2]]
    pieces = [piece for group in groups for piece in group]
    return kernel_call(body, outs, *pieces, vmem=vmem, name="pass_on")


def two_halves(values):
    high = values.astype(BF16)
    return (high, (values - high.astype(F32)).astype(BF16))


def of_halves(high, low):
    return high.astype(F32) + low.astype(F32)


def late_b_kernel(normed_ref, low_ref, small_ref, keep_ref, send_ref, sent_ref):
    half = MODEL_WIDTH // 2
    low = low_ref[...]
    keep_ref[...] = dot_low(normed_ref[:, :half], low, 0, 0).astype(BF16)
    send_ref[:half, :] = dot_low(normed_ref[:, half:], low, 0, 0).astype(BF16)
    small = small_ref[...]
    high, rest = two_halves(jnp.concatenate([small[:, :half], small[:, half:]], axis=0))
    send_ref[half:, :] = jnp.concatenate([high, rest], axis=0)
    sent_ref[...] = of_halves(high, rest)


def late_b_ring_kernel(keep_ref, arrived_ref, small_ref, first_ref, *rest_refs):
    rows = TOK
    total = keep_ref[...].astype(F32) + arrived_ref[: 4 * rows, :].astype(F32)
    lines = small_ref.shape[0]
    small = small_ref[...] + of_halves(
        arrived_ref[4 * rows : 4 * rows + lines, :], arrived_ref[4 * rows + lines :, :]
    )
    high, rest = two_halves(small)
    first_ref[...] = total[:rows]
    tail = jnp.concatenate([high, rest], axis=0)
    for step in (1, 2, 3):
        rest_refs[step - 1][:rows, :] = total[step * rows : (step + 1) * rows].astype(BF16)
        rest_refs[step - 1][rows:, :] = tail
    rest_refs[3][...] = of_halves(high, rest)


def ring_total(refs, rows):
    return refs[0][...] + sum(ref[:rows, :].astype(F32) for ref in refs[1:])


def merge_a_kernel(*refs):
    early, late, (keep_ref, *send_refs) = (refs[:3], refs[3:6], refs[6:])
    total = jnp.concatenate([ring_total(early, TOK), ring_total(late, TOK)], axis=1)
    rows = TOK // 4
    keep_ref[...] = total[:rows]
    for step in (1, 2, 3):
        send_refs[step - 1][...] = total[step * rows : (step + 1) * rows].astype(BF16)


def ring_small(small_ref, pieces):
    first, second, third = pieces
    return (small_ref[...] + second) + (first + third)


def merge_b_kernel(*refs):
    early, late, small_ref = (refs[:3], refs[3:7], refs[7])
    keep_ref, *send_refs, sent_ref = refs[8:]
    total = jnp.concatenate([ring_total(early, TOK), ring_total(late, TOK)], axis=1)
    lines = small_ref.shape[0]
    small = ring_small(
        small_ref, [of_halves(ref[TOK : TOK + lines, :], ref[TOK + lines :, :]) for ref in late[1:]]
    )
    high, rest = two_halves(small)
    tail = jnp.concatenate([high, rest], axis=0)
    rows = TOK // 4
    keep_ref[...] = total[:rows]
    width = total.shape[1]
    for step in (1, 2, 3):
        send_refs[step - 1][:, :width] = total[step * rows : (step + 1) * rows].astype(BF16)
        send_refs[step - 1][:, width:] = tail
    sent_ref[...] = of_halves(high, rest)


def last_ring_kernel(*refs):
    a_refs, b_refs, small_ref = (refs[:4], refs[4:8], refs[8])
    keep_ref, away_ref, sent_ref, pair_ref, cross_ref = refs[9:]
    rows = TOK // 4
    width = b_refs[0].shape[1]
    lines = small_ref.shape[0]
    total_b = b_refs[0][...] + (
        b_refs[1][:, :width].astype(F32) + b_refs[2][:, :width].astype(F32) + b_refs[3][:, :width].astype(F32)
    )
    total = jnp.concatenate([ring_total(a_refs, rows), total_b], axis=1)
    small = ring_small(
        small_ref, [of_halves(ref[:lines, width:], ref[lines:, width:]) for ref in b_refs[1:]]
    )
    high, rest = two_halves(small)
    keep_ref[...] = total[: rows // 2]
    away_ref[:, : total.shape[1]] = total[rows // 2 :].astype(BF16)
    away_ref[:, total.shape[1] :] = jnp.concatenate([high, rest], axis=1)
    small = of_halves(high, rest)
    sent_ref[...] = small
    stop = a_refs[0].shape[1]
    shared = total[:, stop - 2 * NS : stop]
    pair_ref[...] = jnp.concatenate([shared[: rows // 2], small], axis=1)
    shared = shared[rows // 2 :].astype(BF16).astype(F32)
    cross_ref[...] = jnp.concatenate([shared, small], axis=1)


def in_grads_kernel(normed_ref, low_ref, keep_ref, send_ref):
    half = MODEL_WIDTH // 2
    low = low_ref[...]
    keep_ref[...] = dot_low(normed_ref[:, :half], low, 0, 0).astype(BF16)
    send_ref[...] = dot_low(normed_ref[:, half:], low, 0, 0).astype(BF16)


def finish_grads_kernel(keep_ref, theirs_ref, small_ref, pair_ref, cross_ref, *refs):
    out_refs, small_refs = (refs[:-8], refs[-8:])
    others = pair_ref[...] + cross_ref[...]
    at = 0
    for number, ref in enumerate(out_refs):
        lanes = slice(at, at + ref.shape[1])
        total = keep_ref[:, lanes] + theirs_ref[:, lanes].astype(F32)
        ref[...] = total + others[:, : 2 * NS] if number == SHARED else total
        at += ref.shape[1]
    at = keep_ref.shape[1]
    width = small_ref.shape[1]
    own = small_ref[...] + of_halves(theirs_ref[:, at : at + width], theirs_ref[:, at + width :])
    both = own + others[:, 2 * NS :]
    lines = 2 * CONV_K
    own = jnp.concatenate([own[:lines], own[lines:]], axis=1)
    both = jnp.concatenate([both[:lines], both[lines:]], axis=1)
    conv_x_ref, conv_xb_ref, conv_bc_ref, conv_bcb_ref, first_ref, second_ref, heads_ref, rest_ref = small_refs
    conv_x_ref[...] = own[:CONV_K, :WIDTH]
    conv_xb_ref[...] = own[CONV_K, :WIDTH]
    conv_bc_ref[...] = both[:CONV_K, WIDTH:]
    conv_bcb_ref[...] = both[CONV_K, WIDTH:]
    first_ref[...] = both[CONV_K + 1]
    second_ref[...] = both[CONV_K + 2]
    heads_ref[...] = own[CONV_K + 3 :, : 3 * NS]
    rest_ref[...] = own[:, :NS]


def low_b_kernel(query_ref, kv_ref, dt_ref, cosine_ref, sine_ref, out_ref):
    grads = jnp.concatenate([query_ref[...], kv_ref[...]], axis=1)
    out_ref[:, :ROPED] = turn(grads, cosine_ref[...], -sine_ref[...]).astype(BF16)
    out_ref[:, ROPED:] = dt_ref[...]


def slot_of(pair, index):
    y, x, z = (index >> 5, (index >> 3) & 3, (index >> 1) & 3)
    dy = ((pair >> 4) - y) & 1
    dx = ((pair >> 2) - x) & 3
    dz = (pair - z) & 3
    return pl.multiple_of(((dx * 4 + dz) * 2 + dy) * TOK, TOK)


def load_quad(quad, index, own_ref, other_ref):
    parts = []
    for side in (0, 1):
        slot = slot_of(quad * 2 + side, index)
        parts += [own_ref[pl.ds(slot, TOK), :], other_ref[pl.ds(slot, TOK), :]]
    return jnp.concatenate(parts, axis=0)


def head_columns(rows):
    turned = rows.T
    heads = rows.shape[1] // HEAD_SIZE
    return jnp.concatenate(
        [turned[head * HEAD_SIZE : (head + 1) * HEAD_SIZE] for head in range(heads)], axis=1
    )


def head_rows(rows):
    heads = rows.shape[1] // HEAD_SIZE
    return jnp.concatenate(
        [rows[:, head * HEAD_SIZE : (head + 1) * HEAD_SIZE] for head in range(heads)], axis=0
    )


def rows_of_columns(columns):
    heads = columns.shape[1] // TOK
    stacked = jnp.concatenate(
        [columns[:, head * TOK : (head + 1) * TOK] for head in range(heads)], axis=0
    )
    return stacked.T


def quad_mask(shape, quad, index):
    row = rows_of(shape)
    block = quad * 4 + (row >> 8) * 2 + ((index & 1) ^ ((row >> 7) & 1))
    keys = block * TOK + (row & (TOK - 1))
    queries = index * TOK + (lanes_of(shape) & (TOK - 1))
    return keys <= queries


def attend_kernel(index_ref, query_ref, own_ref, other_ref, columns_ref, rows_ref, log_ref, total_ref, even_ref, odd_ref):
    index = index_ref[0]
    query = head_columns(query_ref[...].astype(F32) * HEAD_SIZE ** (-0.5))
    padded = jnp.concatenate([query, jnp.zeros_like(query)], axis=0).astype(BF16)
    total_ref[...] = jnp.zeros_like(total_ref)

    def scores_of(quad):
        quad_kv = load_quad(quad, index, own_ref, other_ref)
        return jnp.dot(quad_kv, padded, preferred_element_type=F32)

    def step(quad, carry, scores):
        peak, weight = carry
        quad_kv = load_quad(quad, index, own_ref, other_ref)
        new_peak = jnp.maximum(peak, jnp.max(scores, axis=0, keepdims=True))
        shrink = jnp.exp(peak - new_peak)
        probs = jnp.exp(scores - new_peak)
        weight = weight * shrink + jnp.sum(probs, axis=0, keepdims=True)
        total_ref[...] = total_ref[...] * shrink + dot_low(quad_kv, probs.astype(BF16), 0, 0)
        return (new_peak, weight)

    lanes = (1, query.shape[1])
    last = index >> 2
    even_ref[...] = scores_of(0)
    scores = scores_of(last)
    scores = jnp.where(quad_mask(scores.shape, last, index), scores, MASKED)
    carry = step(last, (jnp.full(lanes, MASKED, F32), jnp.zeros(lanes, F32)), scores)

    def two_steps(count, carry):
        quad = 2 * count
        odd_ref[...] = scores_of(quad + 1)
        carry = step(quad, carry, even_ref[...])
        even_ref[...] = scores_of(jnp.minimum(quad + 2, last))
        return step(quad + 1, carry, odd_ref[...])

    carry = lax.fori_loop(0, last >> 1, two_steps, carry)
    peak, weight = lax.fori_loop(
        0, last & 1, lambda count, carry: step(last - 1, carry, even_ref[...]), carry
    )
    columns = total_ref[HEAD_SIZE:, :] / weight
    columns_ref[...] = columns
    rows_ref[...] = rows_of_columns(columns).astype(BF16)
    log_ref[...] = peak + jnp.log(weight)


def attend(index, query_low, own_kv, other_kv):
    lanes = QUERY_WIDTH // HEAD_SIZE * TOK
    vmem = pl.BlockSpec(memory_space=pltpu.VMEM)
    return pl.pallas_call(
        attend_kernel,
        out_shape=(
            jax.ShapeDtypeStruct((HEAD_SIZE, lanes), F32),
            jax.ShapeDtypeStruct((TOK, QUERY_WIDTH), BF16),
            jax.ShapeDtypeStruct((1, lanes), F32),
        ),
        in_specs=[pl.BlockSpec(memory_space=pltpu.SMEM), vmem, vmem, vmem],
        out_specs=(vmem, vmem, vmem),
        scratch_shapes=[pltpu.VMEM((2 * HEAD_SIZE, lanes), F32)] + [pltpu.VMEM((4 * TOK, lanes), F32)] * 2,
        compiler_params=pltpu.CompilerParams(vmem_limit_bytes=24 * 2**20),
        cost_estimate=pl.CostEstimate(flops=13 * 10**9, bytes_accessed=0, transcendentals=0),
        name="attend",
    )(index, query_low, own_kv, other_kv)


def attend_back_kernel(
    index_ref, query_ref, grad_ref, columns_ref, log_ref, own_ref, other_ref,
    grad_query_ref, grad_own_ref, grad_other_ref, total_ref, even_ref, odd_ref,
):
    index = index_ref[0]
    scale = HEAD_SIZE ** (-0.5)
    query_rows = query_ref[...].astype(F32) * scale
    grad_rows = grad_ref[...].astype(F32)
    query = head_columns(query_rows)
    grad = head_columns(grad_rows)
    blank = jnp.zeros_like(query)
    query_pad = jnp.concatenate([query, blank], axis=0).astype(BF16)
    grad_pad = jnp.concatenate([blank, grad], axis=0).astype(BF16)
    query_tall = head_rows(query_rows)
    grad_tall = head_rows(grad_rows)
    blank = jnp.zeros_like(query_tall)
    sides = jnp.concatenate(
        [
            jnp.concatenate([query_tall, blank], axis=1),
            jnp.concatenate([blank, grad_tall], axis=1),
        ],
        axis=0,
    ).astype(BF16)
    delta = jnp.sum(grad * columns_ref[...], axis=0, keepdims=True)
    log_total = log_ref[...]
    total_ref[...] = jnp.zeros_like(total_ref)
    grad_own_ref[...] = jnp.zeros_like(grad_own_ref)
    grad_other_ref[...] = jnp.zeros_like(grad_other_ref)

    def products_of(quad):
        quad_kv = load_quad(quad, index, own_ref, other_ref)
        return (
            jnp.dot(quad_kv, query_pad, preferred_element_type=F32),
            jnp.dot(quad_kv, grad_pad, preferred_element_type=F32),
        )

    def step(quad, scores, grad_probs, masked):
        quad_kv = load_quad(quad, index, own_ref, other_ref)
        probs = jnp.exp(scores - log_total)
        if masked:
            probs = jnp.where(quad_mask(scores.shape, quad, index), probs, 0.0)
        grad_scores = (probs * (grad_probs - delta)).astype(BF16)
        total_ref[...] += dot_low(quad_kv, grad_scores, 0, 0)
        both = jnp.concatenate([grad_scores, probs.astype(BF16)], axis=1)
        term = jnp.dot(both, sides, preferred_element_type=F32).astype(BF16)
        for side in (0, 1):
            slot = slot_of(quad * 2 + side, index)
            at = side * 2 * TOK
            grad_own_ref[pl.ds(slot, TOK), :] = term[at : at + TOK]
            grad_other_ref[pl.ds(slot, TOK), :] = term[at + TOK : at + 2 * TOK]

    last = index >> 2
    even_ref[0], even_ref[1] = products_of(0)
    step(last, *products_of(last), True)

    def two_steps(count, carry):
        quad = 2 * count
        odd_ref[0], odd_ref[1] = products_of(quad + 1)
        step(quad, even_ref[0], even_ref[1], False)
        even_ref[0], even_ref[1] = products_of(jnp.minimum(quad + 2, last))
        step(quad + 1, odd_ref[0], odd_ref[1], False)
        return carry

    lax.fori_loop(0, last >> 1, two_steps, 0)

    def final_step(count, carry):
        step(last - 1, even_ref[0], even_ref[1], False)
        return carry

    lax.fori_loop(0, last & 1, final_step, 0)
    grad_query_ref[...] = rows_of_columns(total_ref[:HEAD_SIZE, :] * scale)


def attend_back(index, query_low, grad_low, columns, log_total, own_kv, other_kv):
    vmem = pl.BlockSpec(memory_space=pltpu.VMEM)
    return pl.pallas_call(
        attend_back_kernel,
        out_shape=(
            jax.ShapeDtypeStruct(query_low.shape, F32),
            jax.ShapeDtypeStruct(own_kv.shape, BF16),
            jax.ShapeDtypeStruct(other_kv.shape, BF16),
        ),
        in_specs=[pl.BlockSpec(memory_space=pltpu.SMEM)] + [vmem] * 6,
        out_specs=(vmem, vmem, vmem),
        scratch_shapes=[pltpu.VMEM((2 * HEAD_SIZE, columns.shape[1]), F32)]
        + [pltpu.VMEM((2, 4 * TOK, columns.shape[1]), F32)] * 2,
        compiler_params=pltpu.CompilerParams(vmem_limit_bytes=24 * 2**20),
        cost_estimate=pl.CostEstimate(flops=19 * 10**9, bytes_accessed=0, transcendentals=0),
        name="attend_back",
    )(index, query_low, grad_low, columns, log_total, own_kv, other_kv)


def shards(
    tokens,
    cotangent,
    gain_first,
    z_weight,
    x_weight,
    bc_weight,
    dt_weight,
    conv_x_weight,
    conv_x_bias,
    conv_bc_weight,
    conv_bc_bias,
    dt_bias,
    decay_rate,
    skip_weight,
    out_weight,
    q_weight,
    key_matrix,
    value_matrix,
    o_weight,
    gain_second,
    gate_weight,
    up_weight,
    down_weight,
):
    index = lax.axis_index(SEQ)
    index_word = jnp.reshape(index, (1,)).astype(jnp.int32)
    ff = gate_weight.shape[1]
    in_a_width = WIDTH + 2 * NS
    in_b_width = WIDTH + ROPED + NS

    def padded_heads(values):
        return jnp.pad(values, (0, NS - HEADS))[None, :]

    together = lax.optimization_barrier
    together = lax.optimization_barrier
    with jax.named_scope("gather_near"):
        dt_wide = jnp.pad(dt_weight, ((0, 0), (0, NS - HEADS)))
        near_a = jnp.concatenate([x_weight, bc_weight, gate_weight, up_weight], axis=1)
        near_b = jnp.concatenate(
            [z_weight, q_weight, key_matrix, value_matrix, dt_wide, out_weight, o_weight, down_weight],
            axis=1,
        )
        split = near_a.shape[1]
        theirs = send(jnp.concatenate([near_a, near_b], axis=1), OTHER_Y)
        near_a = fetch(joined([near_a, theirs[:, :split]]), along_x)
        near_b = fetch(joined([near_b, theirs[:, split:]]), along_z)
        near_a, near_b = join_rings(near_a, near_b, vmem=8)
    with jax.named_scope("orders"):
        halo = send(tokens[TOK - (CONV_K - 1) :], ONWARD)
        ahead = jnp.zeros((HALO - (CONV_K - 1), MODEL_WIDTH), BF16)
        tokens_ext = jnp.concatenate([ahead, halo, tokens], axis=0)
        to_a, to_b = one_hot_orders(index)
        normed = rms_norm(tokens_ext.astype(F32), gain_first).astype(BF16)
        normed_a = project(normed, to_a).astype(BF16)
        normed_b = project(normed[HALO:], to_b).astype(BF16)
        cot_b = project(cotangent, to_b).astype(BF16)
        cosine, sine = rotary_tables(index)
        conv_weight = jnp.concatenate([conv_x_weight, conv_bc_weight], axis=1)
        conv_bias = jnp.concatenate([conv_x_bias, conv_bc_bias], axis=0)[None, :]
        decay_wide = padded_heads(decay_rate)
        skip_wide = padded_heads(skip_weight)
        dt_bias_wide = padded_heads(dt_bias)
    with jax.named_scope("gather_in"):
        in_a, rest_a = (near_a[:, :in_a_width], near_a[:, in_a_width:])
        in_b, rest_b = (near_b[:, :in_b_width], near_b[:, in_b_width:])
        (in_a, in_b), (normed_a, normed_b, to_a, to_b) = together(
            ((ring_near(in_a, along_z), ring_near(in_b, along_x)), (normed_a, normed_b, to_a, to_b))
        )
        in_a, in_b = (ring_far(in_a, along_z), ring_far(in_b, along_x))
        (in_a, in_b), (cot_b, cosine, sine) = together(((in_a, in_b), (cot_b, cosine, sine)))
        in_a_own, in_b_own = join_rings(in_a, in_b)
        in_b_other = send(in_b_own, OTHER_CORE)
        in_a_other = send(in_a_own, OTHER_CORE)
    with jax.named_scope("attention_in"):
        gate_raw, query_low, kv_low, dt_pre, step_size, log_decay = kernel_call(
            attention_in_kernel,
            [((TOK, WIDTH), F32, FAR), ((TOK, QUERY_WIDTH), BF16), ((TOK, 2 * HEAD_SIZE), BF16)]
            + [((TOK, NS), F32)] * 3,
            normed_b, in_b_own, in_b_other, cosine, sine, dt_bias_wide, decay_wide,
            name="attention_in",
        )
    with jax.named_scope("gather_kv"):
        own_kv = joined([kv_low, send(kv_low, OTHER_Y)])
    with jax.named_scope("gather_rest"):
        rest_a, rest_b = after((rest_a, rest_b), in_a_own, in_b_own)
        rest_a = ring_near(rest_a, along_z)
        rest_b = ring_near(after(rest_b, kv_low), along_x)
        normed_a_early, rest_a = together((normed_a, rest_a))
    with jax.named_scope("ssm_in"):
        ext, conved, payload = kernel_call(
            ssm_in_kernel,
            [((HALO + TOK, MODEL_WIDTH), F32, FAR), ((TOK, MODEL_WIDTH), F32, FAR),
             ((P_SIZE, SLOTS, NS), F32, FAR)],
            normed_a_early, in_a_own, in_a_other, conv_weight, conv_bias, step_size, log_decay,
            us=3, name="ssm_in",
        )
    with jax.named_scope("state_forward"):
        payload, rest_a, rest_b, own_kv = together((payload, rest_a, rest_b, own_kv))
        spans = swap_spans(payload)
        own_kv = fetch(own_kv, along_z)
        rest_b = ring_far(rest_b, along_x)
        spans, own_kv, rest_a, rest_b = together((spans, own_kv, rest_a, rest_b))
        entering = states_between(spans, spans, False)
        own_kv = fetch(join_rings(own_kv, vmem=4, far=True)[0], along_x)
        rest_a = ring_far(rest_a, along_z)
        entering, own_kv, rest_a, rest_b = together((entering, own_kv, rest_a, rest_b))
        own_kv = join_rings(own_kv, vmem=4)[0]
        other_kv = send(own_kv, OTHER_CORE)
        state_in = swap_spans(entering)
        state_in, own_kv, other_kv, rest_a, rest_b = together((state_in, own_kv, other_kv, rest_a, rest_b))
    with jax.named_scope("gather_rest"):
        rest_a_own, rest_b_own = join_rings(rest_a, rest_b, far=True)
        rest_b_other = send(rest_b_own, OTHER_CORE)
        rest_a_other = send(rest_a_own, OTHER_CORE)
    with jax.named_scope("attention"):
        attended_columns, attended_low, log_total = attend(index_word, query_low, own_kv, other_kv)
    with jax.named_scope("ssm_out"):
        gated_low, y = kernel_call(
            ssm_out_kernel, [((TOK, WIDTH), BF16), ((TOK, WIDTH), F32)],
            conved, step_size, log_decay, state_in, gate_raw, skip_wide,
            us=2, name="ssm_out",
        )
        gated_low, attended_low, rest_a_other, rest_b_other = together(
            (gated_low, attended_low, rest_a_other, rest_b_other)
        )
    with jax.named_scope("mixer_out"):
        mixed = kernel_call(
            mixer_out_kernel, [((TOK, MODEL_WIDTH), BF16)],
            gated_low, attended_low, rest_b_own, rest_b_other, to_b,
            us=2, name="mixer_out",
        )[0]
        mixed_theirs = swap_heads(mixed)
    with jax.named_scope("ffn"):
        grad_inner = kernel_call(
            down_back_kernel, [((TOK, ff), F32)], cot_b, rest_b_own, rest_b_other,
            vmem=12, us=2, name="down_back",
        )[0]
        mixed_theirs, grad_inner = together((mixed_theirs, grad_inner))
        hidden, normed_second, inner_low, grad_ff, second_part = kernel_call(
            ffn_kernel,
            [((TOK, MODEL_WIDTH), F32), ((TOK, MODEL_WIDTH), BF16), ((TOK, ff), BF16),
             ((TOK, 2 * ff), BF16), ((TOK, MODEL_WIDTH), BF16)],
            tokens, mixed, mixed_theirs, gain_second[None, :], grad_inner, to_a,
            rest_a_own, rest_a_other,
            vmem=20, us=5, name="ffn",
        )
        second_theirs = swap_heads(second_part)
        ffn_part = kernel_call(
            ffn_out_kernel, [((TOK, MODEL_WIDTH), BF16)], inner_low, rest_b_own, rest_b_other, to_b,
            vmem=16, us=2, name="ffn_out",
        )[0]
        half = (MODEL_WIDTH // 2,)
        a_keep, a_send, b_keep, b_send = kernel_call(
            ffn_grads_kernel, [(half + (2 * ff,), BF16)] * 2 + [(half + (ff,), BF16)] * 2,
            normed_second, grad_ff, cot_b, inner_low, vmem=16, us=2, name="ffn_grads",
        )
        ffn_keep = (a_keep, b_keep)
        ffn_arrived = (send(a_send, OTHER_CORE), send(b_send, OTHER_CORE))
        second_theirs, ffn_part = together((second_theirs, ffn_part))
    with jax.named_scope("mixer_back"):
        (
            grad_hidden, grad_mixed_b, gain_second_part, grad_attended, grad_y, grad_gate_low, payload_back
        ) = kernel_call(
            mixer_back_kernel,
            [((TOK, MODEL_WIDTH), F32, FAR), ((TOK, MODEL_WIDTH), BF16, FAR), ((1, MODEL_WIDTH), F32),
             ((TOK, QUERY_WIDTH), BF16, FAR), ((TOK, WIDTH), F32, FAR), ((TOK, WIDTH), BF16, FAR),
             ((P_SIZE, SLOTS, NS), F32, FAR)],
            hidden, second_part, second_theirs, gain_second[None, :], cotangent, to_b,
            rest_b_own, rest_b_other, gate_raw, y, conved, log_decay,
            vmem=20, us=3, name="mixer_back",
        )
        ffn_theirs = swap_heads(ffn_part)
    with jax.named_scope("early_grads"):
        early_a, early_b = (2 * ff + WIDTH, ff + WIDTH + QUERY_WIDTH)
        a_keep, a_send, b_keep, b_send = kernel_call(
            mixer_grads_kernel,
            [(half + (WIDTH,), BF16, FAR)] * 2 + [(half + (WIDTH + QUERY_WIDTH,), BF16, FAR)] * 2,
            normed_a, grad_gate_low, grad_mixed_b, gated_low, attended_low, far=range(5), vmem=12, name="mixer_grads",
        )
    with jax.named_scope("state_backward"):
        arrived_back = swap_spans(payload_back)
        arrived_back, a_send, b_send, ffn_arrived = together((arrived_back, a_send, b_send, ffn_arrived))
        leaving = states_between(spans, arrived_back, True)
        a_arrived = send(a_send, OTHER_CORE)
        b_arrived = send(b_send, OTHER_CORE)
        state_grad = swap_spans(leaving)
    with jax.named_scope("early_grads"):
        a_keep, a_ahead, a_behind, a_first, a_second = halve(
            ffn_keep[0], ffn_arrived[0], a_keep, a_arrived, far=True
        )
        b_keep, b_ahead, b_behind, b_first, b_second = halve(
            ffn_keep[1], ffn_arrived[1], b_keep, b_arrived, far=True
        )
        state_grad, a_first, a_second, b_first, b_second = together(
            (state_grad, a_first, a_second, b_first, b_second)
        )
        a_passed = [send(a_first, along_z(1)), send(a_second, along_z(-1))]
        b_passed = [send(b_first, along_x(1)), send(b_second, along_x(-1))]
    with jax.named_scope("ssm_back"):
        low_a, grad_dt_low, small = kernel_call(
            ssm_back_kernel,
            [((HALO + TOK, MODEL_WIDTH), BF16), ((TOK, NS), BF16), ((2 * CONV_K, MODEL_WIDTH), F32)],
            grad_y, conved, step_size, log_decay, dt_pre, state_in, state_grad, ext,
            conv_weight, conv_bias, decay_wide, skip_wide, far=(0, 1, 2, 3, 4, 7),
            scratch=[
                pltpu.VMEM((NS, TOK), F32),
                pltpu.VMEM((2 * HALO + TOK, MODEL_WIDTH), F32),
                pltpu.VMEM((TOK, MODEL_WIDTH), F32),
            ],
            vmem=16, us=8, name="ssm_back",
        )
        low_a, grad_dt_low, small, a_passed, b_passed, ffn_theirs = together(
            (low_a, grad_dt_low, small, a_passed, b_passed, ffn_theirs)
        )
    with jax.named_scope("late_grads"):
        late_keep, late_send = kernel_call(
            in_grads_kernel, [(half + (in_a_width,), BF16)] * 2, normed_a, low_a,
            vmem=12, name="late_grads_a",
        )
        late_arrived = send(late_send, OTHER_CORE)
    with jax.named_scope("early_grads"):
        a_ahead, a_behind, b_ahead, b_behind = pass_on(
            [a_ahead, a_behind] + a_passed, [b_ahead, b_behind] + b_passed
        )
        a_ready = [a_keep, send(a_ahead, along_z(1)), send(a_behind, along_z(-1))]
        b_ready = [b_keep, send(b_ahead, along_x(1)), send(b_behind, along_x(-1))]
    with jax.named_scope("attention_back"):
        grad_query, grad_own_kv, grad_other_kv = attend_back(
            index_word, query_low, grad_attended, attended_columns, log_total, own_kv, other_kv
        )
        (grad_query, grad_own_kv, grad_other_kv), a_ready, b_ready, late_arrived = together(
            ((grad_query, grad_own_kv, grad_other_kv), a_ready, b_ready, late_arrived)
        )
    with jax.named_scope("late_grads"):
        late_keep, late_ahead, late_behind, late_first, late_second = halve(
            late_keep, late_arrived, vmem=8
        )
        late_passed = [send(late_first, along_z(1)), send(late_second, along_z(-1))]
    with jax.named_scope("scatter_kv"):
        kv_arrived = send(grad_other_kv, OTHER_CORE)
        kv_arrived, late_passed = together((kv_arrived, late_passed))
        grad_kv = blocks_of([grad_own_kv, kv_arrived], 4)
        kv_arrived = spread(grad_kv, along_x)
    with jax.named_scope("late_grads"):
        late_ahead, late_behind = pass_on([late_ahead, late_behind] + late_passed, vmem=8)
        a_late = [late_keep, send(late_ahead, along_z(1)), send(late_behind, along_z(-1))]
        kv_arrived, a_late = together((kv_arrived, a_late))
    with jax.named_scope("last_grads"):
        rows = TOK // 4
        wide_a = early_a + in_a_width
        a_last = kernel_call(
            merge_a_kernel, [((rows, wide_a), F32)] + [((rows, wide_a), BF16)] * 3,
            *a_ready, *a_late, vmem=12, name="merge_a",
        )
    with jax.named_scope("project_in_back"):
        returned = send(low_a[HALO - (CONV_K - 1) : HALO], BACKWARD)
        low_own = low_a[HALO:].astype(F32) + jnp.pad(
            returned.astype(F32), ((TOK - (CONV_K - 1), 0), (0, 0))
        )
        from_a = kernel_call(
            project_a_kernel, [((TOK, MODEL_WIDTH), F32)],
            low_own.astype(BF16), grad_gate_low, in_a_own, in_a_other, in_b_own, in_b_other, to_a, to_b,
            vmem=20, us=2, name="project_a",
        )[0]
    with jax.named_scope("scatter_kv"):
        grad_kv = ring_sum(grad_kv, kv_arrived)
        grad_kv = blocks_of([grad_kv], 4)
        kv_arrived = spread(grad_kv, along_z)
        kv_arrived, from_a, a_last = together((kv_arrived, from_a, a_last))
        grad_kv = ring_sum(grad_kv, kv_arrived)
        kv_theirs = send(grad_kv[TOK:].astype(BF16), OTHER_Y)
        a_last = [a_last[0]] + spread(a_last, along_x)
        grad_kv = grad_kv[:TOK] + kv_theirs.astype(F32)
    with jax.named_scope("project_in_back"):
        late_b = ROPED + NS
        low_b = kernel_call(
            low_b_kernel, [((TOK, late_b), BF16)],
            grad_query, grad_kv, grad_dt_low, cosine, sine, vmem=8, name="low_b",
        )[0]
        first_part, gain_first_part = kernel_call(
            project_b_kernel, [((TOK, MODEL_WIDTH), BF16), ((1, MODEL_WIDTH), F32)],
            low_b, from_a, in_b_own, in_b_other, to_b, tokens, vmem=12, us=1, name="project_b",
        )
    with jax.named_scope("late_grads"):
        small = jnp.concatenate(
            [small[: CONV_K + 1], gain_first_part, gain_second_part, small[CONV_K + 3 :]], axis=0
        )
        lines, line = (SLOTS, MODEL_WIDTH // 2)
        b_keep, b_send, small = kernel_call(
            late_b_kernel,
            [(half + (late_b,), BF16), ((line + 2 * lines, late_b), BF16), ((lines, line), F32)],
            normed_b, low_b, small, vmem=12, name="late_grads_b",
        )
        *b_late, small = kernel_call(
            late_b_ring_kernel,
            [((TOK, late_b), F32)] + [((TOK + 2 * lines, late_b), BF16)] * 3 + [((lines, line), F32)],
            b_keep, send(b_send, OTHER_CORE), small, vmem=8, name="late_ring_b",
        )
        b_late = [b_late[0]] + spread(b_late, along_x)
    with jax.named_scope("last_grads"):
        wide_b = early_b + late_b
        *b_last, small = kernel_call(
            merge_b_kernel,
            [((rows, wide_b), F32)] + [((rows, wide_b + line), BF16)] * 3 + [((lines, line), F32)],
            *b_ready, *b_late, small, vmem=12, name="merge_b",
        )
        b_last = [b_last[0]] + spread(b_last, along_z)
        rows = rows // 2
        own, away, small, pair, cross = kernel_call(
            last_ring_kernel,
            [((rows, wide_a + wide_b), F32), ((rows, wide_a + wide_b + 2 * line), BF16),
             ((lines, line), F32), ((rows, 2 * NS + line), F32), ((rows, 2 * NS + line), F32)],
            *a_last, *b_last, small, vmem=8, name="last_ring",
        )
    with jax.named_scope("finish_grads"):
        widths = (ff, ff, WIDTH, WIDTH, 2 * NS, ff, WIDTH, QUERY_WIDTH, QUERY_WIDTH, HEAD_SIZE, HEAD_SIZE, NS)
        (
            grad_gate, grad_up, grad_z, grad_x, grad_bc, grad_down, grad_out, grad_o, grad_q, grad_k,
            grad_v, grad_dt, grad_conv_x, grad_conv_xb, summed_conv_bc, summed_conv_bcb,
            summed_gain_first, summed_gain_second, heads_row, unused
        ) = kernel_call(
            finish_grads_kernel,
            [((rows, width), F32) for width in widths]
            + [((CONV_K, WIDTH), F32), ((WIDTH,), F32), ((CONV_K, 2 * NS), F32), ((2 * NS,), F32),
               ((MODEL_WIDTH,), F32), ((MODEL_WIDTH,), F32), ((1, 3 * NS), F32), ((2 * CONV_K, NS), F32)],
            own, send(away, OTHER_Y), small, swap_heads(pair),
            lax.ppermute(cross, (SEQ, "head"), OTHER_Y_AND_HEAD), vmem=8, name="finish_grads",
        )
        grad_dt = grad_dt[:, :HEADS]
    with jax.named_scope("finish"):
        grad_first = first_part.astype(F32) + swap_heads(first_part).astype(F32)
        grad_tokens = grad_hidden + norm_back(tokens.astype(F32), gain_first[None, :], grad_first)[1]
        output = (hidden + (ffn_part.astype(F32) + ffn_theirs.astype(F32))).astype(BF16)
    with jax.named_scope("small_grads"):
        grad_dt_bias_own = heads_row[0, :HEADS]
        grad_decay_own = heads_row[0, NS : NS + HEADS]
        grad_skip_own = heads_row[0, 2 * NS : 2 * NS + HEADS]
    return (
        output,
        grad_tokens,
        summed_gain_first,
        grad_z,
        grad_x,
        grad_bc,
        grad_dt,
        grad_conv_x,
        grad_conv_xb,
        summed_conv_bc,
        summed_conv_bcb,
        grad_dt_bias_own,
        grad_decay_own,
        grad_skip_own,
        grad_out,
        grad_q,
        grad_k,
        grad_v,
        grad_o,
        summed_gain_second,
        grad_gate,
        grad_up,
        grad_down,
    )


def solution(mesh):
    return jax.shard_map(
        shards,
        mesh=mesh,
        in_specs=(
            P("seq", None),
            P("seq", None),
            P(),
            P("seq", "head"),
            P("seq", "head"),
            P("seq", None),
            P("seq", "head"),
            P(None, "head"),
            P("head"),
            P(),
            P(),
            P("head"),
            P("head"),
            P("head"),
            P("seq", "head"),
            P("seq", "head"),
            P("seq", "head"),
            P("seq", "head"),
            P("seq", "head"),
            P(),
            P("seq", "head"),
            P("seq", "head"),
            P("seq", "head"),
        ),
        out_specs=(
            P("seq", None),
            P("seq", None),
            P(),
            P("seq", "head"),
            P("seq", "head"),
            P("seq", None),
            P("seq", "head"),
            P(None, "head"),
            P("head"),
            P(),
            P(),
            P("head"),
            P("head"),
            P("head"),
            P("seq", "head"),
            P("seq", "head"),
            P("seq", "head"),
            P("seq", "head"),
            P("seq", "head"),
            P(),
            P("seq", "head"),
            P("seq", "head"),
            P("seq", "head"),
        ),
        check_vma=False,
    )
```

```python
import functools

import jax
import jax.numpy as jnp
from jax import lax
from jax.experimental import pallas as pl
from jax.experimental.pallas import tpu as pltpu
from jax.sharding import PartitionSpec as P

MODEL_WIDTH = 1024
NH = 24
P_SIZE = 64
NS = 128
HEAD_SIZE = 64
CONV_K = 4
TOK = 128
SPANS = 64
HEADS = 12
WIDTH = HEADS * P_SIZE
QUERY_WIDTH = 256
ROPED = QUERY_WIDTH + 2 * HEAD_SIZE
SLOTS = 16
SHARED = 4
HALO = 16
KEY_ROWS = SPANS // 2 * TOK

EPS = 1e-06
ROPE_BASE = 100000000000.0
MASKED = -1e30
HIGHEST = lax.Precision.HIGHEST
BF16 = jnp.bfloat16
F32 = jnp.float32
SEQ = "seq"


def place(index):
    return (index // 32, (index // 8) % 4, (index // 2) % 4, index % 2)


def index_of(y, x, z, core):
    return ((y * 4 + x) * 4 + z) * 2 + core


def pairs(move):
    return [(source, index_of(*move(*place(source)))) for source in range(SPANS)]


OTHER_CORE = pairs(lambda y, x, z, c: (y, x, z, 1 - c))
OTHER_Y = pairs(lambda y, x, z, c: (1 - y, x, z, c))
OTHER_HEAD = [(0, 1), (1, 0)]
OTHER_Y_AND_HEAD = [
    (source * 2 + head, target * 2 + 1 - head) for source, target in OTHER_Y for head in range(2)
]
ONWARD = [(span, span + 1) for span in range(SPANS - 1)]
BACKWARD = [(span + 1, span) for span in range(SPANS - 1)]


def along_x(steps):
    return pairs(lambda y, x, z, c: (y, (x + steps) % 4, z, c))


def along_z(steps):
    return pairs(lambda y, x, z, c: (y, x, (z + steps) % 4, c))


def send(value, route):
    return lax.ppermute(value, SEQ, route)


def swap_heads(value):
    return lax.ppermute(value, "head", OTHER_HEAD)


def swap_spans(value):
    return lax.all_to_all(value, SEQ, 0, 0, tiled=True)


def after(value, *others):
    return lax.optimization_barrier((value, others))[0]


def joined(pieces):
    return jnp.concatenate(pieces, axis=0)


def fetch(value, along):
    return [value] + [send(value, along(-step)) for step in (1, 2, 3)]


def ring_near(value, along):
    return (value, send(value, along(-1)), send(value, along(1)))


def ring_far(near, along):
    own, ahead, behind = near
    half = own.shape[0] // 2
    first = send(ahead[:half], along(-1))
    second = send(behind[half:], along(1))
    return [own, ahead, first, second, behind]


def blocks_of(parts, count):
    rows = parts[0].shape[0] // count
    return [
        sum(part[block * rows : (block + 1) * rows].astype(F32) for part in parts)
        for block in range(count)
    ]


def spread(blocks, along):
    return [send(block.astype(BF16), along(step)) for step, block in enumerate(blocks) if step]


def ring_sum(blocks, arrived):
    return blocks[0] + sum(block.astype(F32) for block in arrived)


def scatter_ring(parts, along):
    blocks = blocks_of(parts, 4)
    return ring_sum(blocks, spread(blocks, along))


def one_hot_orders(index):
    y, x, z, c = place(index)
    row = jnp.arange(MODEL_WIDTH, dtype=jnp.int32)
    inner = row % 16
    dy, low, high, dc = ((row // 16) % 2, (row // 32) % 4, (row // 128) % 4, row // 512)

    def one_hot(dx, dz):
        device = index_of((y + dy) % 2, (x + dx) % 4, (z + dz) % 4, (c + dc) % 2)
        return (row[:, None] == (device * 16 + inner)[None, :]).astype(BF16)

    return (one_hot(low, high), one_hot(high, low))


def project(left_side, right_side):
    return jnp.dot(left_side, right_side, preferred_element_type=F32)


def rms_norm(values, norm_gain):
    return values * lax.rsqrt(jnp.mean(values * values, axis=-1, keepdims=True) + EPS) * norm_gain


def rotary_tables(index):
    half = HEAD_SIZE // 2
    frequency = ROPE_BASE ** (-jnp.arange(half, dtype=F32) * (1.0 / half))
    positions = (index * TOK + jnp.arange(TOK, dtype=jnp.int32)).astype(F32)
    angles = positions[:, None] * frequency[None, :]
    cosine, sine = (jnp.cos(angles), jnp.sin(angles))
    turns = QUERY_WIDTH // HEAD_SIZE + 1
    plain = jnp.ones((TOK, HEAD_SIZE), F32)
    return (
        jnp.concatenate([cosine, cosine] * turns + [plain], axis=1),
        jnp.concatenate([-sine, sine] * turns + [0.0 * plain], axis=1),
    )


def dot_f32(left_side, right_side, left_dim=1, right_dim=0):
    return lax.dot_general(
        left_side, right_side, (((left_dim,), (right_dim,)), ((), ())), precision=HIGHEST,
        preferred_element_type=F32,
    )


def dot_low(left_side, right_side, left_dim=1, right_dim=0):
    return lax.dot_general(
        left_side, right_side, (((left_dim,), (right_dim,)), ((), ())), preferred_element_type=F32
    )


def lanes_of(shape):
    return lax.broadcasted_iota(jnp.int32, shape, len(shape) - 1)


def rows_of(shape):
    return lax.broadcasted_iota(jnp.int32, shape, len(shape) - 2)


def head_spread():
    shape = (NS, HEADS * P_SIZE)
    return (lanes_of(shape) // P_SIZE == rows_of(shape)).astype(F32)


def causal_mask():
    return rows_of((TOK, TOK)) >= lanes_of((TOK, TOK))


def sigmoid(values):
    return 1.0 / (1.0 + jnp.exp(-values))


def softplus(values):
    small = jnp.exp(-jnp.abs(values))
    series = small * (1.0 - small * (0.5 - small * (1.0 / 3.0 - small * 0.25)))
    return jnp.maximum(values, 0.0) + jnp.where(small < 0.01, series, jnp.log(1.0 + small))


def turn(values, cosine, sine):
    width = values.shape[1]
    half = HEAD_SIZE // 2
    ahead = pltpu.roll(values, width - half, 1)
    behind = pltpu.roll(values, half, 1)
    other = jnp.where(lanes_of(values.shape) % HEAD_SIZE < half, ahead, behind)
    return values * cosine + other * sine


FAR = "far"


def far_away(value):
    return pltpu.with_memory_space_constraint(value, pltpu.HBM)


def kernel_call(body, outs, *operands, far=(), scratch=(), vmem=16, us=1, name=None):
    vspec = pl.BlockSpec(memory_space=pltpu.VMEM)
    operands = [far_away(value) if at in far else value for at, value in enumerate(operands)]
    return pl.pallas_call(
        body,
        out_shape=tuple(
            pltpu.HBM(*out[:2]) if FAR in out else jax.ShapeDtypeStruct(*out) for out in outs
        ),
        in_specs=[vspec] * len(operands),
        out_specs=(vspec,) * len(outs),
        scratch_shapes=list(scratch),
        compiler_params=pltpu.CompilerParams(vmem_limit_bytes=vmem * 2**20),
        cost_estimate=pl.CostEstimate(flops=us * 10**9, bytes_accessed=0, transcendentals=0),
        name=name,
    )(*operands)


def attention_in_kernel(
    normed_ref, own_ref, other_ref, cosine_ref, sine_ref, dt_bias_ref, decay_ref,
    gate_ref, query_ref, kv_ref, dt_ref, step_ref, log_ref,
):
    normed = normed_ref[...]
    half = MODEL_WIDTH // 2
    raw = dot_low(normed[:, :half], own_ref[...]) + dot_low(normed[:, half:], other_ref[...])
    gate_ref[...] = raw[:, :WIDTH]
    turned = turn(raw[:, WIDTH : WIDTH + ROPED], cosine_ref[...], sine_ref[...]).astype(BF16)
    query_ref[...] = turned[:, :QUERY_WIDTH]
    kv_ref[...] = turned[:, QUERY_WIDTH:]
    dt = raw[:, WIDTH + ROPED :] + dt_bias_ref[...]
    step = softplus(dt)
    dt_ref[...] = dt
    step_ref[...] = step
    log_ref[...] = dot_f32(causal_mask().astype(F32), -step * decay_ref[...])


def convolved(ext_ref, conv_weight, conv_bias):
    summed = conv_bias
    for lag in range(CONV_K):
        summed = summed + conv_weight[lag : lag + 1] * ext_ref[pl.ds(HALO - CONV_K + 1 + lag, TOK), :]
    return summed


def ssm_in_kernel(
    normed_ref, own_ref, other_ref, conv_weight_ref, conv_bias_ref, step_ref, log_ref,
    ext_ref, conv_ref, state_ref,
):
    normed = normed_ref[...]
    half = MODEL_WIDTH // 2
    ext_ref[...] = dot_low(normed[:, :half], own_ref[...]) + dot_low(normed[:, half:], other_ref[...])
    summed = convolved(ext_ref, conv_weight_ref[...], conv_bias_ref[...])
    conved = summed * sigmoid(summed)
    conv_ref[...] = conved
    log_decay = log_ref[...]
    last = log_decay[TOK - 1 :]
    to_end = jnp.exp(last - log_decay) * step_ref[...]
    weighted = conved[:, :WIDTH] * dot_f32(to_end, head_spread())
    local = dot_f32(weighted.T, conved[:, WIDTH : WIDTH + NS])
    state_ref[...] = jnp.zeros_like(state_ref)
    for head in range(HEADS):
        state_ref[:, head, :] = local[head * P_SIZE : (head + 1) * P_SIZE]
    state_ref[:, HEADS, :] = jnp.broadcast_to(jnp.exp(last), (P_SIZE, NS))


def states_kernel(reverse, decay_ref, local_ref, out_ref):
    decays = decay_ref[:, HEADS, :].T[:SLOTS]
    state = jnp.zeros((SLOTS, NS), F32)
    for position in range(SPANS):
        span = SPANS - 1 - position if reverse else position
        out_ref[span] = state
        if position < SPANS - 1:
            state = decays[:, span : span + 1] * state + local_ref[span]


def states_between(decays, local, reverse):
    return kernel_call(
        functools.partial(states_kernel, reverse), [((SPANS, SLOTS, NS), F32, FAR)], decays, local,
        vmem=16, name="states",
    )[0]


def head_decay(log_decay, log_rows, head):
    apart = jnp.minimum(log_decay[:, head : head + 1] - log_rows[head : head + 1], 0.0)
    return jnp.where(causal_mask(), jnp.exp(apart), 0.0)


def stacked_states(state_ref):
    return jnp.concatenate([state_ref[:, head, :] for head in range(HEADS)], axis=0)


def first_of_pair(shape):
    return lanes_of(shape) < P_SIZE


def ssm_out_kernel(
    conv_ref, step_ref, log_ref, state_ref, gate_ref, skip_ref, gated_ref, y_ref
):
    conved = conv_ref[...]
    in_vectors = conved[:, WIDTH : WIDTH + NS]
    out_vectors = conved[:, WIDTH + NS :]
    log_decay = log_ref[...]
    log_rows = log_decay.T
    step_rows = step_ref[...].T
    spread = head_spread()
    both = dot_f32(out_vectors, in_vectors, 1, 1)
    carried = dot_f32(out_vectors, stacked_states(state_ref), 1, 1)
    skip = dot_f32(jnp.broadcast_to(skip_ref[...], (8, NS)), spread)[:1]
    outer = dot_f32(jnp.exp(log_decay), spread) * carried + skip * conved[:, :WIDTH]
    for pair in range(HEADS // 2):
        lanes = slice(pair * 2 * P_SIZE, (pair + 1) * 2 * P_SIZE)
        inputs = conved[:, lanes]
        parts = []
        for head in (2 * pair, 2 * pair + 1):
            mixing = both * head_decay(log_decay, log_rows, head) * step_rows[head : head + 1]
            parts.append(dot_f32(mixing, inputs))
        y = outer[:, lanes] + jnp.where(first_of_pair(inputs.shape), parts[0], parts[1])
        gate = gate_ref[:, lanes]
        y_ref[:, lanes] = y
        gated_ref[:, lanes] = (y * gate * sigmoid(gate)).astype(BF16)


def mixer_out_kernel(gated_ref, attended_ref, own_ref, other_ref, order_ref, out_ref):
    mixed = jnp.concatenate([gated_ref[...], attended_ref[...]], axis=1)
    wide = mixed.shape[1]
    parts = [dot_low(mixed, ref[:, :wide], 1, 1).astype(BF16) for ref in (own_ref, other_ref)]
    out_ref[...] = dot_low(jnp.concatenate(parts, axis=1), order_ref[...], 1, 1).astype(BF16)


def ffn_kernel(
    tokens_ref, mixed_ref, theirs_ref, gain_ref, grad_inner_ref, order_a_ref,
    gate_up_own_ref, gate_up_other_ref,
    hidden_ref, turned_ref, inner_ref, grad_ref, second_ref,
):
    half = MODEL_WIDTH // 2
    hidden = tokens_ref[...].astype(F32) + (mixed_ref[...].astype(F32) + theirs_ref[...].astype(F32))
    hidden_ref[...] = hidden
    scale = lax.rsqrt(jnp.mean(hidden * hidden, axis=1, keepdims=True) + EPS)
    normed = (hidden * scale * gain_ref[...]).astype(BF16)
    turned = dot_low(normed, order_a_ref[...]).astype(BF16)
    turned_ref[...] = turned
    ff = gate_up_own_ref.shape[1] // 2
    gate = dot_low(turned[:, :half], gate_up_own_ref[:, :ff]) + dot_low(
        turned[:, half:], gate_up_other_ref[:, :ff]
    )
    up = dot_low(turned[:, :half], gate_up_own_ref[:, ff:]) + dot_low(
        turned[:, half:], gate_up_other_ref[:, ff:]
    )
    grad_inner = grad_inner_ref[...]
    opened = sigmoid(gate)
    silu = gate * opened
    inner_ref[...] = (silu * up).astype(BF16)
    grad_gate = (grad_inner * up * (opened * (1.0 + gate * (1.0 - opened)))).astype(BF16)
    grads = jnp.concatenate([grad_gate, (grad_inner * silu).astype(BF16)], axis=1)
    grad_ref[...] = grads
    parts = [dot_low(grads, ref[...], 1, 1).astype(BF16) for ref in (gate_up_own_ref, gate_up_other_ref)]
    second_ref[...] = dot_low(jnp.concatenate(parts, axis=1), order_a_ref[...], 1, 1).astype(BF16)


def down_back_kernel(cot_ref, own_ref, other_ref, out_ref):
    ff = own_ref.shape[1] // 2
    half = MODEL_WIDTH // 2
    out_ref[...] = dot_low(cot_ref[:, :half], own_ref[:, ff:]) + dot_low(
        cot_ref[:, half:], other_ref[:, ff:]
    )


def ffn_out_kernel(inner_ref, own_ref, other_ref, order_ref, out_ref):
    ff = inner_ref.shape[1]
    inner = inner_ref[...]
    parts = [dot_low(inner, ref[:, ff:], 1, 1).astype(BF16) for ref in (own_ref, other_ref)]
    out_ref[...] = dot_low(jnp.concatenate(parts, axis=1), order_ref[...], 1, 1).astype(BF16)


def norm_back(values, gain, grad):
    scale = lax.rsqrt(jnp.mean(values * values, axis=1, keepdims=True) + EPS)
    weighted = grad * gain
    along = jnp.mean(weighted * values, axis=1, keepdims=True)
    return (scale, weighted * scale - values * (scale * scale * scale * along))


def mixer_back_kernel(
    hidden_ref, second_ref, theirs_ref, gain_ref, cot_ref, order_ref, own_ref, other_ref,
    gate_ref, y_ref, conv_ref, log_ref,
    grad_hidden_ref, turned_ref, grad_gain_ref, grad_attended_ref, grad_y_ref, grad_gate_ref,
    state_ref,
):
    half = MODEL_WIDTH // 2
    hidden = hidden_ref[...]
    mine = second_ref[...].astype(F32)
    scale, back = norm_back(hidden, gain_ref[...], mine + theirs_ref[...].astype(F32))
    grad_gain_ref[...] = jnp.sum(mine * hidden * scale, axis=0, keepdims=True)
    grad_hidden = cot_ref[...].astype(F32) + back
    grad_hidden_ref[...] = grad_hidden
    turned = dot_low(grad_hidden.astype(BF16), order_ref[...]).astype(BF16)
    turned_ref[...] = turned
    wide = WIDTH + QUERY_WIDTH
    grads = dot_low(turned[:, :half], own_ref[:, :wide]) + dot_low(turned[:, half:], other_ref[:, :wide])
    grad_attended_ref[...] = grads[:, WIDTH:].astype(BF16)
    grad_gated = grads[:, :WIDTH]
    gate = gate_ref[...]
    opened = sigmoid(gate)
    grad_y = grad_gated * gate * opened
    grad_y_ref[...] = grad_y
    grad_gate_ref[...] = (grad_gated * y_ref[...] * (opened * (1.0 + gate * (1.0 - opened)))).astype(BF16)
    weighted = grad_y * dot_f32(jnp.exp(log_ref[...]), head_spread())
    local = dot_f32(weighted.T, conv_ref[:, WIDTH + NS :])
    state_ref[...] = jnp.zeros_like(state_ref)
    for head in range(HEADS):
        state_ref[:, head, :] = local[head * P_SIZE : (head + 1) * P_SIZE]


def ffn_grads_kernel(
    normed_ref, grad_ff_ref, cot_ref, inner_ref, a_keep_ref, a_send_ref, b_keep_ref, b_send_ref
):
    half = MODEL_WIDTH // 2
    for part, (a_ref, b_ref) in enumerate(((a_keep_ref, b_keep_ref), (a_send_ref, b_send_ref))):
        lanes = slice(part * half, (part + 1) * half)
        a_ref[...] = dot_low(normed_ref[:, lanes], grad_ff_ref[...], 0, 0).astype(BF16)
        b_ref[...] = dot_low(cot_ref[:, lanes], inner_ref[...], 0, 0).astype(BF16)


def mixer_grads_kernel(
    normed_ref, grad_gate_ref, grad_mixed_ref, gated_ref, attended_ref,
    a_keep_ref, a_send_ref, b_keep_ref, b_send_ref,
):
    half = MODEL_WIDTH // 2
    for part, (a_ref, b_ref) in enumerate(((a_keep_ref, b_keep_ref), (a_send_ref, b_send_ref))):
        lanes = slice(part * half, (part + 1) * half)
        a_ref[...] = dot_low(normed_ref[HALO:, lanes], grad_gate_ref[...], 0, 0).astype(BF16)
        mixed = grad_mixed_ref[:, lanes]
        b_ref[:, :WIDTH] = dot_low(mixed, gated_ref[...], 0, 0).astype(BF16)
        b_ref[:, WIDTH:] = dot_low(mixed, attended_ref[...], 0, 0).astype(BF16)


def ssm_back_kernel(
    grad_y_ref, conv_ref, step_ref, log_ref, dt_ref, state_ref, grad_state_ref, ext_ref,
    conv_weight_ref, conv_bias_ref, decay_ref, skip_ref,
    grad_ext_ref, grad_dt_ref, small_ref, row_ref, pad_ref, grad_conv_ref,
):
    conved = conv_ref[...]
    grad_y = grad_y_ref[...]
    in_vectors = conved[:, WIDTH : WIDTH + NS]
    out_vectors = conved[:, WIDTH + NS :]
    step = step_ref[...]
    step_rows = step.T
    log_decay = log_ref[...]
    log_rows = log_decay.T
    last = log_decay[TOK - 1 :]
    spread = head_spread()
    states = stacked_states(state_ref)
    grad_states = stacked_states(grad_state_ref)
    now = jnp.exp(log_decay)
    leave = jnp.exp(last - log_decay)
    to_end = leave * step
    both = dot_f32(out_vectors, in_vectors, 1, 1)
    carried = dot_f32(out_vectors, states, 1, 1)
    pushed = dot_f32(in_vectors, grad_states, 1, 1)
    now_wide = dot_f32(now, spread)
    to_end_wide = dot_f32(to_end, spread)
    skip_wide = dot_f32(jnp.broadcast_to(skip_ref[...], (8, NS)), spread)[:1]
    inputs = conved[:, :WIDTH]
    grad_out = dot_f32(grad_y * now_wide, states)
    grad_in = dot_f32(inputs * to_end_wide, grad_states)
    outer = grad_y * skip_wide + to_end_wide * pushed
    grad_log = dot_f32(grad_y * carried * now_wide, spread, 1, 1)
    grad_to_end = dot_f32(inputs * pushed, spread, 1, 1)
    skip_sum = dot_f32(grad_y * inputs, spread, 1, 1)
    grad_step = grad_to_end * leave
    into_end = grad_to_end * to_end
    grad_log = grad_log - into_end
    stays = jnp.sum((states * grad_states).reshape(HEADS, P_SIZE, NS), axis=1)
    stays = jnp.concatenate([stays, jnp.zeros((NS - HEADS, NS), F32)], axis=0)
    stays = jnp.sum(stays.T, axis=0, keepdims=True)
    grad_last = jnp.sum(into_end, axis=0, keepdims=True) + jnp.exp(last) * stays
    grad_both = jnp.zeros((TOK, TOK), F32)
    row_ref[...] = jnp.zeros_like(row_ref)
    for pair in range(HEADS // 2):
        lanes = slice(pair * 2 * P_SIZE, (pair + 1) * 2 * P_SIZE)
        pair_inputs = conved[:, lanes]
        pair_grads = grad_y[:, lanes]
        first = first_of_pair(pair_inputs.shape)
        parts = []
        for side, head in enumerate((2 * pair, 2 * pair + 1)):
            decay = head_decay(log_decay, log_rows, head)
            step_row = step_rows[head : head + 1]
            mine = jnp.where(first if side == 0 else jnp.logical_not(first), pair_grads, 0.0)
            grad_mixing = dot_f32(mine, pair_inputs, 1, 1) * decay
            grad_both = grad_both + grad_mixing * step_row
            apart = grad_mixing * both
            row_ref[head : head + 1, :] = jnp.sum(apart, axis=0, keepdims=True)
            along = jnp.sum(apart * step_row, axis=1, keepdims=True)
            grad_log = grad_log + jnp.where(lanes_of((TOK, NS)) == head, along, 0.0)
            mixing = both * decay * step_row
            parts.append(dot_f32(mixing.T, pair_grads))
        grad_conv_ref[:, lanes] = outer[:, lanes] + jnp.where(first, parts[0], parts[1])
    rows = row_ref[...].T
    grad_step = grad_step + rows
    grad_log = grad_log - rows * step
    grad_log = grad_log + jnp.where(rows_of((TOK, NS)) == TOK - 1, grad_last, 0.0)
    grad_rate = dot_f32((rows_of((TOK, TOK)) <= lanes_of((TOK, TOK))).astype(F32), grad_log)
    grad_step = grad_step - grad_rate * decay_ref[...]
    grad_dt = grad_step * sigmoid(dt_ref[...])
    grad_dt_ref[...] = jnp.where(lanes_of((TOK, NS)) < HEADS, grad_dt, 0.0).astype(BF16)
    grad_conv_ref[:, WIDTH : WIDTH + NS] = grad_in + dot_f32(grad_both.T, out_vectors)
    grad_conv_ref[:, WIDTH + NS :] = grad_out + dot_f32(grad_both, in_vectors)
    summed = convolved(ext_ref, conv_weight_ref[...], conv_bias_ref[...])
    opened = sigmoid(summed)
    grad_summed = grad_conv_ref[...] * (opened * (1.0 + summed * (1.0 - opened)))
    pad_ref[...] = jnp.zeros_like(pad_ref)
    pad_ref[pl.ds(HALO, TOK), :] = grad_summed
    conv_weight = conv_weight_ref[...]
    total = 0.0
    for lag in range(CONV_K):
        total = total + conv_weight[lag : lag + 1] * pad_ref[pl.ds(CONV_K - 1 - lag, HALO + TOK), :]
        small_ref[lag : lag + 1, :] = jnp.sum(
            grad_summed * ext_ref[pl.ds(HALO - CONV_K + 1 + lag, TOK), :], axis=0, keepdims=True
        )
    grad_ext_ref[...] = total.astype(BF16)
    small_ref[CONV_K : CONV_K + 1, :] = jnp.sum(grad_summed, axis=0, keepdims=True)
    small_ref[CONV_K + 1 : CONV_K + 3, :] = jnp.zeros((2, MODEL_WIDTH), F32)
    heads_row = jnp.concatenate(
        [
            jnp.sum(grad_dt, axis=0, keepdims=True),
            -jnp.sum(grad_rate * step, axis=0, keepdims=True),
            jnp.sum(skip_sum, axis=0, keepdims=True),
            jnp.zeros((1, MODEL_WIDTH - 3 * NS), F32),
        ],
        axis=1,
    )
    small_ref[CONV_K + 3 : CONV_K + 4, :] = heads_row


def project_a_kernel(
    low_ref, grad_gate_ref, a_own_ref, a_other_ref, b_own_ref, b_other_ref, order_a_ref, order_b_ref, out_ref
):
    parts = [dot_low(low_ref[...], ref[...], 1, 1).astype(BF16) for ref in (a_own_ref, a_other_ref)]
    from_a = dot_low(jnp.concatenate(parts, axis=1), order_a_ref[...], 1, 1)
    gate = grad_gate_ref[...]
    parts = [dot_low(gate, ref[:, :WIDTH], 1, 1).astype(BF16) for ref in (b_own_ref, b_other_ref)]
    out_ref[...] = from_a + dot_low(jnp.concatenate(parts, axis=1), order_b_ref[...], 1, 1)


def project_b_kernel(
    low_ref, from_ref, own_ref, other_ref, order_ref, tokens_ref, first_ref, grad_gain_ref
):
    parts = [dot_low(low_ref[...], ref[:, WIDTH:], 1, 1).astype(BF16) for ref in (own_ref, other_ref)]
    first = from_ref[...] + dot_low(jnp.concatenate(parts, axis=1), order_ref[...], 1, 1)
    first = first.astype(BF16)
    first_ref[...] = first
    tokens = tokens_ref[...].astype(F32)
    scale = lax.rsqrt(jnp.mean(tokens * tokens, axis=1, keepdims=True) + EPS)
    grad_gain_ref[...] = jnp.sum(first.astype(F32) * tokens * scale, axis=0, keepdims=True)


def join_kernel(counts, *refs):
    pieces = list(refs[: sum(counts)])
    for count, out_ref in zip(counts, refs[sum(counts) :]):
        at = 0
        for ref in pieces[:count]:
            out_ref[at : at + ref.shape[0], :] = ref[...]
            at += ref.shape[0]
        pieces = pieces[count:]


def join_rings(*groups, vmem=12, far=False):
    outs = [((sum(piece.shape[0] for piece in group), group[0].shape[1]), BF16) for group in groups]
    pieces = [piece for group in groups for piece in group]
    if far:
        pieces = [far_away(piece) for piece in pieces]
    counts = tuple(len(group) for group in groups)
    return kernel_call(functools.partial(join_kernel, counts), outs, *pieces, vmem=vmem, name="join_rings")


def pass_on_kernel(*refs):
    for ahead, behind, from_behind, from_ahead, ahead_out, behind_out in zip(*[iter(refs)] * 6):
        half = from_ahead.shape[0]
        ahead_out[:half, :] = (ahead[:half, :].astype(F32) + from_behind[...].astype(F32)).astype(BF16)
        ahead_out[half:, :] = ahead[half:, :]
        behind_out[:half, :] = behind[:half, :]
        behind_out[half:, :] = (behind[half:, :].astype(F32) + from_ahead[...].astype(F32)).astype(BF16)


def halve_kernel(*refs):
    groups = (len(refs) - 5) // 2
    rows = refs[0].shape[0] // 4
    outs = refs[2 * groups :]
    starts = ((0, rows), (rows, rows), (3 * rows, rows), (2 * rows, rows // 2), (2 * rows + rows // 2, rows // 2))
    at = 0
    for group in range(groups):
        keep_ref, arrived_ref = refs[2 * group : 2 * group + 2]
        lanes = slice(at, at + keep_ref.shape[1])
        at += keep_ref.shape[1]
        for (start, size), out_ref in zip(starts, outs):
            part = slice(start, start + size)
            total = keep_ref[part, :].astype(F32) + arrived_ref[part, :].astype(F32)
            out_ref[:, lanes] = total.astype(out_ref.dtype)


def halve(*parts, vmem=16, far=False):
    rows = parts[0].shape[0] // 4
    width = sum(part.shape[1] for part in parts[::2])
    sizes = ((rows, F32), (rows, BF16), (rows, BF16), (rows // 2, BF16), (rows // 2, BF16))
    return kernel_call(
        halve_kernel, [((size, width), dtype) + ((FAR,) if far else ()) for size, dtype in sizes], *parts,
        far=range(len(parts)) if far else (), vmem=vmem, us=2,
        name="halve",
    )


def pass_on(*groups, vmem=16):
    def body(*refs):
        count = 4 * len(groups)
        ins, outs = (refs[:count], refs[count:])
        mixed = []
        for group in range(len(groups)):
            mixed += ins[4 * group : 4 * group + 4] + outs[2 * group : 2 * group + 2]
        pass_on_kernel(*mixed)

    outs = [(piece.shape, BF16) for group in groups for piece in group[:2]]
    pieces = [piece for group in groups for piece in group]
    return kernel_call(body, outs, *pieces, vmem=vmem, name="pass_on")


def two_halves(values):
    high = values.astype(BF16)
    return (high, (values - high.astype(F32)).astype(BF16))


def of_halves(high, low):
    return high.astype(F32) + low.astype(F32)


def late_b_kernel(normed_ref, low_ref, small_ref, keep_ref, send_ref, sent_ref):
    half = MODEL_WIDTH // 2
    low = low_ref[...]
    keep_ref[...] = dot_low(normed_ref[:, :half], low, 0, 0).astype(BF16)
    send_ref[:half, :] = dot_low(normed_ref[:, half:], low, 0, 0).astype(BF16)
    small = small_ref[...]
    high, rest = two_halves(jnp.concatenate([small[:, :half], small[:, half:]], axis=0))
    send_ref[half:, :] = jnp.concatenate([high, rest], axis=0)
    sent_ref[...] = of_halves(high, rest)


def late_b_ring_kernel(keep_ref, arrived_ref, small_ref, first_ref, *rest_refs):
    rows = TOK
    total = keep_ref[...].astype(F32) + arrived_ref[: 4 * rows, :].astype(F32)
    lines = small_ref.shape[0]
    small = small_ref[...] + of_halves(
        arrived_ref[4 * rows : 4 * rows + lines, :], arrived_ref[4 * rows + lines :, :]
    )
    high, rest = two_halves(small)
    first_ref[...] = total[:rows]
    tail = jnp.concatenate([high, rest], axis=0)
    for step in (1, 2, 3):
        rest_refs[step - 1][:rows, :] = total[step * rows : (step + 1) * rows].astype(BF16)
        rest_refs[step - 1][rows:, :] = tail
    rest_refs[3][...] = of_halves(high, rest)


def ring_total(refs, rows):
    return refs[0][...] + sum(ref[:rows, :].astype(F32) for ref in refs[1:])


def merge_a_kernel(*refs):
    early, late, (keep_ref, *send_refs) = (refs[:3], refs[3:6], refs[6:])
    total = jnp.concatenate([ring_total(early, TOK), ring_total(late, TOK)], axis=1)
    rows = TOK // 4
    keep_ref[...] = total[:rows]
    for step in (1, 2, 3):
        send_refs[step - 1][...] = total[step * rows : (step + 1) * rows].astype(BF16)


def ring_small(small_ref, pieces):
    first, second, third = pieces
    return (small_ref[...] + second) + (first + third)


def merge_b_kernel(*refs):
    early, late, small_ref = (refs[:3], refs[3:7], refs[7])
    keep_ref, *send_refs, sent_ref = refs[8:]
    total = jnp.concatenate([ring_total(early, TOK), ring_total(late, TOK)], axis=1)
    lines = small_ref.shape[0]
    small = ring_small(
        small_ref, [of_halves(ref[TOK : TOK + lines, :], ref[TOK + lines :, :]) for ref in late[1:]]
    )
    high, rest = two_halves(small)
    tail = jnp.concatenate([high, rest], axis=0)
    rows = TOK // 4
    keep_ref[...] = total[:rows]
    width = total.shape[1]
    for step in (1, 2, 3):
        send_refs[step - 1][:, :width] = total[step * rows : (step + 1) * rows].astype(BF16)
        send_refs[step - 1][:, width:] = tail
    sent_ref[...] = of_halves(high, rest)


def last_ring_kernel(*refs):
    a_refs, b_refs, small_ref = (refs[:4], refs[4:8], refs[8])
    keep_ref, away_ref, sent_ref, pair_ref, cross_ref = refs[9:]
    rows = TOK // 4
    width = b_refs[0].shape[1]
    lines = small_ref.shape[0]
    total_b = b_refs[0][...] + (
        b_refs[1][:, :width].astype(F32) + b_refs[2][:, :width].astype(F32) + b_refs[3][:, :width].astype(F32)
    )
    total = jnp.concatenate([ring_total(a_refs, rows), total_b], axis=1)
    small = ring_small(
        small_ref, [of_halves(ref[:lines, width:], ref[lines:, width:]) for ref in b_refs[1:]]
    )
    high, rest = two_halves(small)
    keep_ref[...] = total[: rows // 2]
    away_ref[:, : total.shape[1]] = total[rows // 2 :].astype(BF16)
    away_ref[:, total.shape[1] :] = jnp.concatenate([high, rest], axis=1)
    small = of_halves(high, rest)
    sent_ref[...] = small
    stop = a_refs[0].shape[1]
    shared = total[:, stop - 2 * NS : stop]
    pair_ref[...] = jnp.concatenate([shared[: rows // 2], small], axis=1)
    shared = shared[rows // 2 :].astype(BF16).astype(F32)
    cross_ref[...] = jnp.concatenate([shared, small], axis=1)


def in_grads_kernel(normed_ref, low_ref, keep_ref, send_ref):
    half = MODEL_WIDTH // 2
    low = low_ref[...]
    keep_ref[...] = dot_low(normed_ref[:, :half], low, 0, 0).astype(BF16)
    send_ref[...] = dot_low(normed_ref[:, half:], low, 0, 0).astype(BF16)


def finish_grads_kernel(keep_ref, theirs_ref, small_ref, pair_ref, cross_ref, *refs):
    out_refs, small_refs = (refs[:-8], refs[-8:])
    others = pair_ref[...] + cross_ref[...]
    at = 0
    for number, ref in enumerate(out_refs):
        lanes = slice(at, at + ref.shape[1])
        total = keep_ref[:, lanes] + theirs_ref[:, lanes].astype(F32)
        ref[...] = total + others[:, : 2 * NS] if number == SHARED else total
        at += ref.shape[1]
    at = keep_ref.shape[1]
    width = small_ref.shape[1]
    own = small_ref[...] + of_halves(theirs_ref[:, at : at + width], theirs_ref[:, at + width :])
    both = own + others[:, 2 * NS :]
    lines = 2 * CONV_K
    own = jnp.concatenate([own[:lines], own[lines:]], axis=1)
    both = jnp.concatenate([both[:lines], both[lines:]], axis=1)
    conv_x_ref, conv_xb_ref, conv_bc_ref, conv_bcb_ref, first_ref, second_ref, heads_ref, rest_ref = small_refs
    conv_x_ref[...] = own[:CONV_K, :WIDTH]
    conv_xb_ref[...] = own[CONV_K, :WIDTH]
    conv_bc_ref[...] = both[:CONV_K, WIDTH:]
    conv_bcb_ref[...] = both[CONV_K, WIDTH:]
    first_ref[...] = both[CONV_K + 1]
    second_ref[...] = both[CONV_K + 2]
    heads_ref[...] = own[CONV_K + 3 :, : 3 * NS]
    rest_ref[...] = own[:, :NS]


def low_b_kernel(query_ref, kv_ref, dt_ref, cosine_ref, sine_ref, out_ref):
    grads = jnp.concatenate([query_ref[...], kv_ref[...]], axis=1)
    out_ref[:, :ROPED] = turn(grads, cosine_ref[...], -sine_ref[...]).astype(BF16)
    out_ref[:, ROPED:] = dt_ref[...]


def slot_of(pair, index):
    y, x, z = (index >> 5, (index >> 3) & 3, (index >> 1) & 3)
    dy = ((pair >> 4) - y) & 1
    dx = ((pair >> 2) - x) & 3
    dz = (pair - z) & 3
    return pl.multiple_of(((dx * 4 + dz) * 2 + dy) * TOK, TOK)


def load_quad(quad, index, own_ref, other_ref):
    parts = []
    for side in (0, 1):
        slot = slot_of(quad * 2 + side, index)
        parts += [own_ref[pl.ds(slot, TOK), :], other_ref[pl.ds(slot, TOK), :]]
    return jnp.concatenate(parts, axis=0)


def head_columns(rows):
    turned = rows.T
    heads = rows.shape[1] // HEAD_SIZE
    return jnp.concatenate(
        [turned[head * HEAD_SIZE : (head + 1) * HEAD_SIZE] for head in range(heads)], axis=1
    )


def head_rows(rows):
    heads = rows.shape[1] // HEAD_SIZE
    return jnp.concatenate(
        [rows[:, head * HEAD_SIZE : (head + 1) * HEAD_SIZE] for head in range(heads)], axis=0
    )


def rows_of_columns(columns):
    heads = columns.shape[1] // TOK
    stacked = jnp.concatenate(
        [columns[:, head * TOK : (head + 1) * TOK] for head in range(heads)], axis=0
    )
    return stacked.T


def quad_mask(shape, quad, index):
    row = rows_of(shape)
    block = quad * 4 + (row >> 8) * 2 + ((index & 1) ^ ((row >> 7) & 1))
    keys = block * TOK + (row & (TOK - 1))
    queries = index * TOK + (lanes_of(shape) & (TOK - 1))
    return keys <= queries


def attend_kernel(index_ref, query_ref, own_ref, other_ref, columns_ref, rows_ref, log_ref, total_ref, even_ref, odd_ref):
    index = index_ref[0]
    query = head_columns(query_ref[...].astype(F32) * HEAD_SIZE ** (-0.5))
    padded = jnp.concatenate([query, jnp.zeros_like(query)], axis=0).astype(BF16)
    total_ref[...] = jnp.zeros_like(total_ref)

    def scores_of(quad):
        quad_kv = load_quad(quad, index, own_ref, other_ref)
        return jnp.dot(quad_kv, padded, preferred_element_type=F32)

    def step(quad, carry, scores):
        peak, weight = carry
        quad_kv = load_quad(quad, index, own_ref, other_ref)
        new_peak = jnp.maximum(peak, jnp.max(scores, axis=0, keepdims=True))
        shrink = jnp.exp(peak - new_peak)
        probs = jnp.exp(scores - new_peak)
        weight = weight * shrink + jnp.sum(probs, axis=0, keepdims=True)
        total_ref[...] = total_ref[...] * shrink + dot_low(quad_kv, probs.astype(BF16), 0, 0)
        return (new_peak, weight)

    lanes = (1, query.shape[1])
    last = index >> 2
    even_ref[...] = scores_of(0)
    scores = scores_of(last)
    scores = jnp.where(quad_mask(scores.shape, last, index), scores, MASKED)
    carry = step(last, (jnp.full(lanes, MASKED, F32), jnp.zeros(lanes, F32)), scores)

    def two_steps(count, carry):
        quad = 2 * count
        odd_ref[...] = scores_of(quad + 1)
        carry = step(quad, carry, even_ref[...])
        even_ref[...] = scores_of(jnp.minimum(quad + 2, last))
        return step(quad + 1, carry, odd_ref[...])

    carry = lax.fori_loop(0, last >> 1, two_steps, carry)
    peak, weight = lax.fori_loop(
        0, last & 1, lambda count, carry: step(last - 1, carry, even_ref[...]), carry
    )
    columns = total_ref[HEAD_SIZE:, :] / weight
    columns_ref[...] = columns
    rows_ref[...] = rows_of_columns(columns).astype(BF16)
    log_ref[...] = peak + jnp.log(weight)


def attend(index, query_low, own_kv, other_kv):
    lanes = QUERY_WIDTH // HEAD_SIZE * TOK
    vmem = pl.BlockSpec(memory_space=pltpu.VMEM)
    return pl.pallas_call(
        attend_kernel,
        out_shape=(
            jax.ShapeDtypeStruct((HEAD_SIZE, lanes), F32),
            jax.ShapeDtypeStruct((TOK, QUERY_WIDTH), BF16),
            jax.ShapeDtypeStruct((1, lanes), F32),
        ),
        in_specs=[pl.BlockSpec(memory_space=pltpu.SMEM), vmem, vmem, vmem],
        out_specs=(vmem, vmem, vmem),
        scratch_shapes=[pltpu.VMEM((2 * HEAD_SIZE, lanes), F32)] + [pltpu.VMEM((4 * TOK, lanes), F32)] * 2,
        compiler_params=pltpu.CompilerParams(vmem_limit_bytes=24 * 2**20),
        cost_estimate=pl.CostEstimate(flops=13 * 10**9, bytes_accessed=0, transcendentals=0),
        name="attend",
    )(index, query_low, own_kv, other_kv)


def attend_back_kernel(
    index_ref, query_ref, grad_ref, columns_ref, log_ref, own_ref, other_ref,
    grad_query_ref, grad_own_ref, grad_other_ref, total_ref, even_ref, odd_ref,
):
    index = index_ref[0]
    scale = HEAD_SIZE ** (-0.5)
    query_rows = query_ref[...].astype(F32) * scale
    grad_rows = grad_ref[...].astype(F32)
    query = head_columns(query_rows)
    grad = head_columns(grad_rows)
    blank = jnp.zeros_like(query)
    query_pad = jnp.concatenate([query, blank], axis=0).astype(BF16)
    grad_pad = jnp.concatenate([blank, grad], axis=0).astype(BF16)
    query_tall = head_rows(query_rows)
    grad_tall = head_rows(grad_rows)
    blank = jnp.zeros_like(query_tall)
    sides = jnp.concatenate(
        [
            jnp.concatenate([query_tall, blank], axis=1),
            jnp.concatenate([blank, grad_tall], axis=1),
        ],
        axis=0,
    ).astype(BF16)
    delta = jnp.sum(grad * columns_ref[...], axis=0, keepdims=True)
    log_total = log_ref[...]
    total_ref[...] = jnp.zeros_like(total_ref)
    grad_own_ref[...] = jnp.zeros_like(grad_own_ref)
    grad_other_ref[...] = jnp.zeros_like(grad_other_ref)

    def products_of(quad):
        quad_kv = load_quad(quad, index, own_ref, other_ref)
        return (
            jnp.dot(quad_kv, query_pad, preferred_element_type=F32),
            jnp.dot(quad_kv, grad_pad, preferred_element_type=F32),
        )

    def step(quad, scores, grad_probs, masked):
        quad_kv = load_quad(quad, index, own_ref, other_ref)
        probs = jnp.exp(scores - log_total)
        if masked:
            probs = jnp.where(quad_mask(scores.shape, quad, index), probs, 0.0)
        grad_scores = (probs * (grad_probs - delta)).astype(BF16)
        total_ref[...] += dot_low(quad_kv, grad_scores, 0, 0)
        both = jnp.concatenate([grad_scores, probs.astype(BF16)], axis=1)
        term = jnp.dot(both, sides, preferred_element_type=F32).astype(BF16)
        for side in (0, 1):
            slot = slot_of(quad * 2 + side, index)
            at = side * 2 * TOK
            grad_own_ref[pl.ds(slot, TOK), :] = term[at : at + TOK]
            grad_other_ref[pl.ds(slot, TOK), :] = term[at + TOK : at + 2 * TOK]

    last = index >> 2
    even_ref[0], even_ref[1] = products_of(0)
    step(last, *products_of(last), True)

    def two_steps(count, carry):
        quad = 2 * count
        odd_ref[0], odd_ref[1] = products_of(quad + 1)
        step(quad, even_ref[0], even_ref[1], False)
        even_ref[0], even_ref[1] = products_of(jnp.minimum(quad + 2, last))
        step(quad + 1, odd_ref[0], odd_ref[1], False)
        return carry

    lax.fori_loop(0, last >> 1, two_steps, 0)

    def final_step(count, carry):
        step(last - 1, even_ref[0], even_ref[1], False)
        return carry

    lax.fori_loop(0, last & 1, final_step, 0)
    grad_query_ref[...] = rows_of_columns(total_ref[:HEAD_SIZE, :] * scale)


def attend_back(index, query_low, grad_low, columns, log_total, own_kv, other_kv):
    vmem = pl.BlockSpec(memory_space=pltpu.VMEM)
    return pl.pallas_call(
        attend_back_kernel,
        out_shape=(
            jax.ShapeDtypeStruct(query_low.shape, F32),
            jax.ShapeDtypeStruct(own_kv.shape, BF16),
            jax.ShapeDtypeStruct(other_kv.shape, BF16),
        ),
        in_specs=[pl.BlockSpec(memory_space=pltpu.SMEM)] + [vmem] * 6,
        out_specs=(vmem, vmem, vmem),
        scratch_shapes=[pltpu.VMEM((2 * HEAD_SIZE, columns.shape[1]), F32)]
        + [pltpu.VMEM((2, 4 * TOK, columns.shape[1]), F32)] * 2,
        compiler_params=pltpu.CompilerParams(vmem_limit_bytes=24 * 2**20),
        cost_estimate=pl.CostEstimate(flops=19 * 10**9, bytes_accessed=0, transcendentals=0),
        name="attend_back",
    )(index, query_low, grad_low, columns, log_total, own_kv, other_kv)


def shards(
    tokens,
    cotangent,
    gain_first,
    z_weight,
    x_weight,
    bc_weight,
    dt_weight,
    conv_x_weight,
    conv_x_bias,
    conv_bc_weight,
    conv_bc_bias,
    dt_bias,
    decay_rate,
    skip_weight,
    out_weight,
    q_weight,
    key_matrix,
    value_matrix,
    o_weight,
    gain_second,
    gate_weight,
    up_weight,
    down_weight,
):
    index = lax.axis_index(SEQ)
    index_word = jnp.reshape(index, (1,)).astype(jnp.int32)
    ff = gate_weight.shape[1]
    in_a_width = WIDTH + 2 * NS
    in_b_width = WIDTH + ROPED + NS

    def padded_heads(values):
        return jnp.pad(values, (0, NS - HEADS))[None, :]

    together = lax.optimization_barrier
    together = lax.optimization_barrier
    with jax.named_scope("gather_near"):
        dt_wide = jnp.pad(dt_weight, ((0, 0), (0, NS - HEADS)))
        near_a = jnp.concatenate([x_weight, bc_weight, gate_weight, up_weight], axis=1)
        near_b = jnp.concatenate(
            [z_weight, q_weight, key_matrix, value_matrix, dt_wide, out_weight, o_weight, down_weight],
            axis=1,
        )
        split = near_a.shape[1]
        theirs = send(jnp.concatenate([near_a, near_b], axis=1), OTHER_Y)
        near_a = fetch(joined([near_a, theirs[:, :split]]), along_x)
        near_b = fetch(joined([near_b, theirs[:, split:]]), along_z)
        near_a, near_b = join_rings(near_a, near_b, vmem=8)
    with jax.named_scope("orders"):
        halo = send(tokens[TOK - (CONV_K - 1) :], ONWARD)
        ahead = jnp.zeros((HALO - (CONV_K - 1), MODEL_WIDTH), BF16)
        tokens_ext = jnp.concatenate([ahead, halo, tokens], axis=0)
        to_a, to_b = one_hot_orders(index)
        normed = rms_norm(tokens_ext.astype(F32), gain_first).astype(BF16)
        normed_a = project(normed, to_a).astype(BF16)
        normed_b = project(normed[HALO:], to_b).astype(BF16)
        cot_b = project(cotangent, to_b).astype(BF16)
        cosine, sine = rotary_tables(index)
        conv_weight = jnp.concatenate([conv_x_weight, conv_bc_weight], axis=1)
        conv_bias = jnp.concatenate([conv_x_bias, conv_bc_bias], axis=0)[None, :]
        decay_wide = padded_heads(decay_rate)
        skip_wide = padded_heads(skip_weight)
        dt_bias_wide = padded_heads(dt_bias)
    with jax.named_scope("gather_in"):
        in_a, rest_a = (near_a[:, :in_a_width], near_a[:, in_a_width:])
        in_b, rest_b = (near_b[:, :in_b_width], near_b[:, in_b_width:])
        (in_a, in_b), (normed_a, normed_b, to_a, to_b) = together(
            ((ring_near(in_a, along_z), ring_near(in_b, along_x)), (normed_a, normed_b, to_a, to_b))
        )
        in_a, in_b = (ring_far(in_a, along_z), ring_far(in_b, along_x))
        (in_a, in_b), (cot_b, cosine, sine) = together(((in_a, in_b), (cot_b, cosine, sine)))
        in_a_own, in_b_own = join_rings(in_a, in_b)
        in_b_other = send(in_b_own, OTHER_CORE)
        in_a_other = send(in_a_own, OTHER_CORE)
    with jax.named_scope("attention_in"):
        gate_raw, query_low, kv_low, dt_pre, step_size, log_decay = kernel_call(
            attention_in_kernel,
            [((TOK, WIDTH), F32, FAR), ((TOK, QUERY_WIDTH), BF16), ((TOK, 2 * HEAD_SIZE), BF16)]
            + [((TOK, NS), F32)] * 3,
            normed_b, in_b_own, in_b_other, cosine, sine, dt_bias_wide, decay_wide,
            name="attention_in",
        )
    with jax.named_scope("gather_kv"):
        own_kv = joined([kv_low, send(kv_low, OTHER_Y)])
    with jax.named_scope("gather_rest"):
        rest_a, rest_b = after((rest_a, rest_b), in_a_own, in_b_own)
        rest_a = ring_near(rest_a, along_z)
        rest_b = ring_near(after(rest_b, kv_low), along_x)
        normed_a_early, rest_a = together((normed_a, rest_a))
    with jax.named_scope("ssm_in"):
        ext, conved, payload = kernel_call(
            ssm_in_kernel,
            [((HALO + TOK, MODEL_WIDTH), F32, FAR), ((TOK, MODEL_WIDTH), F32, FAR),
             ((P_SIZE, SLOTS, NS), F32, FAR)],
            normed_a_early, in_a_own, in_a_other, conv_weight, conv_bias, step_size, log_decay,
            us=3, name="ssm_in",
        )
    with jax.named_scope("state_forward"):
        payload, rest_a, rest_b, own_kv = together((payload, rest_a, rest_b, own_kv))
        spans = swap_spans(payload)
        own_kv = fetch(own_kv, along_z)
        rest_b = ring_far(rest_b, along_x)
        spans, own_kv, rest_a, rest_b = together((spans, own_kv, rest_a, rest_b))
        entering = states_between(spans, spans, False)
        own_kv = fetch(join_rings(own_kv, vmem=4, far=True)[0], along_x)
        rest_a = ring_far(rest_a, along_z)
        entering, own_kv, rest_a, rest_b = together((entering, own_kv, rest_a, rest_b))
        own_kv = join_rings(own_kv, vmem=4)[0]
        other_kv = send(own_kv, OTHER_CORE)
        state_in = swap_spans(entering)
        state_in, own_kv, other_kv, rest_a, rest_b = together((state_in, own_kv, other_kv, rest_a, rest_b))
    with jax.named_scope("gather_rest"):
        rest_a_own, rest_b_own = join_rings(rest_a, rest_b, far=True)
        rest_b_other = send(rest_b_own, OTHER_CORE)
        rest_a_other = send(rest_a_own, OTHER_CORE)
    with jax.named_scope("attention"):
        attended_columns, attended_low, log_total = attend(index_word, query_low, own_kv, other_kv)
    with jax.named_scope("ssm_out"):
        gated_low, y = kernel_call(
            ssm_out_kernel, [((TOK, WIDTH), BF16), ((TOK, WIDTH), F32)],
            conved, step_size, log_decay, state_in, gate_raw, skip_wide,
            us=2, name="ssm_out",
        )
        gated_low, attended_low, rest_a_other, rest_b_other = together(
            (gated_low, attended_low, rest_a_other, rest_b_other)
        )
    with jax.named_scope("mixer_out"):
        mixed = kernel_call(
            mixer_out_kernel, [((TOK, MODEL_WIDTH), BF16)],
            gated_low, attended_low, rest_b_own, rest_b_other, to_b,
            us=2, name="mixer_out",
        )[0]
        mixed_theirs = swap_heads(mixed)
    with jax.named_scope("ffn"):
        grad_inner = kernel_call(
            down_back_kernel, [((TOK, ff), F32)], cot_b, rest_b_own, rest_b_other,
            vmem=12, us=2, name="down_back",
        )[0]
        mixed_theirs, grad_inner = together((mixed_theirs, grad_inner))
        hidden, normed_second, inner_low, grad_ff, second_part = kernel_call(
            ffn_kernel,
            [((TOK, MODEL_WIDTH), F32), ((TOK, MODEL_WIDTH), BF16, FAR), ((TOK, ff), BF16),
             ((TOK, 2 * ff), BF16, FAR), ((TOK, MODEL_WIDTH), BF16)],
            tokens, mixed, mixed_theirs, gain_second[None, :], grad_inner, to_a,
            rest_a_own, rest_a_other,
            vmem=20, us=5, name="ffn",
        )
        second_theirs = swap_heads(second_part)
        ffn_part = kernel_call(
            ffn_out_kernel, [((TOK, MODEL_WIDTH), BF16)], inner_low, rest_b_own, rest_b_other, to_b,
            vmem=16, us=2, name="ffn_out",
        )[0]
        half = (MODEL_WIDTH // 2,)
        second_theirs, ffn_part = together((second_theirs, ffn_part))
    with jax.named_scope("mixer_back"):
        (
            grad_hidden, grad_mixed_b, gain_second_part, grad_attended, grad_y, grad_gate_low, payload_back
        ) = kernel_call(
            mixer_back_kernel,
            [((TOK, MODEL_WIDTH), F32, FAR), ((TOK, MODEL_WIDTH), BF16, FAR), ((1, MODEL_WIDTH), F32),
             ((TOK, QUERY_WIDTH), BF16, FAR), ((TOK, WIDTH), F32, FAR), ((TOK, WIDTH), BF16, FAR),
             ((P_SIZE, SLOTS, NS), F32, FAR)],
            hidden, second_part, second_theirs, gain_second[None, :], cotangent, to_b,
            rest_b_own, rest_b_other, gate_raw, y, conved, log_decay,
            vmem=20, us=3, name="mixer_back",
        )
        ffn_theirs = swap_heads(ffn_part)
    with jax.named_scope("early_grads"):
        early_a, early_b = (2 * ff + WIDTH, ff + WIDTH + QUERY_WIDTH)
        a_keep, a_send, b_keep, b_send = kernel_call(
            mixer_grads_kernel,
            [(half + (WIDTH,), BF16, FAR)] * 2 + [(half + (WIDTH + QUERY_WIDTH,), BF16, FAR)] * 2,
            normed_a, grad_gate_low, grad_mixed_b, gated_low, attended_low, far=range(5), vmem=12, name="mixer_grads",
        )
        a_first_keep, a_first_send, b_first_keep, b_first_send = kernel_call(
            ffn_grads_kernel, [(half + (2 * ff,), BF16, FAR)] * 2 + [(half + (ff,), BF16, FAR)] * 2,
            normed_second, after(grad_ff, a_send), cot_b, inner_low, far=(0, 1), vmem=16, us=2, name="ffn_grads",
        )
        ffn_keep = (a_first_keep, b_first_keep)
        ffn_arrived = (send(a_first_send, OTHER_CORE), send(b_first_send, OTHER_CORE))
    with jax.named_scope("state_backward"):
        arrived_back = swap_spans(payload_back)
        arrived_back, a_send, b_send, ffn_keep = together((arrived_back, a_send, b_send, ffn_keep))
        leaving = states_between(spans, arrived_back, True)
        a_arrived = send(a_send, OTHER_CORE)
        b_arrived = send(b_send, OTHER_CORE)
        state_grad = swap_spans(leaving)
    with jax.named_scope("early_grads"):
        a_keep, a_ahead, a_behind, a_first, a_second = halve(
            ffn_keep[0], ffn_arrived[0], a_keep, a_arrived, far=True
        )
        b_keep, b_ahead, b_behind, b_first, b_second = halve(
            ffn_keep[1], ffn_arrived[1], b_keep, b_arrived, far=True
        )
        state_grad, a_first, a_second, b_first, b_second = together(
            (state_grad, a_first, a_second, b_first, b_second)
        )
        a_passed = [send(a_first, along_z(1)), send(a_second, along_z(-1))]
        b_passed = [send(b_first, along_x(1)), send(b_second, along_x(-1))]
    with jax.named_scope("ssm_back"):
        low_a, grad_dt_low, small = kernel_call(
            ssm_back_kernel,
            [((HALO + TOK, MODEL_WIDTH), BF16), ((TOK, NS), BF16), ((2 * CONV_K, MODEL_WIDTH), F32)],
            grad_y, conved, step_size, log_decay, dt_pre, state_in, state_grad, ext,
            conv_weight, conv_bias, decay_wide, skip_wide, far=(0, 1, 2, 3, 4, 7),
            scratch=[
                pltpu.VMEM((NS, TOK), F32),
                pltpu.VMEM((2 * HALO + TOK, MODEL_WIDTH), F32),
                pltpu.VMEM((TOK, MODEL_WIDTH), F32),
            ],
            vmem=16, us=8, name="ssm_back",
        )
        low_a, grad_dt_low, small, a_passed, b_passed, ffn_theirs = together(
            (low_a, grad_dt_low, small, a_passed, b_passed, ffn_theirs)
        )
    with jax.named_scope("late_grads"):
        late_keep, late_send = kernel_call(
            in_grads_kernel, [(half + (in_a_width,), BF16)] * 2, normed_a, low_a,
            vmem=12, name="late_grads_a",
        )
        late_arrived = send(late_send, OTHER_CORE)
    with jax.named_scope("early_grads"):
        a_ahead, a_behind, b_ahead, b_behind = pass_on(
            [a_ahead, a_behind] + a_passed, [b_ahead, b_behind] + b_passed
        )
        a_ready = [a_keep, send(a_ahead, along_z(1)), send(a_behind, along_z(-1))]
        b_ready = [b_keep, send(b_ahead, along_x(1)), send(b_behind, along_x(-1))]
    with jax.named_scope("attention_back"):
        grad_query, grad_own_kv, grad_other_kv = attend_back(
            index_word, query_low, grad_attended, attended_columns, log_total, own_kv, other_kv
        )
        (grad_query, grad_own_kv, grad_other_kv), a_ready, b_ready, late_arrived = together(
            ((grad_query, grad_own_kv, grad_other_kv), a_ready, b_ready, late_arrived)
        )
    with jax.named_scope("late_grads"):
        late_keep, late_ahead, late_behind, late_first, late_second = halve(
            late_keep, late_arrived, vmem=8
        )
        late_passed = [send(late_first, along_z(1)), send(late_second, along_z(-1))]
    with jax.named_scope("scatter_kv"):
        kv_arrived = send(grad_other_kv, OTHER_CORE)
        kv_arrived, late_passed = together((kv_arrived, late_passed))
        grad_kv = blocks_of([grad_own_kv, kv_arrived], 4)
        kv_arrived = spread(grad_kv, along_x)
    with jax.named_scope("late_grads"):
        late_ahead, late_behind = pass_on([late_ahead, late_behind] + late_passed, vmem=8)
        a_late = [late_keep, send(late_ahead, along_z(1)), send(late_behind, along_z(-1))]
        kv_arrived, a_late = together((kv_arrived, a_late))
    with jax.named_scope("last_grads"):
        rows = TOK // 4
        wide_a = early_a + in_a_width
        a_last = kernel_call(
            merge_a_kernel, [((rows, wide_a), F32)] + [((rows, wide_a), BF16)] * 3,
            *a_ready, *a_late, vmem=12, name="merge_a",
        )
    with jax.named_scope("project_in_back"):
        returned = send(low_a[HALO - (CONV_K - 1) : HALO], BACKWARD)
        low_own = low_a[HALO:].astype(F32) + jnp.pad(
            returned.astype(F32), ((TOK - (CONV_K - 1), 0), (0, 0))
        )
        from_a = kernel_call(
            project_a_kernel, [((TOK, MODEL_WIDTH), F32)],
            low_own.astype(BF16), grad_gate_low, in_a_own, in_a_other, in_b_own, in_b_other, to_a, to_b,
            vmem=20, us=2, name="project_a",
        )[0]
    with jax.named_scope("scatter_kv"):
        grad_kv = ring_sum(grad_kv, kv_arrived)
        grad_kv = blocks_of([grad_kv], 4)
        kv_arrived = spread(grad_kv, along_z)
        kv_arrived, from_a, a_last = together((kv_arrived, from_a, a_last))
        grad_kv = ring_sum(grad_kv, kv_arrived)
        kv_theirs = send(grad_kv[TOK:].astype(BF16), OTHER_Y)
        a_last = [a_last[0]] + spread(a_last, along_x)
        grad_kv = grad_kv[:TOK] + kv_theirs.astype(F32)
    with jax.named_scope("project_in_back"):
        late_b = ROPED + NS
        low_b = kernel_call(
            low_b_kernel, [((TOK, late_b), BF16)],
            grad_query, grad_kv, grad_dt_low, cosine, sine, vmem=8, name="low_b",
        )[0]
        first_part, gain_first_part = kernel_call(
            project_b_kernel, [((TOK, MODEL_WIDTH), BF16), ((1, MODEL_WIDTH), F32)],
            low_b, from_a, in_b_own, in_b_other, to_b, tokens, vmem=12, us=1, name="project_b",
        )
    with jax.named_scope("late_grads"):
        small = jnp.concatenate(
            [small[: CONV_K + 1], gain_first_part, gain_second_part, small[CONV_K + 3 :]], axis=0
        )
        lines, line = (SLOTS, MODEL_WIDTH // 2)
        b_keep, b_send, small = kernel_call(
            late_b_kernel,
            [(half + (late_b,), BF16), ((line + 2 * lines, late_b), BF16), ((lines, line), F32)],
            normed_b, low_b, small, vmem=12, name="late_grads_b",
        )
        *b_late, small = kernel_call(
            late_b_ring_kernel,
            [((TOK, late_b), F32)] + [((TOK + 2 * lines, late_b), BF16)] * 3 + [((lines, line), F32)],
            b_keep, send(b_send, OTHER_CORE), small, vmem=8, name="late_ring_b",
        )
        b_late = [b_late[0]] + spread(b_late, along_x)
    with jax.named_scope("last_grads"):
        wide_b = early_b + late_b
        *b_last, small = kernel_call(
            merge_b_kernel,
            [((rows, wide_b), F32)] + [((rows, wide_b + line), BF16)] * 3 + [((lines, line), F32)],
            *b_ready, *b_late, small, vmem=12, name="merge_b",
        )
        b_last = [b_last[0]] + spread(b_last, along_z)
        rows = rows // 2
        own, away, small, pair, cross = kernel_call(
            last_ring_kernel,
            [((rows, wide_a + wide_b), F32), ((rows, wide_a + wide_b + 2 * line), BF16),
             ((lines, line), F32), ((rows, 2 * NS + line), F32), ((rows, 2 * NS + line), F32)],
            *a_last, *b_last, small, vmem=8, name="last_ring",
        )
    with jax.named_scope("finish_grads"):
        widths = (ff, ff, WIDTH, WIDTH, 2 * NS, ff, WIDTH, QUERY_WIDTH, QUERY_WIDTH, HEAD_SIZE, HEAD_SIZE, NS)
        (
            grad_gate, grad_up, grad_z, grad_x, grad_bc, grad_down, grad_out, grad_o, grad_q, grad_k,
            grad_v, grad_dt, grad_conv_x, grad_conv_xb, summed_conv_bc, summed_conv_bcb,
            summed_gain_first, summed_gain_second, heads_row, unused
        ) = kernel_call(
            finish_grads_kernel,
            [((rows, width), F32) for width in widths]
            + [((CONV_K, WIDTH), F32), ((WIDTH,), F32), ((CONV_K, 2 * NS), F32), ((2 * NS,), F32),
               ((MODEL_WIDTH,), F32), ((MODEL_WIDTH,), F32), ((1, 3 * NS), F32), ((2 * CONV_K, NS), F32)],
            own, send(away, OTHER_Y), small, swap_heads(pair),
            lax.ppermute(cross, (SEQ, "head"), OTHER_Y_AND_HEAD), vmem=8, name="finish_grads",
        )
        grad_dt = grad_dt[:, :HEADS]
    with jax.named_scope("finish"):
        grad_first = first_part.astype(F32) + swap_heads(first_part).astype(F32)
        grad_tokens = grad_hidden + norm_back(tokens.astype(F32), gain_first[None, :], grad_first)[1]
        output = (hidden + (ffn_part.astype(F32) + ffn_theirs.astype(F32))).astype(BF16)
    with jax.named_scope("small_grads"):
        grad_dt_bias_own = heads_row[0, :HEADS]
        grad_decay_own = heads_row[0, NS : NS + HEADS]
        grad_skip_own = heads_row[0, 2 * NS : 2 * NS + HEADS]
    return (
        output,
        grad_tokens,
        summed_gain_first,
        grad_z,
        grad_x,
        grad_bc,
        grad_dt,
        grad_conv_x,
        grad_conv_xb,
        summed_conv_bc,
        summed_conv_bcb,
        grad_dt_bias_own,
        grad_decay_own,
        grad_skip_own,
        grad_out,
        grad_q,
        grad_k,
        grad_v,
        grad_o,
        summed_gain_second,
        grad_gate,
        grad_up,
        grad_down,
    )


def solution(mesh):
    return jax.shard_map(
        shards,
        mesh=mesh,
        in_specs=(
            P("seq", None),
            P("seq", None),
            P(),
            P("seq", "head"),
            P("seq", "head"),
            P("seq", None),
            P("seq", "head"),
            P(None, "head"),
            P("head"),
            P(),
            P(),
            P("head"),
            P("head"),
            P("head"),
            P("seq", "head"),
            P("seq", "head"),
            P("seq", "head"),
            P("seq", "head"),
            P("seq", "head"),
            P(),
            P("seq", "head"),
            P("seq", "head"),
            P("seq", "head"),
        ),
        out_specs=(
            P("seq", None),
            P("seq", None),
            P(),
            P("seq", "head"),
            P("seq", "head"),
            P("seq", None),
            P("seq", "head"),
            P(None, "head"),
            P("head"),
            P(),
            P(),
            P("head"),
            P("head"),
            P("head"),
            P("seq", "head"),
            P("seq", "head"),
            P("seq", "head"),
            P("seq", "head"),
            P("seq", "head"),
            P(),
            P("seq", "head"),
            P("seq", "head"),
            P("seq", "head"),
        ),
        check_vma=False,
    )
```
